32 devices in a mesh: dp: 4 (over y, x), expert: 8 (over z, core).
Axes of the slice: x: 2, y: 2, z: 4, core: 2. Of those that a mesh axis runs over, the one named last changes fastest.
Arguments:
- tokens: bfloat16 [512, 4096], P(('dp', 'expert')), may hold values from -6 to 6
- cotangent: bfloat16 [512, 4096], P(('dp', 'expert')), may hold values from -6 to 6
- gate_prob: float32 [512, 8], P(('dp', 'expert')), may hold values from 0.05 to 0.6
- expert_ids: int32 [512, 8], P(('dp', 'expert')), may hold values from 0 to 63, all different within a row; in each aligned block of 16 rows (0 to 15, 16 to 31, ...) at most 3 rows name the same one
- placement: int32 [64], replicated, may hold values from 0 to 63, each once
- gate_weight: bfloat16 [64, 768, 4096], P('expert', 'dp'), may hold values from -0.09375 to 0.09375
- up_weight: bfloat16 [64, 768, 4096], P('expert', 'dp'), may hold values from -0.09375 to 0.09375
- down_weight: bfloat16 [64, 768, 4096], P('expert', 'dp'), may hold values from -0.21875 to 0.21875
Outputs:
- mixed: bfloat16 [512, 4096], P(('dp', 'expert'))
- token_grad: bfloat16 [512, 4096], P(('dp', 'expert'))
- gate_grad: float32 [512, 8], P(('dp', 'expert'))
- gate_weight_grad: bfloat16 [64, 768, 4096], P('expert', 'dp')
- up_weight_grad: bfloat16 [64, 768, 4096], P('expert', 'dp')
- down_weight_grad: bfloat16 [64, 768, 4096], P('expert', 'dp')
The draws below stay inside these ranges and needn't reach their ends.
Inputs may be any that keep to these rules, and one draw needn't show every extreme that they name: `expert_ids`: in each row the 8 experts differ. In each aligned block of 16 tokens (the tokens of one device) no expert is named by more than 3 tokens, and in some blocks one is named by exactly 3. `placement`: A permutation: each slot serves exactly one expert, and no expert is replicated.
All inputs are finite; a program needn't handle non-finite values.
Results may differ from the reference program's by a relative error of at most 0.015.
Values may be sent and summed in bfloat16 or wider, within the bound.
No kernel may reach another device: no remote copies, remote signals or barrier semaphores. Data moves between devices by JAX's collectives and lax.ppermute only.
A program may use at most 192 MiB of HBM per device.

```python
import math
import jax
import jax.numpy as jnp
import numpy as np
from jax import lax

D = 4096
FF = 768
EXPERTS = 64
TOP = 8
TOK_DEV = 16
CAP = 3
TOKENS = 512
N_DP = 4


def steps_of(rng, shape, cuts, low, top_value):
    def one(axis_at, shards_of):
        heights = jax.random.uniform(jax.random.fold_in(jax.random.fold_in(rng, 6), axis_at), (shards_of,), jnp.float32, low / len(cuts), top_value / len(cuts))
        return jnp.repeat(jnp.exp(heights), shape[axis_at] // shards_of).reshape((-1,) + (1,) * (len(shape) - axis_at - 1))

    gain = one(*cuts[0])
    for cut in cuts[1:]:
        gain = gain * one(*cut)
    return gain


def deal_out(own_key, own, number, rows, amount, top, reach, lean):
    order = jax.random.permutation(own_key, amount)
    packed, ordinary = shares(amount, rows * top, reach, lean, True), shares(amount, rows * top, reach, lean, False)
    places = jnp.arange(amount)

    def named(sizes, offset_by):
        used = int((sizes > 0).sum())
        fixed = max(1, used // 4)
        passed = fixed + (places - fixed + offset_by * (used - fixed)) % max(1, amount - fixed)
        return jnp.zeros((amount,), jnp.int32).at[order[jnp.where(places < fixed, places, passed)]].set(jnp.asarray(sizes, jnp.int32))

    sizes = jnp.where(number % 4 == 0, named(packed, number // 4), named(ordinary, number - number // 4 - 1))
    mixed = jax.random.permutation(jax.random.fold_in(own, 3), amount)
    source_of, taker = mixed[0:amount // 2 * 2:2], mixed[1:amount // 2 * 2:2]
    room = jnp.minimum(sizes[source_of] - 1, reach - sizes[taker]) // 2
    room = jnp.where((source_of == order[0]) | (taker == order[0]) | (sizes[taker] == 0), 0, jnp.maximum(room, 0))
    passed = jax.random.randint(jax.random.fold_in(own, 4), (amount // 2,), 0, 1 << 20) % (room + 1)
    sizes = sizes.at[source_of].add(-passed).at[taker].add(passed)
    members = jnp.searchsorted(jnp.cumsum(sizes), jnp.arange(rows * top), side="right").astype(jnp.int32)
    grid = members.reshape(top, rows).T
    grid = grid[jax.random.permutation(jax.random.fold_in(own, 1), rows)]
    offset_by = jax.random.randint(jax.random.fold_in(own, 2), (rows, 1), 0, top)
    return jnp.take_along_axis(grid, (jnp.arange(top)[None, :] + offset_by) % top, axis=1)


def shares(amount, total, limit, skew, full):
    loads = [(1 << 20) // math.isqrt(rank ** skew) + 1 for rank in range(1, amount + 1)]
    largest = limit if full else min(limit, max(-(-total // amount), total * loads[0] // sum(loads)))
    least = 1 if total - largest >= amount - 1 else 0
    holding, rest = [largest] + [least] * (amount - 1), total - largest - least * (amount - 1)
    while rest > 0:
        free = [i for i in range(1, amount) if holding[i] < largest] or [i for i in range(1, amount) if holding[i] < limit]
        pool, remaining = sum([loads[i] for i in free]), rest
        for i in free:
            addition = min(limit - holding[i], max(1, remaining * loads[i] // pool), rest)
            holding[i] = holding[i] + addition
            rest = rest - addition
    return np.array(holding)


def scatter_about(rng, dims, spread, bound, shards=(), held_as=jnp.bfloat16):
    loudness = steps_of(rng, dims, shards, -0.22, 0.18) if shards else 1.0
    array = jax.random.normal(rng, dims, jnp.float32) * spread * loudness
    return jnp.minimum(jnp.maximum(array, -bound), bound).astype(held_as)


def setup_inputs(seed: int = 0) -> dict:
    seeds = jax.random.split(jax.random.key(seed), 9)
    tokens = scatter_about(seeds[0], (TOKENS, D), 1.0, 6.0, ((0, 32),))
    cotangent = scatter_about(seeds[1], (TOKENS, D), 1.0, 6.0, ((0, 32),))
    gate_prob = jnp.clip(0.05 + 0.55 * jax.random.uniform(seeds[2], (TOKENS, TOP), jnp.float32) ** steps_of(seeds[2], (TOKENS, TOP), ((0, 32),), -0.2, 0.2), 0.05, 0.6)
    expert_ids_keys = jax.random.split(jax.random.fold_in(seeds[3], 1), TOKENS // TOK_DEV)
    expert_ids_turns = jax.random.permutation(jax.random.fold_in(seeds[3], 3), TOKENS // TOK_DEV)
    expert_ids = jax.vmap(lambda own, number: deal_out(jax.random.fold_in(seeds[3], 2), own, number, TOK_DEV, EXPERTS, TOP, CAP, 2))(expert_ids_keys, expert_ids_turns).reshape((TOKENS, TOP))
    placement = jax.random.permutation(seeds[4], EXPERTS).astype(jnp.int32)
    gate_weight = scatter_about(seeds[5], (EXPERTS, FF, D), D ** -0.5, 0.09375, ((0, 8), (1, 4)))
    up_weight = scatter_about(seeds[6], (EXPERTS, FF, D), D ** -0.5, 0.09375, ((0, 8), (1, 4)))
    down_weight = scatter_about(seeds[7], (EXPERTS, FF, D), FF ** -0.5, 0.21875, ((0, 8), (1, 4)))
    return {"tokens": tokens, "cotangent": cotangent, "gate_prob": gate_prob, "expert_ids": expert_ids, "placement": placement, "gate_weight": gate_weight, "up_weight": up_weight, "down_weight": down_weight}


def gated(values):
    sigmoid_v = jax.nn.sigmoid(values)
    return values * sigmoid_v, sigmoid_v * (1.0 + values * (1.0 - sigmoid_v))


def settle(values):
    kept = lax.optimization_barrier(values.astype(jnp.bfloat16))
    return kept.astype(jnp.float32)


def rounded_sum(partial_terms):
    kept = lax.optimization_barrier(partial_terms.astype(jnp.bfloat16))
    return jnp.sum(kept.astype(jnp.float32), axis=0).astype(jnp.bfloat16)


def reference(tokens, cotangent, gate_prob, expert_ids, placement, gate_weight, up_weight, down_weight):
    pair_total = TOKENS * TOP
    most_rows = (TOKENS // TOK_DEV) * CAP
    quarter = FF // N_DP
    slot_ids = jnp.take(placement, expert_ids.reshape(-1), axis=0).astype(jnp.int32)
    one_hot = (slot_ids[:, None] == jnp.arange(EXPERTS, dtype=jnp.int32)[None, :]).astype(jnp.int32)
    earlier_count = jnp.sum((jnp.cumsum(one_hot, axis=0) - one_hot) * one_hot, axis=1).astype(jnp.int32)
    table = jnp.full((EXPERTS * most_rows,), pair_total, jnp.int32)
    table = table.at[slot_ids * most_rows + earlier_count].set(jnp.arange(pair_total, dtype=jnp.int32))
    table = table.reshape(EXPERTS, most_rows)
    zero_row = jnp.zeros((1, D), jnp.bfloat16)
    token_ext = jnp.concatenate([tokens, zero_row], axis=0)
    cot_ext = jnp.concatenate([cotangent, zero_row], axis=0)
    prob_ext = jnp.concatenate([gate_prob.reshape(-1), jnp.zeros((1,), jnp.float32)], axis=0)

    def expert_step(state_carry, inputs):
        out_acc, grad_acc, dgate_acc = state_carry
        row_pairs, w_gate, w_up, w_down = inputs
        token_idx = jnp.where(row_pairs < pair_total, row_pairs // TOP, TOKENS).astype(jnp.int32)
        routed = token_ext[token_idx].astype(jnp.float32)
        route_prob = prob_ext[row_pairs].astype(jnp.float32)
        routed_cot = cot_ext[token_idx].astype(jnp.float32)
        scaled_grad = settle(route_prob[:, None] * routed_cot)
        gate_full = w_gate.astype(jnp.float32)
        up_full = w_up.astype(jnp.float32)
        down_full = w_down.astype(jnp.float32)
        gate_pre = jnp.dot(routed, gate_full.T, preferred_element_type=jnp.float32)
        up_pre = jnp.dot(routed, up_full.T, preferred_element_type=jnp.float32)
        silu_v, slope = gated(gate_pre)
        hidden = settle(silu_v * up_pre)
        parts_out = jnp.einsum('rqf,qfd->qrd', hidden.reshape(most_rows, N_DP, quarter), down_full.reshape(N_DP, quarter, D))
        out_rows = rounded_sum(parts_out)
        d_hidden = jnp.dot(scaled_grad, down_full.T, preferred_element_type=jnp.float32)
        d_gate_pre = settle(d_hidden * up_pre * slope)
        d_up_pre = settle(d_hidden * silu_v)
        parts_back = jnp.einsum('rqf,qfd->qrd', d_gate_pre.reshape(most_rows, N_DP, quarter), gate_full.reshape(N_DP, quarter, D))
        parts_back = parts_back + jnp.einsum('rqf,qfd->qrd', d_up_pre.reshape(most_rows, N_DP, quarter), up_full.reshape(N_DP, quarter, D))
        back_rows = rounded_sum(parts_back)
        down_grad = jnp.dot(hidden.T, scaled_grad, preferred_element_type=jnp.float32).astype(jnp.bfloat16)
        gate_grad_w = jnp.dot(d_gate_pre.T, routed, preferred_element_type=jnp.float32).astype(jnp.bfloat16)
        up_grad_w = jnp.dot(d_up_pre.T, routed, preferred_element_type=jnp.float32).astype(jnp.bfloat16)
        out_value = out_rows.astype(jnp.float32)
        out_acc = out_acc.at[token_idx].add(route_prob[:, None] * out_value)
        grad_acc = grad_acc.at[token_idx].add(back_rows.astype(jnp.float32))
        dgate_acc = dgate_acc.at[row_pairs].set(jnp.sum(routed_cot * out_value, axis=1))
        return (out_acc, grad_acc, dgate_acc), (gate_grad_w, up_grad_w, down_grad)

    start = (jnp.zeros((TOKENS + 1, D), jnp.float32), jnp.zeros((TOKENS + 1, D), jnp.float32), jnp.zeros((pair_total + 1,), jnp.float32))
    finals, weight_grads = lax.scan(expert_step, start, (table, gate_weight, up_weight, down_weight))
    out_acc, grad_acc, dgate_acc = finals
    mixed = out_acc[:TOKENS].astype(jnp.bfloat16)
    token_grad = grad_acc[:TOKENS].astype(jnp.bfloat16)
    gate_grad = dgate_acc[:pair_total].reshape(TOKENS, TOP)
    return (mixed, token_grad, gate_grad, weight_grads[0], weight_grads[1], weight_grads[2])
```

```python
import jax
import jax.numpy as jnp
from jax import lax
from jax.sharding import PartitionSpec as P

CAP = 3
AXES = ("dp", "expert")
CORE, Z, X, Y = 1, (2, 4, 6), 8, 16


def gated(values):
    sigmoid_v = jax.nn.sigmoid(values)
    return (values * sigmoid_v, sigmoid_v * (1.0 + values * (1.0 - sigmoid_v)))


def swap(values, even, odd=None):
    odd = even if odd is None else odd
    count = lax.axis_size("dp") * lax.axis_size("expert")
    pairs = [(i, i ^ (odd if i & CORE else even)) for i in range(count)]
    return lax.ppermute(values, AXES, pairs)


def gather_rows(block):
    rows = jnp.concatenate([block] + [swap(block, bit) for bit in Z])
    rows = jnp.concatenate([rows, swap(rows, X, Y)])
    rows = jnp.concatenate([rows, swap(rows, Y, X)])
    return jnp.concatenate([rows, swap(rows, CORE)])


def arrival():
    def own(first, second):
        order = [0, *Z]
        order = order + [first ^ i for i in order]
        return order + [second ^ i for i in order]

    even, odd = own(X, Y), own(Y, X)
    return jnp.array([even + [CORE ^ i for i in odd], odd + [CORE ^ i for i in even]], jnp.int32)


def add(a, b):
    return (a.astype(jnp.float32) + b.astype(jnp.float32)).astype(jnp.bfloat16)


def scatter_sum(own, other, tok_count):
    rows = add(own, swap(other, CORE))
    half = rows.shape[0] // 2
    rows = add(rows[:half], swap(rows[half:], Y, X))
    half = half // 2
    rows = add(rows[:half], swap(rows[half:], X, Y))
    parts = [rows[:tok_count]] + [
        swap(rows[tok_count * (i + 1) : tok_count * (i + 2)], bit) for i, bit in enumerate(Z)
    ]
    total = parts[0].astype(jnp.float32)
    for part in parts[1:]:
        total = total + part.astype(jnp.float32)
    return total.astype(jnp.bfloat16)


def slots_of(expert_ids, placement):
    total = placement.shape[0]
    matches = expert_ids[:, :, None] == jnp.arange(total, dtype=jnp.int32)
    return jnp.sum(jnp.where(matches, placement, 0), axis=2)


def dense_body(
    tokens, cotangent, gate_prob, expert_ids, placement, gate_weight, up_weight, down_weight
):
    tok_count, width = tokens.shape
    local, hidden_count, _ = gate_weight.shape
    total_experts = placement.shape[0]
    units = local * hidden_count
    me = lax.axis_index(AXES)
    dp_size, ex_size = lax.axis_size("dp"), lax.axis_size("expert")
    devices = dp_size * ex_size
    w_gate = gate_weight.reshape(units, width)
    w_up = up_weight.reshape(units, width)
    w_down = down_weight.reshape(units, width)

    slots = slots_of(expert_ids, placement)
    used = slots[:, :, None] == jnp.arange(total_experts, dtype=jnp.int32)
    prob = jnp.sum(jnp.where(used, gate_prob[:, :, None], 0.0), axis=1)
    prob = lax.all_gather(prob, AXES, axis=0)
    order = me ^ arrival()[me & CORE]
    prob = prob[order].reshape(devices * tok_count, total_experts)
    prob = lax.dynamic_slice_in_dim(prob, lax.axis_index("expert") * local, local, axis=1)
    expert_of = jnp.arange(units, dtype=jnp.int32) // hidden_count
    prob_units = jnp.zeros((devices * tok_count, units), jnp.float32)
    for e in range(local):
        prob_units = jnp.where(expert_of == e, prob[:, e : e + 1], prob_units)
    taken = prob_units > 0.0

    rows = gather_rows(tokens)
    grads = gather_rows(cotangent)
    across = (((1,), (1,)), ((), ()))
    down_rows = (((0,), (0,)), ((), ()))

    def dot(a, b, dims=(((1,), (0,)), ((), ()))):
        return lax.dot_general(a, b, dims, preferred_element_type=jnp.float32)

    gate_pre = dot(rows, w_gate, across)
    up_pre = dot(rows, w_up, across)
    silu_v, slope = gated(gate_pre)
    hidden = jnp.where(taken, silu_v * up_pre, 0.0)
    scaled = (hidden * prob_units).astype(jnp.bfloat16)
    half = devices * tok_count // 2
    out_other = dot(scaled[half:], w_down).astype(jnp.bfloat16)
    out_own = dot(scaled[:half], w_down).astype(jnp.bfloat16)
    mixed = scatter_sum(out_own, out_other, tok_count)

    d_plain = dot(grads, w_down, across)
    gate_terms = hidden * d_plain
    d_hidden = d_plain * prob_units
    d_gate = (d_hidden * up_pre * slope).astype(jnp.bfloat16)
    d_up = (d_hidden * silu_v).astype(jnp.bfloat16)
    back_other = (dot(d_gate[half:], w_gate) + dot(d_up[half:], w_up)).astype(jnp.bfloat16)
    back_own = (dot(d_gate[:half], w_gate) + dot(d_up[:half], w_up)).astype(jnp.bfloat16)
    token_grad = scatter_sum(back_own, back_other, tok_count)

    pick = (expert_of[:, None] == jnp.arange(local, dtype=jnp.int32)).astype(jnp.float32)
    shares = jnp.dot(gate_terms, pick, precision=lax.Precision.HIGHEST)
    shares = shares.reshape(devices, tok_count, local)[_inverse(order)]
    shares = lax.all_to_all(shares, AXES, split_axis=0, concat_axis=0, tiled=True)
    shares = shares.reshape(dp_size, ex_size, tok_count, local).sum(axis=0)
    shares = shares.transpose(1, 0, 2).reshape(tok_count, 1, total_experts)
    gate_grad = jnp.sum(jnp.where(used, shares, 0.0), axis=2)

    gate_weight_grad = dot(d_gate, rows, down_rows).astype(jnp.bfloat16)
    up_weight_grad = dot(d_up, rows, down_rows).astype(jnp.bfloat16)
    down_weight_grad = dot(scaled, grads, down_rows).astype(jnp.bfloat16)
    shape = gate_weight.shape
    return (
        mixed,
        token_grad,
        gate_grad,
        gate_weight_grad.reshape(shape),
        up_weight_grad.reshape(shape),
        down_weight_grad.reshape(shape),
    )


def _inverse(order):
    count = order.shape[0]
    places = jnp.arange(count, dtype=jnp.int32)
    return jnp.sum(jnp.where(order[None, :] == places[:, None], places[None, :], 0), axis=1)


def routed_body(tokens, cotangent, gate_prob, expert_ids, placement, gate_weight, up_weight, down_weight):
    tok_count, model_width = tokens.shape
    top_count = expert_ids.shape[1]
    expert_devs = lax.axis_size("expert")
    local_experts = gate_weight.shape[0]
    total_experts = placement.shape[0]
    capacity = CAP
    flat_ids = expert_ids.reshape(-1)
    matches_id = flat_ids[:, None] == jnp.arange(total_experts, dtype=jnp.int32)[None, :]
    slot_ids = jnp.sum(jnp.where(matches_id, placement[None, :], 0), axis=1)
    pair_order = jnp.arange(flat_ids.shape[0], dtype=jnp.int32)
    earlier = (slot_ids[:, None] == slot_ids[None, :]) & (pair_order[None, :] < pair_order[:, None])
    position = slot_ids * capacity + jnp.sum(earlier.astype(jnp.int32), axis=1)
    matches = jnp.arange(total_experts * capacity, dtype=jnp.int32)[:, None] == position[None, :]
    matches = matches.reshape(total_experts * capacity, tok_count, top_count)
    dispatch = jnp.any(matches, axis=2).astype(jnp.bfloat16)
    weight_map = jnp.sum(jnp.where(matches, gate_prob[None, :, :], 0.0), axis=2)
    sent_rows = jnp.dot(dispatch, tokens, preferred_element_type=jnp.float32).astype(jnp.bfloat16)
    sent_grads = jnp.dot(
        weight_map, cotangent.astype(jnp.float32), precision=lax.Precision.HIGHEST
    ).astype(jnp.bfloat16)
    block_shape = (1, expert_devs, local_experts, capacity, model_width)
    sent_rows = sent_rows.reshape(block_shape)
    sent_grads = sent_grads.reshape(block_shape)
    got_rows, got_grads = (
        lax.all_to_all(sent_rows, "expert", split_axis=1, concat_axis=1, tiled=True),
        lax.all_to_all(sent_grads, "expert", split_axis=1, concat_axis=1, tiled=True),
    )
    routed, routed_grads = (
        lax.all_gather(got_rows, "dp", axis=0, tiled=True),
        lax.all_gather(got_grads, "dp", axis=0, tiled=True),
    )
    gate_pre = jnp.einsum(
        "asjcd,jfd->asjcf", routed, gate_weight, preferred_element_type=jnp.float32
    )
    up_pre = jnp.einsum("asjcd,jfd->asjcf", routed, up_weight, preferred_element_type=jnp.float32)
    silu_v, slope = gated(gate_pre)
    hidden = (silu_v * up_pre).astype(jnp.bfloat16)
    out_part = jnp.einsum(
        "asjcf,jfd->asjcd", hidden, down_weight, preferred_element_type=jnp.float32
    )
    d_hidden = jnp.einsum(
        "asjcd,jfd->asjcf", routed_grads, down_weight, preferred_element_type=jnp.float32
    )
    d_gate_pre = (d_hidden * up_pre * slope).astype(jnp.bfloat16)
    d_up_pre = (d_hidden * silu_v).astype(jnp.bfloat16)
    back_part = jnp.einsum(
        "asjcf,jfd->asjcd", d_gate_pre, gate_weight, preferred_element_type=jnp.float32
    )
    back_part = back_part + jnp.einsum(
        "asjcf,jfd->asjcd", d_up_pre, up_weight, preferred_element_type=jnp.float32
    )
    down_grad = jnp.einsum(
        "asjcf,asjcd->jfd", hidden, routed_grads, preferred_element_type=jnp.float32
    ).astype(jnp.bfloat16)
    gate_grad_w = jnp.einsum(
        "asjcf,asjcd->jfd", d_gate_pre, routed, preferred_element_type=jnp.float32
    ).astype(jnp.bfloat16)
    up_grad_w = jnp.einsum(
        "asjcf,asjcd->jfd", d_up_pre, routed, preferred_element_type=jnp.float32
    ).astype(jnp.bfloat16)
    summed = (
        lax.psum_scatter(
            out_part.astype(jnp.bfloat16), "dp", scatter_dimension=0, tiled=True
        ).astype(jnp.float32),
        lax.psum_scatter(
            back_part.astype(jnp.bfloat16), "dp", scatter_dimension=0, tiled=True
        ).astype(jnp.float32),
    )
    back_out, back_grad = (
        lax.all_to_all(
            summed[0].astype(jnp.bfloat16), "expert", split_axis=1, concat_axis=1, tiled=True
        ),
        lax.all_to_all(
            summed[1].astype(jnp.bfloat16), "expert", split_axis=1, concat_axis=1, tiled=True
        ),
    )
    out_flat = back_out.reshape(total_experts * capacity, model_width)
    grad_flat = back_grad.reshape(total_experts * capacity, model_width)
    chosen_out = out_flat[position].reshape(tok_count, top_count, model_width)
    chosen_grad = grad_flat[position].reshape(tok_count, top_count, model_width)
    mixed = jnp.einsum(
        "tk,tkd->td", gate_prob, chosen_out.astype(jnp.float32), precision=lax.Precision.HIGHEST
    ).astype(jnp.bfloat16)
    gate_grad = jnp.einsum("td,tkd->tk", cotangent, chosen_out, preferred_element_type=jnp.float32)
    token_grad = jnp.sum(chosen_grad.astype(jnp.float32), axis=1).astype(jnp.bfloat16)
    return (mixed, token_grad, gate_grad, gate_grad_w, up_grad_w, down_grad)


def body(*args):
    tokens, gate_weight = args[0], args[5]
    mesh_fits = (lax.axis_size("dp"), lax.axis_size("expert")) == (4, 8)
    if mesh_fits and tokens.shape[0] <= gate_weight.shape[0] * CAP:
        return dense_body(*args)
    return routed_body(*args)


def solution(mesh):
    return jax.shard_map(
        body,
        mesh=mesh,
        in_specs=(
            P(("dp", "expert"), None),
            P(("dp", "expert"), None),
            P(("dp", "expert"), None),
            P(("dp", "expert"), None),
            P(),
            P("expert", "dp", None),
            P("expert", "dp", None),
            P("expert", "dp", None),
        ),
        out_specs=(
            P(("dp", "expert"), None),
            P(("dp", "expert"), None),
            P(("dp", "expert"), None),
            P("expert", "dp", None),
            P("expert", "dp", None),
            P("expert", "dp", None),
        ),
        check_vma=False,
    )
```

```python
import functools

import jax
import jax.numpy as jnp
from jax import lax
from jax.experimental import pallas as pl
from jax.experimental.pallas import tpu as pltpu
from jax.sharding import PartitionSpec as P

CAP = 3
AXES = ("dp", "expert")
CORE, Z1, Z2, Z3, X, Y = 1, 2, 4, 6, 8, 16
GROUPS = ((0,), (Z1, Z2), (Z3,))
CHUNK = 512
MIB = 1 << 20


def gated(values):
    sigmoid_v = jax.nn.sigmoid(values)
    return (values * sigmoid_v, sigmoid_v * (1.0 + values * (1.0 - sigmoid_v)))


def swap(values, even, odd=None):
    odd = even if odd is None else odd
    count = lax.axis_size("dp") * lax.axis_size("expert")
    pairs = [(i, i ^ (odd if i & CORE else even)) for i in range(count)]
    return lax.ppermute(values, AXES, pairs)


def gather_rows(block):
    near, far = swap(block, Z1), swap(block, Z2)
    last = swap(far, Z1)
    pieces = []
    for rows in (block, jnp.concatenate([near, far]), last):
        rows = jnp.concatenate([rows, swap(rows, X, Y)])
        pieces += [rows, swap(rows, Y, X)]
    own = jnp.concatenate(pieces)
    return own, swap(own, CORE)


def arrival():
    def own(first, second):
        order = []
        for group in GROUPS:
            order += [b ^ a ^ z for b in (0, second) for a in (0, first) for z in group]
        return order

    even, odd = own(X, Y), own(Y, X)
    return jnp.array([even + [CORE ^ i for i in odd], odd + [CORE ^ i for i in even]], jnp.int32)


def add(a, b):
    return (a.astype(jnp.float32) + b.astype(jnp.float32)).astype(jnp.bfloat16)


def scatter_sum(own, other, tok_count):
    from_other = swap(other, CORE)
    ends, at = [], 0
    for group in GROUPS:
        ends.append((at, len(group) * tok_count))
        at += 4 * len(group) * tok_count
    sums = {}
    for at, size in reversed(ends):
        rows = add(own[at : at + 4 * size], from_other[at : at + 4 * size])
        rows = add(rows[: 2 * size], swap(rows[2 * size :], Y, X))
        sums[at] = add(rows[:size], swap(rows[size:], X, Y))
    mine, middle, last = (sums[at] for at, _ in ends)
    far = add(middle[tok_count:], swap(last, Z1))
    near = swap(middle[:tok_count], Z1)
    far = swap(far, Z2)
    total = mine.astype(jnp.float32) + near.astype(jnp.float32) + far.astype(jnp.float32)
    return total.astype(jnp.bfloat16)


def slots_of(expert_ids, placement):
    total = placement.shape[0]
    matches = expert_ids[:, :, None] == jnp.arange(total, dtype=jnp.int32)
    return jnp.sum(jnp.where(matches, placement, 0), axis=2)


NT = (((1,), (1,)), ((), ()))
NN = (((1,), (0,)), ((), ()))


def dot(a, b, dims=NN):
    return lax.dot_general(a, b, dims, preferred_element_type=jnp.float32)


def dispatch(pick_ref, own_ref, other_ref, x_ref):
    width = own_ref.shape[1]
    experts, places = x_ref.shape[1], x_ref.shape[2]
    for half, source in enumerate((own_ref, other_ref)):
        for at in range(0, width, CHUNK):
            rows = dot(pick_ref[half], source[:, at : at + CHUNK]).astype(jnp.bfloat16)
            for e in range(experts):
                x_ref[half, e, :, at : at + CHUNK] = rows[e * places : (e + 1) * places]


def placed(x_ref, e):
    return jnp.concatenate([x_ref[0, e], x_ref[1, e]], axis=0)


def up_kernel(pick_ref, prob_ref, own_ref, other_ref, gate_ref, up_ref, x_ref, g_ref, u_ref, h_ref, ht_ref):
    e = pl.program_id(0)

    @pl.when(e == 0)
    def _():
        dispatch(pick_ref, own_ref, other_ref, x_ref)

    rows = placed(x_ref, e)
    g = dot(gate_ref[0], rows, NT)
    u = dot(up_ref[0], rows, NT)
    g_ref[0] = g
    u_ref[0] = u
    silu_v, _ = gated(g)
    scaled = silu_v * u * prob_ref[0]
    ht_ref[0] = scaled.astype(jnp.bfloat16)
    h_ref[0] = scaled.T.astype(jnp.bfloat16)


def slope_kernel(pick_ref, prob_ref, own_ref, other_ref, down_ref, g_ref, u_ref,
                 x_ref, dg_ref, du_ref, dgt_ref, dut_ref, share_ref):
    e = pl.program_id(0)

    @pl.when(e == 0)
    def _():
        dispatch(pick_ref, own_ref, other_ref, x_ref)

    plain = dot(down_ref[0], placed(x_ref, e), NT)
    g, u = g_ref[0], u_ref[0]
    silu_v, slope = gated(g)
    share_ref[0] = jnp.sum(silu_v * u * plain, axis=0, keepdims=True)
    scaled = plain * prob_ref[0]
    dg = scaled * u * slope
    du = scaled * silu_v
    dgt_ref[0] = dg.astype(jnp.bfloat16)
    dut_ref[0] = du.astype(jnp.bfloat16)
    dg_ref[0] = dg.T.astype(jnp.bfloat16)
    du_ref[0] = du.T.astype(jnp.bfloat16)


def back_kernel(terms, put_ref, *refs):
    lefts, rights = refs[:terms], refs[terms : 2 * terms]
    own_ref, other_ref, rows_ref = refs[2 * terms :]
    experts, places = rights[0].shape[0], put_ref.shape[2] // rights[0].shape[0]
    for e in range(experts):
        rows = dot(lefts[0][e], rights[0][e])
        for left, right in zip(lefts[1:], rights[1:]):
            rows = rows + dot(left[e], right[e])
        rows = rows.astype(jnp.bfloat16)
        for half in range(2):
            rows_ref[half, e * places : (e + 1) * places] = rows[half * places : (half + 1) * places]
    own_ref[...] = dot(put_ref[0], rows_ref[0]).astype(jnp.bfloat16)
    other_ref[...] = dot(put_ref[1], rows_ref[1]).astype(jnp.bfloat16)


def grad_kernel(x_ref, *refs):
    count = len(refs) // 2
    rows = jnp.concatenate([x_ref[0, 0], x_ref[1, 0]], axis=0)
    for left, out in zip(refs[:count], refs[count:]):
        for at in range(0, rows.shape[1], CHUNK):
            out[0, :, at : at + CHUNK] = dot(left[0], rows[:, at : at + CHUNK]).astype(jnp.bfloat16)


def whole(shape):
    return pl.BlockSpec(shape, lambda i: (0,) * len(shape))


def each(shape):
    return pl.BlockSpec((1, *shape[1:]), lambda i: (i,) + (0,) * (len(shape) - 1))


def call(kernel, grid, ins, args, outs, shapes, scratch=(), flops=0):
    moved = sum(a.size * a.dtype.itemsize for a in (*args, *shapes))
    return pl.pallas_call(
        kernel,
        grid=(grid,),
        in_specs=ins,
        out_specs=outs,
        out_shape=shapes,
        scratch_shapes=scratch,
        compiler_params=pltpu.CompilerParams(vmem_limit_bytes=48 * MIB),
        cost_estimate=pl.CostEstimate(flops=flops, bytes_accessed=moved, transcendentals=0),
    )(*args)


def up_call(pick, prob, own, other, w_gate, w_up):
    experts, hidden, width = w_gate.shape
    places = pick.shape[1] // experts
    rows = 2 * places
    args = (pick, prob, own, other, w_gate, w_up)
    shapes = [
        jax.ShapeDtypeStruct((2, experts, places, width), jnp.bfloat16),
        jax.ShapeDtypeStruct((experts, hidden, rows), jnp.float32),
        jax.ShapeDtypeStruct((experts, hidden, rows), jnp.float32),
        jax.ShapeDtypeStruct((experts, rows, hidden), jnp.bfloat16),
        jax.ShapeDtypeStruct((experts, hidden, rows), jnp.bfloat16),
    ]
    ins = [whole(pick.shape), each(prob.shape), whole(own.shape), whole(other.shape)]
    ins += [each(w_gate.shape), each(w_up.shape)]
    outs = [whole(shapes[0].shape)] + [each(s.shape) for s in shapes[1:]]
    flops = 4 * experts * rows * hidden * width + 2 * experts * rows * own.shape[0] * width
    return call(up_kernel, experts, ins, args, outs, shapes, flops=flops)


def slope_call(pick, prob, own, other, w_down, g, u):
    experts, hidden, width = w_down.shape
    places = pick.shape[1] // experts
    rows = 2 * places
    args = (pick, prob, own, other, w_down, g, u)
    shapes = [
        jax.ShapeDtypeStruct((2, experts, places, width), jnp.bfloat16),
        jax.ShapeDtypeStruct((experts, rows, hidden), jnp.bfloat16),
        jax.ShapeDtypeStruct((experts, rows, hidden), jnp.bfloat16),
        jax.ShapeDtypeStruct((experts, hidden, rows), jnp.bfloat16),
        jax.ShapeDtypeStruct((experts, hidden, rows), jnp.bfloat16),
        jax.ShapeDtypeStruct((experts, 1, rows), jnp.float32),
    ]
    ins = [whole(pick.shape), each(prob.shape), whole(own.shape), whole(other.shape)]
    ins += [each(w_down.shape), each(g.shape), each(u.shape)]
    outs = [whole(shapes[0].shape)] + [each(s.shape) for s in shapes[1:]]
    flops = 2 * experts * rows * hidden * width + 2 * experts * rows * own.shape[0] * width
    return call(slope_kernel, experts, ins, args, outs, shapes, flops=flops)


def back_call(put, lefts, rights):
    experts, hidden, width = rights[0].shape
    rows = lefts[0].shape[1]
    count = put.shape[1]
    terms = len(lefts)
    args = (put, *lefts, *rights)
    shapes = [jax.ShapeDtypeStruct((count, width), jnp.bfloat16)] * 2
    ins = [whole(put.shape)] + [whole(a.shape) for a in lefts]
    ins += [pl.BlockSpec((experts, hidden, CHUNK), lambda i: (0, 0, i))] * terms
    outs = [pl.BlockSpec((count, CHUNK), lambda i: (0, i))] * 2
    scratch = [pltpu.VMEM((2, put.shape[2], CHUNK), jnp.bfloat16)]
    flops = 2 * experts * rows * width * (hidden * terms + count)
    kernel = functools.partial(back_kernel, terms)
    return call(kernel, width // CHUNK, ins, args, outs, shapes, scratch, flops=flops)


def grad_call(x, lefts):
    _, experts, places, width = x.shape
    hidden = lefts[0].shape[1]
    args = (x, *lefts)
    shapes = [jax.ShapeDtypeStruct((experts, hidden, width), jnp.bfloat16)] * len(lefts)
    ins = [pl.BlockSpec((2, 1, places, width), lambda i: (0, i, 0, 0))]
    ins += [each(a.shape) for a in lefts]
    outs = [each(s.shape) for s in shapes]
    flops = 4 * experts * places * hidden * width * len(lefts)
    return call(grad_kernel, experts, ins, args, outs, shapes, flops=flops)


def dense_body(
    tokens, cotangent, gate_prob, expert_ids, placement, gate_weight, up_weight, down_weight
):
    tok_count, width = tokens.shape
    local, hidden_count, _ = gate_weight.shape
    total_experts = placement.shape[0]
    me = lax.axis_index(AXES)
    dp_size, ex_size = lax.axis_size("dp"), lax.axis_size("expert")
    devices = dp_size * ex_size
    half = devices * tok_count // 2
    places = devices // 2 * CAP

    slots = slots_of(expert_ids, placement)
    used = slots[:, :, None] == jnp.arange(total_experts, dtype=jnp.int32)
    prob = jnp.sum(jnp.where(used, gate_prob[:, :, None], 0.0), axis=1)
    prob = jnp.concatenate(gather_rows(prob))
    prob = lax.dynamic_slice_in_dim(prob, lax.axis_index("expert") * local, local, axis=1)

    prob = prob.reshape(2, devices // 2, tok_count, local).transpose(0, 3, 1, 2)
    taken = prob > 0.0
    before = jnp.arange(tok_count)[:, None] < jnp.arange(tok_count)[None, :]
    rank = dot(taken.astype(jnp.bfloat16), before.astype(jnp.bfloat16), (((3,), (0,)), ((), ())))
    block = jnp.arange(devices // 2, dtype=jnp.int32)[:, None]
    place = jnp.where(taken, rank.astype(jnp.int32) + block * CAP, -1).reshape(2, local, 1, half)
    hit = place == jnp.arange(places, dtype=jnp.int32)[:, None]
    prob_rows = jnp.sum(jnp.where(hit, prob.reshape(2, local, 1, half), 0.0), axis=3)
    prob_rows = prob_rows.transpose(1, 0, 2).reshape(local, 1, 2 * places)
    pick = hit.astype(jnp.bfloat16).reshape(2, local * places, half)
    put = pick.transpose(0, 2, 1)

    rows_own, rows_other = gather_rows(tokens)
    grads_own, grads_other = gather_rows(cotangent)

    x, g, u, h, ht = up_call(pick, prob_rows, rows_own, rows_other, gate_weight, up_weight)
    mixed = scatter_sum(*back_call(put, [h], [down_weight]), tok_count)
    c, dg, du, dgt, dut, share = slope_call(
        pick, prob_rows, grads_own, grads_other, down_weight, g, u
    )
    token_grad = scatter_sum(*back_call(put, [dg, du], [gate_weight, up_weight]), tok_count)

    share = share.reshape(local, 2, places).transpose(1, 0, 2)[:, :, :, None]
    share = jnp.sum(jnp.where(hit, share, 0.0), axis=2)
    share = share.reshape(2, local, devices // 2, tok_count).transpose(0, 2, 3, 1)
    share = share.reshape(devices, tok_count, local)
    order = me ^ arrival()[me & CORE]
    spots = jnp.arange(devices, dtype=jnp.int32)
    inverse = jnp.sum(jnp.where(order[None, :] == spots[:, None], spots[None, :], 0), axis=1)
    share = lax.all_to_all(share[inverse], AXES, split_axis=0, concat_axis=0, tiled=True)
    share = share.reshape(dp_size, ex_size, tok_count, local).sum(axis=0)
    share = share.transpose(1, 0, 2).reshape(tok_count, 1, total_experts)
    gate_grad = jnp.sum(jnp.where(used, share, 0.0), axis=2)

    down_weight_grad = grad_call(c, [ht])[0]
    gate_weight_grad, up_weight_grad = grad_call(x, [dgt, dut])
    return (mixed, token_grad, gate_grad, gate_weight_grad, up_weight_grad, down_weight_grad)


def routed_body(tokens, cotangent, gate_prob, expert_ids, placement, gate_weight, up_weight, down_weight):
    tok_count, model_width = tokens.shape
    top_count = expert_ids.shape[1]
    expert_devs = lax.axis_size("expert")
    local_experts = gate_weight.shape[0]
    total_experts = placement.shape[0]
    capacity = CAP
    flat_ids = expert_ids.reshape(-1)
    matches_id = flat_ids[:, None] == jnp.arange(total_experts, dtype=jnp.int32)[None, :]
    slot_ids = jnp.sum(jnp.where(matches_id, placement[None, :], 0), axis=1)
    pair_order = jnp.arange(flat_ids.shape[0], dtype=jnp.int32)
    earlier = (slot_ids[:, None] == slot_ids[None, :]) & (pair_order[None, :] < pair_order[:, None])
    position = slot_ids * capacity + jnp.sum(earlier.astype(jnp.int32), axis=1)
    matches = jnp.arange(total_experts * capacity, dtype=jnp.int32)[:, None] == position[None, :]
    matches = matches.reshape(total_experts * capacity, tok_count, top_count)
    dispatch = jnp.any(matches, axis=2).astype(jnp.bfloat16)
    weight_map = jnp.sum(jnp.where(matches, gate_prob[None, :, :], 0.0), axis=2)
    sent_rows = jnp.dot(dispatch, tokens, preferred_element_type=jnp.float32).astype(jnp.bfloat16)
    sent_grads = jnp.dot(
        weight_map, cotangent.astype(jnp.float32), precision=lax.Precision.HIGHEST
    ).astype(jnp.bfloat16)
    block_shape = (1, expert_devs, local_experts, capacity, model_width)
    sent_rows = sent_rows.reshape(block_shape)
    sent_grads = sent_grads.reshape(block_shape)
    got_rows, got_grads = (
        lax.all_to_all(sent_rows, "expert", split_axis=1, concat_axis=1, tiled=True),
        lax.all_to_all(sent_grads, "expert", split_axis=1, concat_axis=1, tiled=True),
    )
    routed, routed_grads = (
        lax.all_gather(got_rows, "dp", axis=0, tiled=True),
        lax.all_gather(got_grads, "dp", axis=0, tiled=True),
    )
    gate_pre = jnp.einsum(
        "asjcd,jfd->asjcf", routed, gate_weight, preferred_element_type=jnp.float32
    )
    up_pre = jnp.einsum("asjcd,jfd->asjcf", routed, up_weight, preferred_element_type=jnp.float32)
    silu_v, slope = gated(gate_pre)
    hidden = (silu_v * up_pre).astype(jnp.bfloat16)
    out_part = jnp.einsum(
        "asjcf,jfd->asjcd", hidden, down_weight, preferred_element_type=jnp.float32
    )
    d_hidden = jnp.einsum(
        "asjcd,jfd->asjcf", routed_grads, down_weight, preferred_element_type=jnp.float32
    )
    d_gate_pre = (d_hidden * up_pre * slope).astype(jnp.bfloat16)
    d_up_pre = (d_hidden * silu_v).astype(jnp.bfloat16)
    back_part = jnp.einsum(
        "asjcf,jfd->asjcd", d_gate_pre, gate_weight, preferred_element_type=jnp.float32
    )
    back_part = back_part + jnp.einsum(
        "asjcf,jfd->asjcd", d_up_pre, up_weight, preferred_element_type=jnp.float32
    )
    down_grad = jnp.einsum(
        "asjcf,asjcd->jfd", hidden, routed_grads, preferred_element_type=jnp.float32
    ).astype(jnp.bfloat16)
    gate_grad_w = jnp.einsum(
        "asjcf,asjcd->jfd", d_gate_pre, routed, preferred_element_type=jnp.float32
    ).astype(jnp.bfloat16)
    up_grad_w = jnp.einsum(
        "asjcf,asjcd->jfd", d_up_pre, routed, preferred_element_type=jnp.float32
    ).astype(jnp.bfloat16)
    summed = (
        lax.psum_scatter(
            out_part.astype(jnp.bfloat16), "dp", scatter_dimension=0, tiled=True
        ).astype(jnp.float32),
        lax.psum_scatter(
            back_part.astype(jnp.bfloat16), "dp", scatter_dimension=0, tiled=True
        ).astype(jnp.float32),
    )
    back_out, back_grad = (
        lax.all_to_all(
            summed[0].astype(jnp.bfloat16), "expert", split_axis=1, concat_axis=1, tiled=True
        ),
        lax.all_to_all(
            summed[1].astype(jnp.bfloat16), "expert", split_axis=1, concat_axis=1, tiled=True
        ),
    )
    out_flat = back_out.reshape(total_experts * capacity, model_width)
    grad_flat = back_grad.reshape(total_experts * capacity, model_width)
    chosen_out = out_flat[position].reshape(tok_count, top_count, model_width)
    chosen_grad = grad_flat[position].reshape(tok_count, top_count, model_width)
    mixed = jnp.einsum(
        "tk,tkd->td", gate_prob, chosen_out.astype(jnp.float32), precision=lax.Precision.HIGHEST
    ).astype(jnp.bfloat16)
    gate_grad = jnp.einsum("td,tkd->tk", cotangent, chosen_out, preferred_element_type=jnp.float32)
    token_grad = jnp.sum(chosen_grad.astype(jnp.float32), axis=1).astype(jnp.bfloat16)
    return (mixed, token_grad, gate_grad, gate_grad_w, up_grad_w, down_grad)


def body(*args):
    tokens, gate_weight = args[0], args[5]
    mesh_fits = (lax.axis_size("dp"), lax.axis_size("expert")) == (4, 8)
    if mesh_fits and tokens.shape[0] <= gate_weight.shape[0] * CAP:
        return dense_body(*args)
    return routed_body(*args)


def solution(mesh):
    return jax.shard_map(
        body,
        mesh=mesh,
        in_specs=(
            P(("dp", "expert"), None),
            P(("dp", "expert"), None),
            P(("dp", "expert"), None),
            P(("dp", "expert"), None),
            P(),
            P("expert", "dp", None),
            P("expert", "dp", None),
            P("expert", "dp", None),
        ),
        out_specs=(
            P(("dp", "expert"), None),
            P(("dp", "expert"), None),
            P(("dp", "expert"), None),
            P("expert", "dp", None),
            P("expert", "dp", None),
            P("expert", "dp", None),
        ),
        check_vma=False,
    )
```

```python
import functools

import jax
import jax.numpy as jnp
from jax import lax
from jax.experimental import pallas as pl
from jax.experimental.pallas import tpu as pltpu
from jax.sharding import PartitionSpec as P

CAP = 3
AXES = ("dp", "expert")
CORE, Z1, Z2, Z3, X, Y = 1, 2, 4, 6, 8, 16
GROUPS = ((0,), (1, 2), (3,))
CHUNK = 512
MIB = 1 << 20

NT = (((1,), (1,)), ((), ()))
NN = (((1,), (0,)), ((), ()))


def gated(values):
    sigmoid_v = jax.nn.sigmoid(values)
    return (values * sigmoid_v, sigmoid_v * (1.0 + values * (1.0 - sigmoid_v)))


def swap(values, even, odd=None):
    odd = even if odd is None else odd
    count = lax.axis_size("dp") * lax.axis_size("expert")
    pairs = [(i, i ^ (odd if i & CORE else even)) for i in range(count)]
    return lax.ppermute(values, AXES, pairs)


def add(*parts):
    total = parts[0].astype(jnp.float32)
    for part in parts[1:]:
        total = total + part.astype(jnp.float32)
    return total.astype(jnp.bfloat16)


def together(*values):
    return lax.optimization_barrier(values)


def slots_of(expert_ids, placement):
    total = placement.shape[0]
    matches = expert_ids[:, :, None] == jnp.arange(total, dtype=jnp.int32)
    return jnp.sum(jnp.where(matches, placement, 0), axis=2)


def dot(a, b, dims=NN):
    return lax.dot_general(a, b, dims, preferred_element_type=jnp.float32)


def iota(shape, axis):
    return lax.broadcasted_iota(jnp.int32, shape, axis)


def fetch(x_ref, e):
    return jnp.concatenate([x_ref[0, e], x_ref[1, e]], axis=0)


def dispatch(pick, rows_ref, half, x_ref):
    experts, places, width = x_ref.shape[1:]
    for at in range(0, width, CHUNK):
        rows = dot(pick, rows_ref[half, :, at : at + CHUNK]).astype(jnp.bfloat16)
        for e in range(experts):
            x_ref[half, e, :, at : at + CHUNK] = rows[e * places : (e + 1) * places]


def join_groups(pieces, rows_ref, half, tok_count):
    for piece, group in zip(pieces, GROUPS):
        size = len(group) * tok_count
        for quarter in range(4):
            at = (quarter * 4 + group[0]) * tok_count
            rows_ref[half, at : at + size] = piece[quarter * size : (quarter + 1) * size]


def up_kernel(tok_count, own0, own1, own2, other0, other1, other2, mine_ref, mine_t_ref, both_t_ref,
              gate_ref, up_ref, x_out, put_ref, pick_ref, prob_ref, g_ref, u_ref, h_ref, ht_ref,
              rows_ref, x_ref, sem):
    e = pl.program_id(0)
    experts, places, width = x_ref.shape[1:]
    count = rows_ref.shape[1]

    @pl.when(e == 0)
    def _():
        join_groups((own0, own1, own2), rows_ref, 0, tok_count)
        join_groups((other0, other1, other2), rows_ref, 1, tok_count)
        row, col = iota((count, count), 0), iota((count, count), 1)
        block = lax.div(row, tok_count)
        before = ((col < row) & (lax.div(col, tok_count) == block)).astype(jnp.bfloat16)
        columns = both_t_ref.shape[1]
        first = (lax.div(iota((count, columns), 0), tok_count) * CAP).astype(jnp.float32)
        spot = lax.rem(iota((count, experts * places), 1), places).astype(jnp.float32)
        spot_t = lax.rem(iota((experts * places, count), 0), places).astype(jnp.float32)
        for half in range(2):
            prob = rows_ref[half, :, width:]
            taken = prob.astype(jnp.float32) > 0.0
            rank = dot(before, jnp.where(taken, 1.0, 0.0).astype(jnp.bfloat16))
            place = jnp.where(taken, rank + first, -1.0).astype(jnp.bfloat16)
            put = jnp.where(dot(place, mine_ref[...]) == spot, 1.0, 0.0).astype(jnp.bfloat16)
            pick = dot(mine_t_ref[...], place, NT) == spot_t
            pick = jnp.where(pick, 1.0, 0.0).astype(jnp.bfloat16)
            put_ref[half] = put
            pick_ref[half] = pick
            weight = jnp.sum(dot(pick, prob) * both_t_ref[...], axis=1, keepdims=True)
            weight = jnp.broadcast_to(weight, (experts * places, columns))
            for i in range(experts):
                prob_ref[half, i] = weight[i * places : (i + 1) * places]
            dispatch(pick, rows_ref, half, x_ref)
        pltpu.make_async_copy(x_ref, x_out, sem).start()

    rows = fetch(x_ref, e)
    g = dot(rows, gate_ref[0], NT)
    u = dot(rows, up_ref[0], NT)
    g_ref[0] = g
    u_ref[0] = u
    silu_v, _ = gated(g)
    scaled = silu_v * u * fetch(prob_ref, e)[:, :1]
    h_ref[0] = scaled.astype(jnp.bfloat16)
    ht_ref[0] = scaled.T.astype(jnp.bfloat16)

    @pl.when(e == pl.num_programs(0) - 1)
    def _():
        pltpu.make_async_copy(x_ref, x_out, sem).wait()


def slope_kernel(own0, own1, other0, other1, pick_ref, put_ref, prob_ref, mine_ref, down_ref, g_ref, u_ref,
                 x_out, dg_ref, du_ref, dgt_ref, dut_ref, share_ref, rows_ref, x_ref, terms_ref, sem):
    e = pl.program_id(0)
    places = x_ref.shape[2]

    @pl.when(e == 0)
    def _():
        for half, pieces in enumerate(((own0, own1), (other0, other1))):
            size = own0.shape[0]
            rows_ref[half, :size] = pieces[0][...]
            rows_ref[half, size:] = pieces[1][...]
            dispatch(pick_ref[half], rows_ref, half, x_ref)
        pltpu.make_async_copy(x_ref, x_out, sem).start()

    plain = dot(fetch(x_ref, e), down_ref[0], NT)
    g, u = g_ref[0], u_ref[0]
    silu_v, slope = gated(g)
    share = jnp.sum(silu_v * u * plain, axis=1, keepdims=True)
    for half in range(2):
        part = share[half * places : (half + 1) * places] * mine_ref[e].astype(jnp.float32)
        terms_ref[half, e] = part.astype(jnp.bfloat16)
    scaled = plain * fetch(prob_ref, e)[:, :1]
    dg = scaled * u * slope
    du = scaled * silu_v
    dg_ref[0] = dg.astype(jnp.bfloat16)
    du_ref[0] = du.astype(jnp.bfloat16)
    dgt_ref[0] = dg.T.astype(jnp.bfloat16)
    dut_ref[0] = du.T.astype(jnp.bfloat16)

    @pl.when(e == pl.num_programs(0) - 1)
    def _():
        for half in range(2):
            terms = terms_ref[half].reshape(put_ref.shape[2], terms_ref.shape[3])
            share_ref[half] = dot(put_ref[half], terms).astype(jnp.bfloat16)
        pltpu.make_async_copy(x_ref, x_out, sem).wait()


def back_kernel(terms, steps, put_ref, *refs):
    lefts, rights = refs[:terms], refs[terms : 2 * terms]
    extra_ref = refs[2 * terms] if len(refs) > 2 * terms + 3 else None
    own_ref, other_ref, rows_ref = refs[-3:]
    experts, places = rights[0].shape[0], put_ref.shape[2] // rights[0].shape[0]

    @pl.when(pl.program_id(0) < steps)
    def _():
        for e in range(experts):
            rows = dot(lefts[0][e], rights[0][e])
            for left, right in zip(lefts[1:], rights[1:]):
                rows = rows + dot(left[e], right[e])
            rows = rows.astype(jnp.bfloat16)
            for half in range(2):
                rows_ref[half, e * places : (e + 1) * places] = rows[half * places : (half + 1) * places]
        own_ref[...] = dot(put_ref[0], rows_ref[0]).astype(jnp.bfloat16)
        other_ref[...] = dot(put_ref[1], rows_ref[1]).astype(jnp.bfloat16)

    if extra_ref is not None:

        @pl.when(pl.program_id(0) == steps)
        def _():
            columns = extra_ref.shape[2]
            own_ref[:, :columns] = extra_ref[0]
            other_ref[:, :columns] = extra_ref[1]


def grad_kernel(x_ref, left, out):
    rows = jnp.concatenate([x_ref[0, 0], x_ref[1, 0]], axis=0)
    for at in range(0, rows.shape[1], CHUNK):
        out[0, :, at : at + CHUNK] = dot(left[0], rows[:, at : at + CHUNK]).astype(jnp.bfloat16)


def whole(a):
    shape = a.shape
    return pl.BlockSpec(shape, lambda i: (0,) * len(shape))


def each(a):
    shape = a.shape
    return pl.BlockSpec((1, *shape[1:]), lambda i: (i,) + (0,) * (len(shape) - 1))


def bf16(*shape):
    return jax.ShapeDtypeStruct(shape, jnp.bfloat16)


def f32(*shape):
    return jax.ShapeDtypeStruct(shape, jnp.float32)


def call(kernel, grid, ins, args, outs, shapes, scratch=(), flops=0):
    moved = sum(a.size * a.dtype.itemsize for a in (*args, *shapes))
    return pl.pallas_call(
        kernel,
        grid=(grid,),
        in_specs=ins,
        out_specs=outs,
        out_shape=shapes,
        scratch_shapes=scratch,
        compiler_params=pltpu.CompilerParams(vmem_limit_bytes=56 * MIB),
        cost_estimate=pl.CostEstimate(flops=flops, bytes_accessed=moved, transcendentals=0),
    )(*args)


def up_call(own, other, maps, w_gate, w_up, tok_count):
    experts, hidden, width = w_gate.shape
    held = own[0].shape[1]
    count = sum(piece.shape[0] for piece in own)
    columns = held - width
    places = count // tok_count * CAP
    rows = 2 * places
    args = (*own, *other, *maps, w_gate, w_up)
    shapes = [
        bf16(2, experts, places, width),
        bf16(2, count, experts * places),
        bf16(2, experts * places, count),
        f32(2, experts, places, columns),
        f32(experts, rows, hidden),
        f32(experts, rows, hidden),
        bf16(experts, rows, hidden),
        bf16(experts, hidden, rows),
    ]
    ins = [whole(a) for a in args[:-2]] + [each(w_gate), each(w_up)]
    outs = [pl.BlockSpec(memory_space=pl.ANY)]
    outs += [whole(s) for s in shapes[1:4]] + [each(s) for s in shapes[4:]]
    scratch = [
        pltpu.VMEM((2, count, held), jnp.bfloat16),
        pltpu.VMEM((2, experts, places, width), jnp.bfloat16),
        pltpu.SemaphoreType.DMA,
    ]
    flops = 4 * experts * rows * hidden * width + 2 * experts * rows * count * width
    return call(
        functools.partial(up_kernel, tok_count), experts, ins, args, outs, shapes, scratch, flops
    )


def slope_call(own, other, pick, put, prob, mine, w_down, g, u):
    experts, hidden, width = w_down.shape
    count, places, columns = pick.shape[2], prob.shape[2], prob.shape[3]
    rows = 2 * places
    args = (*own, *other, pick, put, prob, mine, w_down, g, u)
    shapes = [
        bf16(2, experts, places, width),
        bf16(experts, rows, hidden),
        bf16(experts, rows, hidden),
        bf16(experts, hidden, rows),
        bf16(experts, hidden, rows),
        bf16(2, count, columns),
    ]
    ins = [whole(a) for a in args[:-3]] + [each(w_down), each(g), each(u)]
    outs = [pl.BlockSpec(memory_space=pl.ANY)]
    outs += [each(s) for s in shapes[1:5]] + [whole(shapes[5])]
    scratch = [
        pltpu.VMEM((2, count, width), jnp.bfloat16),
        pltpu.VMEM((2, experts, places, width), jnp.bfloat16),
        pltpu.VMEM((2, experts, places, columns), jnp.bfloat16),
        pltpu.SemaphoreType.DMA,
    ]
    flops = 2 * experts * rows * hidden * width + 2 * experts * rows * count * width
    return call(slope_kernel, experts, ins, args, outs, shapes, scratch, flops)


def back_call(put, lefts, rights, start, stop, extra=None):
    experts, hidden, _ = rights[0].shape
    rows = lefts[0].shape[1]
    count = put.shape[1]
    terms = len(lefts)
    first, steps = start // CHUNK, (stop - start) // CHUNK
    columns = stop - start + (0 if extra is None else extra.shape[2])
    args = (put, *lefts, *rights) + (() if extra is None else (extra,))
    shapes = [bf16(count, columns)] * 2
    ins = [whole(put)] + [whole(a) for a in lefts]
    last = first + steps - 1
    ins += [
        pl.BlockSpec((experts, hidden, CHUNK), lambda i: (0, 0, jnp.minimum(first + i, last)))
    ] * terms
    ins += [] if extra is None else [whole(extra)]
    outs = [pl.BlockSpec((count, CHUNK), lambda i: (0, i))] * 2
    scratch = [pltpu.VMEM((2, put.shape[2], CHUNK), jnp.bfloat16)]
    flops = 2 * experts * rows * (stop - start) * (hidden * terms + count)
    kernel = functools.partial(back_kernel, terms, steps)
    grid = steps + (0 if extra is None else 1)
    return call(kernel, grid, ins, args, outs, shapes, scratch, flops)


def grad_call(x, left):
    _, experts, places, width = x.shape
    hidden = left.shape[1]
    shape = bf16(experts, hidden, width)
    ins = [pl.BlockSpec((2, 1, places, width), lambda i: (0, i, 0, 0)), each(left)]
    flops = 4 * experts * places * hidden * width
    return call(grad_kernel, experts, ins, (x, left), [each(shape)], [shape], flops=flops)[0]


def dense_body(
    tokens, cotangent, gate_prob, expert_ids, placement, gate_weight, up_weight, down_weight
):
    tok_count, width = tokens.shape
    local = gate_weight.shape[0]
    total_experts = placement.shape[0]
    devices = lax.axis_size("dp") * lax.axis_size("expert")
    places = devices // 2 * CAP
    count = devices // 2 * tok_count
    quarter, middle = count // 4, width // 2

    slots = slots_of(expert_ids, placement)
    used = slots[:, :, None] == jnp.arange(total_experts, dtype=jnp.int32)
    prob = jnp.sum(jnp.where(used, gate_prob[:, :, None], 0.0), axis=1)
    high = lax.reduce_precision(prob, 8, 7)
    extended = jnp.concatenate(
        [tokens, high.astype(jnp.bfloat16), (prob - high).astype(jnp.bfloat16)], axis=1
    )

    slot = lax.axis_index("expert") * local + jnp.arange(local * places, dtype=jnp.int32) // places
    spots = jnp.arange(2 * total_experts, dtype=jnp.int32)
    mine = (slot[:, None] == spots[None, :]).astype(jnp.bfloat16)
    both = (slot[:, None] == spots[None, :] % total_experts).astype(jnp.float32)
    maps = ((slot[None, :] == spots[:, None]).astype(jnp.bfloat16), mine, both)

    near, far = swap(extended, Z1), swap(extended, Z2)
    cotangent, near, far = together(cotangent, near, far)
    own, other = [], []
    for rows in (extended, jnp.concatenate([near, far]), swap(far, Z1)):
        rows = jnp.concatenate([rows, swap(rows, X, Y)])
        rows = jnp.concatenate([rows, swap(rows, Y, X)])
        own.append(rows)
        other.append(swap(rows, CORE))

    grads = jnp.concatenate([cotangent] + [swap(cotangent, bit) for bit in (Z1, Z2, Z3)])
    grads = jnp.concatenate([grads, swap(grads, X, Y)])
    *rows, grads = together(*own, *other, grads)
    far_grads = swap(grads, Y, X)
    grads_other = swap(grads, CORE)

    x, put, pick, prob_rows, g, u, h, ht = up_call(
        rows[:3], rows[3:], maps, gate_weight, up_weight, tok_count
    )
    h, far_grads = together(h, far_grads)
    far_grads_other = swap(far_grads, CORE)

    sums, sums_other = back_call(put, [h], [down_weight], 0, width)
    sums = add(sums, swap(sums_other, CORE))
    sums, far_grads_other = together(sums, far_grads_other)
    from_second = swap(sums[2 * quarter :], Y, X)

    c, dg, du, dgt, dut, share = slope_call(
        (grads, far_grads),
        (grads_other, far_grads_other),
        pick,
        put,
        prob_rows,
        mine.reshape(local, places, -1),
        down_weight,
        g,
        u,
    )
    weights = [gate_weight, up_weight]
    left, left_other = back_call(put, [dg, du], weights, 0, middle)
    from_left = swap(left_other, CORE)
    from_second, left, dg, du = together(from_second, left, dg, du)
    sums = add(sums[: 2 * quarter], from_second)
    sums, dg, du = together(sums, dg, du)
    from_first = swap(sums[quarter:], X, Y)
    right, right_other = back_call(put, [dg, du], weights, middle, width, share)

    from_right = swap(right_other, CORE)
    from_left, right = together(from_left, right)
    left = add(left, from_left)
    left, ht = together(left, ht)
    from_left = swap(left[2 * quarter :], Y, X)
    down_weight_grad = grad_call(c, ht)

    from_right, from_first, down_weight_grad = together(from_right, from_first, down_weight_grad)
    right = add(right, from_right)
    sums = add(sums[:quarter], from_first)
    right, sums, dgt = together(right, sums, dgt)
    from_right = swap(right[2 * quarter :], Y, X)

    def over_z(values):
        parts = [values[i * tok_count : (i + 1) * tok_count] for i in range(4)]
        return parts[:1] + [swap(part, bit) for part, bit in zip(parts[1:], (Z1, Z2, Z3))]

    mixed = over_z(sums)
    gate_weight_grad = grad_call(x, dgt)

    from_left, gate_weight_grad = together(from_left, gate_weight_grad)
    left = add(left[: 2 * quarter], from_left)
    left, dut = together(left, dut)
    from_left = swap(left[quarter:], X, Y)
    up_weight_grad = grad_call(x, dut)

    from_right, up_weight_grad = together(from_right, up_weight_grad)
    right = add(right[: 2 * quarter], from_right)
    from_right = swap(right[quarter:], X, Y)
    left = over_z(add(left[:quarter], from_left))
    right = add(*over_z(add(right[:quarter], from_right)))
    token_grad = jnp.concatenate([add(*left), right[:, : width - middle]], axis=1)
    share = right[:, width - middle : width - middle + total_experts].astype(jnp.float32)
    gate_grad = jnp.sum(jnp.where(used, share[:, None, :], 0.0), axis=2)
    return (add(*mixed), token_grad, gate_grad, gate_weight_grad, up_weight_grad, down_weight_grad)


def routed_body(tokens, cotangent, gate_prob, expert_ids, placement, gate_weight, up_weight, down_weight):
    tok_count, model_width = tokens.shape
    top_count = expert_ids.shape[1]
    expert_devs = lax.axis_size("expert")
    local_experts = gate_weight.shape[0]
    total_experts = placement.shape[0]
    capacity = CAP
    flat_ids = expert_ids.reshape(-1)
    matches_id = flat_ids[:, None] == jnp.arange(total_experts, dtype=jnp.int32)[None, :]
    slot_ids = jnp.sum(jnp.where(matches_id, placement[None, :], 0), axis=1)
    pair_order = jnp.arange(flat_ids.shape[0], dtype=jnp.int32)
    earlier = (slot_ids[:, None] == slot_ids[None, :]) & (pair_order[None, :] < pair_order[:, None])
    position = slot_ids * capacity + jnp.sum(earlier.astype(jnp.int32), axis=1)
    matches = jnp.arange(total_experts * capacity, dtype=jnp.int32)[:, None] == position[None, :]
    matches = matches.reshape(total_experts * capacity, tok_count, top_count)
    dispatch = jnp.any(matches, axis=2).astype(jnp.bfloat16)
    weight_map = jnp.sum(jnp.where(matches, gate_prob[None, :, :], 0.0), axis=2)
    sent_rows = jnp.dot(dispatch, tokens, preferred_element_type=jnp.float32).astype(jnp.bfloat16)
    sent_grads = jnp.dot(
        weight_map, cotangent.astype(jnp.float32), precision=lax.Precision.HIGHEST
    ).astype(jnp.bfloat16)
    block_shape = (1, expert_devs, local_experts, capacity, model_width)
    sent_rows = sent_rows.reshape(block_shape)
    sent_grads = sent_grads.reshape(block_shape)
    got_rows, got_grads = (
        lax.all_to_all(sent_rows, "expert", split_axis=1, concat_axis=1, tiled=True),
        lax.all_to_all(sent_grads, "expert", split_axis=1, concat_axis=1, tiled=True),
    )
    routed, routed_grads = (
        lax.all_gather(got_rows, "dp", axis=0, tiled=True),
        lax.all_gather(got_grads, "dp", axis=0, tiled=True),
    )
    gate_pre = jnp.einsum(
        "asjcd,jfd->asjcf", routed, gate_weight, preferred_element_type=jnp.float32
    )
    up_pre = jnp.einsum("asjcd,jfd->asjcf", routed, up_weight, preferred_element_type=jnp.float32)
    silu_v, slope = gated(gate_pre)
    hidden = (silu_v * up_pre).astype(jnp.bfloat16)
    out_part = jnp.einsum(
        "asjcf,jfd->asjcd", hidden, down_weight, preferred_element_type=jnp.float32
    )
    d_hidden = jnp.einsum(
        "asjcd,jfd->asjcf", routed_grads, down_weight, preferred_element_type=jnp.float32
    )
    d_gate_pre = (d_hidden * up_pre * slope).astype(jnp.bfloat16)
    d_up_pre = (d_hidden * silu_v).astype(jnp.bfloat16)
    back_part = jnp.einsum(
        "asjcf,jfd->asjcd", d_gate_pre, gate_weight, preferred_element_type=jnp.float32
    )
    back_part = back_part + jnp.einsum(
        "asjcf,jfd->asjcd", d_up_pre, up_weight, preferred_element_type=jnp.float32
    )
    down_grad = jnp.einsum(
        "asjcf,asjcd->jfd", hidden, routed_grads, preferred_element_type=jnp.float32
    ).astype(jnp.bfloat16)
    gate_grad_w = jnp.einsum(
        "asjcf,asjcd->jfd", d_gate_pre, routed, preferred_element_type=jnp.float32
    ).astype(jnp.bfloat16)
    up_grad_w = jnp.einsum(
        "asjcf,asjcd->jfd", d_up_pre, routed, preferred_element_type=jnp.float32
    ).astype(jnp.bfloat16)
    summed = (
        lax.psum_scatter(
            out_part.astype(jnp.bfloat16), "dp", scatter_dimension=0, tiled=True
        ).astype(jnp.float32),
        lax.psum_scatter(
            back_part.astype(jnp.bfloat16), "dp", scatter_dimension=0, tiled=True
        ).astype(jnp.float32),
    )
    back_out, back_grad = (
        lax.all_to_all(
            summed[0].astype(jnp.bfloat16), "expert", split_axis=1, concat_axis=1, tiled=True
        ),
        lax.all_to_all(
            summed[1].astype(jnp.bfloat16), "expert", split_axis=1, concat_axis=1, tiled=True
        ),
    )
    out_flat = back_out.reshape(total_experts * capacity, model_width)
    grad_flat = back_grad.reshape(total_experts * capacity, model_width)
    chosen_out = out_flat[position].reshape(tok_count, top_count, model_width)
    chosen_grad = grad_flat[position].reshape(tok_count, top_count, model_width)
    mixed = jnp.einsum(
        "tk,tkd->td", gate_prob, chosen_out.astype(jnp.float32), precision=lax.Precision.HIGHEST
    ).astype(jnp.bfloat16)
    gate_grad = jnp.einsum("td,tkd->tk", cotangent, chosen_out, preferred_element_type=jnp.float32)
    token_grad = jnp.sum(chosen_grad.astype(jnp.float32), axis=1).astype(jnp.bfloat16)
    return (mixed, token_grad, gate_grad, gate_grad_w, up_grad_w, down_grad)


def body(*args):
    tokens, gate_weight = args[0], args[5]
    mesh_fits = (lax.axis_size("dp"), lax.axis_size("expert")) == (4, 8)
    if mesh_fits and tokens.shape[0] <= gate_weight.shape[0] * CAP:
        return dense_body(*args)
    return routed_body(*args)


def solution(mesh):
    return jax.shard_map(
        body,
        mesh=mesh,
        in_specs=(
            P(("dp", "expert"), None),
            P(("dp", "expert"), None),
            P(("dp", "expert"), None),
            P(("dp", "expert"), None),
            P(),
            P("expert", "dp", None),
            P("expert", "dp", None),
            P("expert", "dp", None),
        ),
        out_specs=(
            P(("dp", "expert"), None),
            P(("dp", "expert"), None),
            P(("dp", "expert"), None),
            P("expert", "dp", None),
            P("expert", "dp", None),
            P("expert", "dp", None),
        ),
        check_vma=False,
    )
```

```python
import functools

import jax
import jax.numpy as jnp
from jax import lax
from jax.experimental import pallas as pl
from jax.experimental.pallas import tpu as pltpu
from jax.sharding import PartitionSpec as P

CAP = 3
AXES = ("dp", "expert")
CORE, Z1, Z2, Z3, X, Y = 1, 2, 4, 6, 8, 16
GROUPS = ((0,), (1, 2), (3,))
CHUNK = 512
MIB = 1 << 20

NT = (((1,), (1,)), ((), ()))
NN = (((1,), (0,)), ((), ()))


def gated(values):
    sigmoid_v = jax.nn.sigmoid(values)
    return (values * sigmoid_v, sigmoid_v * (1.0 + values * (1.0 - sigmoid_v)))


def swap(values, even, odd=None):
    odd = even if odd is None else odd
    count = lax.axis_size("dp") * lax.axis_size("expert")
    pairs = [(i, i ^ (odd if i & CORE else even)) for i in range(count)]
    return lax.ppermute(values, AXES, pairs)


def add(*parts):
    total = parts[0].astype(jnp.float32)
    for part in parts[1:]:
        total = total + part.astype(jnp.float32)
    return total.astype(jnp.bfloat16)


def together(*values):
    return lax.optimization_barrier(values)


def slots_of(expert_ids, placement):
    total = placement.shape[0]
    matches = expert_ids[:, :, None] == jnp.arange(total, dtype=jnp.int32)
    return jnp.sum(jnp.where(matches, placement, 0), axis=2)


def dot(a, b, dims=NN):
    return lax.dot_general(a, b, dims, preferred_element_type=jnp.float32)


def iota(shape, axis):
    return lax.broadcasted_iota(jnp.int32, shape, axis)


def expert_copy(source, held, sems, e):
    return pltpu.make_async_copy(source.at[e], held.at[e], sems.at[e])


def dispatch(pick, rows_ref, half, x_ref):
    experts, both, width = x_ref.shape
    places = both // 2
    for at in range(0, width, CHUNK):
        rows = dot(pick, rows_ref[half, :, at : at + CHUNK]).astype(jnp.bfloat16)
        for e in range(experts):
            x_ref[e, half * places : (half + 1) * places, at : at + CHUNK] = rows[
                e * places : (e + 1) * places
            ]


def join_groups(pieces, rows_ref, half, tok_count):
    for piece, group in zip(pieces, GROUPS):
        size = len(group) * tok_count
        for quarter in range(4):
            at = (quarter * 4 + group[0]) * tok_count
            rows_ref[half, at : at + size] = piece[quarter * size : (quarter + 1) * size]


def up_kernel(tok_count, own0, own1, own2, other0, other1, other2, mine_ref, mine_t_ref, both_t_ref,
              gate_ref, up_ref, x_out, put_ref, pick_ref, prob_ref, g_ref, u_ref, h_ref, ht_ref,
              rows_ref, x_ref, held_ref, held_sems, sem):
    e = pl.program_id(0)
    experts, both, width = x_ref.shape
    places = both // 2
    count = rows_ref.shape[1]

    @pl.when(e == 0)
    def _():
        for i in range(experts):
            expert_copy(gate_ref, held_ref.at[0], held_sems.at[0], i).start()
            expert_copy(up_ref, held_ref.at[1], held_sems.at[1], i).start()
        join_groups((own0, own1, own2), rows_ref, 0, tok_count)
        join_groups((other0, other1, other2), rows_ref, 1, tok_count)
        row, col = iota((count, count), 0), iota((count, count), 1)
        block = lax.div(row, tok_count)
        before = ((col < row) & (lax.div(col, tok_count) == block)).astype(jnp.bfloat16)
        columns = both_t_ref.shape[1]
        first = (lax.div(iota((count, columns), 0), tok_count) * CAP).astype(jnp.float32)
        spot = lax.rem(iota((count, experts * places), 1), places).astype(jnp.float32)
        spot_t = lax.rem(iota((experts * places, count), 0), places).astype(jnp.float32)
        for half in range(2):
            prob = rows_ref[half, :, width:]
            taken = prob.astype(jnp.float32) > 0.0
            rank = dot(before, jnp.where(taken, 1.0, 0.0).astype(jnp.bfloat16))
            place = jnp.where(taken, rank + first, -1.0).astype(jnp.bfloat16)
            put = jnp.where(dot(place, mine_ref[...]) == spot, 1.0, 0.0).astype(jnp.bfloat16)
            pick = dot(mine_t_ref[...], place, NT) == spot_t
            pick = jnp.where(pick, 1.0, 0.0).astype(jnp.bfloat16)
            put_ref[half] = put
            pick_ref[half] = pick
            weight = jnp.sum(dot(pick, prob) * both_t_ref[...], axis=1, keepdims=True)
            weight = jnp.broadcast_to(weight, (experts * places, columns))
            for i in range(experts):
                prob_ref[i, half * places : (half + 1) * places] = weight[i * places : (i + 1) * places]
            dispatch(pick, rows_ref, half, x_ref)
        pltpu.make_async_copy(x_ref, x_out, sem).start()

    rows = x_ref[e]
    expert_copy(gate_ref, held_ref.at[0], held_sems.at[0], e).wait()
    g = dot(rows, held_ref[0, e], NT)
    expert_copy(up_ref, held_ref.at[1], held_sems.at[1], e).wait()
    u = dot(rows, held_ref[1, e], NT)
    g_ref[0] = g
    u_ref[0] = u
    silu_v, _ = gated(g)
    scaled = silu_v * u * prob_ref[e][:, :1]
    h_ref[0] = scaled.astype(jnp.bfloat16)
    ht_ref[0] = scaled.T.astype(jnp.bfloat16)

    @pl.when(e == pl.num_programs(0) - 1)
    def _():
        pltpu.make_async_copy(x_ref, x_out, sem).wait()


def slope_kernel(own0, own1, other0, other1, pick_ref, put_ref, prob_ref, mine_ref, down_ref, g_ref, u_ref,
                 x_out, dg_ref, du_ref, dgt_ref, dut_ref, share_ref, rows_ref, x_ref, terms_ref,
                 held_ref, held_sems, sem):
    e = pl.program_id(0)
    experts = x_ref.shape[0]
    places = x_ref.shape[1] // 2

    @pl.when(e == 0)
    def _():
        for i in range(experts):
            expert_copy(down_ref, held_ref, held_sems, i).start()
        for half, pieces in enumerate(((own0, own1), (other0, other1))):
            size = own0.shape[0]
            rows_ref[half, :size] = pieces[0][...]
            rows_ref[half, size:] = pieces[1][...]
            dispatch(pick_ref[half], rows_ref, half, x_ref)
        pltpu.make_async_copy(x_ref, x_out, sem).start()

    expert_copy(down_ref, held_ref, held_sems, e).wait()
    plain = dot(x_ref[e], held_ref[e], NT)
    g, u = g_ref[0], u_ref[0]
    silu_v, slope = gated(g)
    share = jnp.sum(silu_v * u * plain, axis=1, keepdims=True)
    for half in range(2):
        part = share[half * places : (half + 1) * places] * mine_ref[e].astype(jnp.float32)
        terms_ref[half, e] = part.astype(jnp.bfloat16)
    scaled = plain * prob_ref[e][:, :1]
    dg = scaled * u * slope
    du = scaled * silu_v
    dg_ref[0] = dg.astype(jnp.bfloat16)
    du_ref[0] = du.astype(jnp.bfloat16)
    dgt_ref[0] = dg.T.astype(jnp.bfloat16)
    dut_ref[0] = du.T.astype(jnp.bfloat16)

    @pl.when(e == pl.num_programs(0) - 1)
    def _():
        for half in range(2):
            terms = terms_ref[half].reshape(put_ref.shape[2], terms_ref.shape[3])
            share_ref[half] = dot(put_ref[half], terms).astype(jnp.bfloat16)
        pltpu.make_async_copy(x_ref, x_out, sem).wait()


def back_kernel(terms, start, steps, put_ref, *refs):
    lefts, rights = refs[:terms], refs[terms : 2 * terms]
    extra_ref = refs[2 * terms] if len(refs) > 2 * terms + 5 else None
    own_ref, other_ref, rows_ref, held_ref, sems = refs[-5:]
    experts, places = rights[0].shape[0], put_ref.shape[2] // rights[0].shape[0]
    step = pl.program_id(0)

    def copy(i, at):
        columns = pl.ds(pl.multiple_of(start + at * CHUNK, CHUNK), CHUNK)
        return pltpu.make_async_copy(rights[i].at[:, :, columns], held_ref.at[i, at], sems.at[i, at])

    @pl.when(step == 0)
    def _():
        for at in range(steps):
            for i in range(terms):
                copy(i, at).start()

    @pl.when(step < steps)
    def _():
        for i in range(terms):
            copy(i, step).wait()
        for e in range(experts):
            rows = dot(lefts[0][e], held_ref[0, step, e])
            for i in range(1, terms):
                rows = rows + dot(lefts[i][e], held_ref[i, step, e])
            rows = rows.astype(jnp.bfloat16)
            for half in range(2):
                rows_ref[half, e * places : (e + 1) * places] = rows[half * places : (half + 1) * places]
        own_ref[...] = dot(put_ref[0], rows_ref[0]).astype(jnp.bfloat16)
        other_ref[...] = dot(put_ref[1], rows_ref[1]).astype(jnp.bfloat16)

    if extra_ref is not None:

        @pl.when(step == steps)
        def _():
            columns = extra_ref.shape[2]
            own_ref[:, :columns] = extra_ref[0]
            other_ref[:, :columns] = extra_ref[1]


def grad_kernel(x_ref, *refs):
    count = len(refs) // 2
    for at in range(0, x_ref.shape[2], CHUNK):
        rows = x_ref[0, :, at : at + CHUNK]
        for left, out in zip(refs[:count], refs[count:]):
            out[0, :, at : at + CHUNK] = dot(left[0], rows).astype(jnp.bfloat16)


def whole(a):
    shape = a.shape
    return pl.BlockSpec(shape, lambda i: (0,) * len(shape), pipeline_mode=pl.Buffered(1))


def kept(a):
    shape = a.shape
    return pl.BlockSpec(shape, lambda i: (0,) * len(shape))


def each(a):
    shape = a.shape
    return pl.BlockSpec((1, *shape[1:]), lambda i: (i,) + (0,) * (len(shape) - 1))


def bf16(*shape):
    return jax.ShapeDtypeStruct(shape, jnp.bfloat16)


def f32(*shape):
    return jax.ShapeDtypeStruct(shape, jnp.float32)


def call(kernel, grid, ins, args, outs, shapes, scratch=(), flops=0):
    moved = sum(a.size * a.dtype.itemsize for a in (*args, *shapes))
    return pl.pallas_call(
        kernel,
        grid=(grid,),
        in_specs=ins,
        out_specs=outs,
        out_shape=shapes,
        scratch_shapes=scratch,
        compiler_params=pltpu.CompilerParams(vmem_limit_bytes=56 * MIB),
        cost_estimate=pl.CostEstimate(flops=flops, bytes_accessed=moved, transcendentals=0),
    )(*args)


def up_call(own, other, maps, w_gate, w_up, tok_count):
    experts, hidden, width = w_gate.shape
    held = own[0].shape[1]
    count = sum(piece.shape[0] for piece in own)
    columns = held - width
    places = count // tok_count * CAP
    rows = 2 * places
    args = (*own, *other, *maps, w_gate, w_up)
    shapes = [
        bf16(experts, rows, width),
        bf16(2, count, experts * places),
        bf16(2, experts * places, count),
        f32(experts, rows, columns),
        f32(experts, rows, hidden),
        f32(experts, rows, hidden),
        bf16(experts, rows, hidden),
        bf16(experts, hidden, rows),
    ]
    ins = [whole(a) for a in args[:-2]] + [pl.BlockSpec(memory_space=pl.ANY)] * 2
    outs = [pl.BlockSpec(memory_space=pl.ANY)]
    outs += [kept(s) for s in shapes[1:4]] + [each(s) for s in shapes[4:]]
    scratch = [
        pltpu.VMEM((2, count, held), jnp.bfloat16),
        pltpu.VMEM((experts, rows, width), jnp.bfloat16),
        pltpu.VMEM((2, *w_gate.shape), jnp.bfloat16),
        pltpu.SemaphoreType.DMA((2, experts)),
        pltpu.SemaphoreType.DMA,
    ]
    flops = 4 * experts * rows * hidden * width + 2 * experts * rows * count * width
    return call(
        functools.partial(up_kernel, tok_count), experts, ins, args, outs, shapes, scratch, flops
    )


def slope_call(own, other, pick, put, prob, mine, w_down, g, u):
    experts, hidden, width = w_down.shape
    count, rows, columns = pick.shape[2], prob.shape[1], prob.shape[2]
    places = rows // 2
    args = (*own, *other, pick, put, prob, mine, w_down, g, u)
    shapes = [
        bf16(experts, rows, width),
        bf16(experts, rows, hidden),
        bf16(experts, rows, hidden),
        bf16(experts, hidden, rows),
        bf16(experts, hidden, rows),
        bf16(2, count, columns),
    ]
    ins = [whole(a) for a in args[:-3]] + [pl.BlockSpec(memory_space=pl.ANY), each(g), each(u)]
    outs = [pl.BlockSpec(memory_space=pl.ANY)]
    outs += [each(s) for s in shapes[1:5]] + [kept(shapes[5])]
    scratch = [
        pltpu.VMEM((2, count, width), jnp.bfloat16),
        pltpu.VMEM((experts, rows, width), jnp.bfloat16),
        pltpu.VMEM((2, experts, places, columns), jnp.bfloat16),
        pltpu.VMEM(w_down.shape, jnp.bfloat16),
        pltpu.SemaphoreType.DMA((experts,)),
        pltpu.SemaphoreType.DMA,
    ]
    flops = 2 * experts * rows * hidden * width + 2 * experts * rows * count * width
    return call(slope_kernel, experts, ins, args, outs, shapes, scratch, flops)


def back_call(put, lefts, rights, start, stop, extra=None):
    experts, hidden, _ = rights[0].shape
    rows = lefts[0].shape[1]
    count = put.shape[1]
    terms = len(lefts)
    steps = (stop - start) // CHUNK
    columns = stop - start + (0 if extra is None else extra.shape[2])
    args = (put, *lefts, *rights) + (() if extra is None else (extra,))
    shapes = [bf16(count, columns)] * 2
    ins = [whole(put)] + [whole(a) for a in lefts]
    ins += [pl.BlockSpec(memory_space=pl.ANY)] * terms
    ins += [] if extra is None else [whole(extra)]
    outs = [pl.BlockSpec((count, CHUNK), lambda i: (0, i))] * 2
    scratch = [
        pltpu.VMEM((2, put.shape[2], CHUNK), jnp.bfloat16),
        pltpu.VMEM((terms, steps, experts, hidden, CHUNK), jnp.bfloat16),
        pltpu.SemaphoreType.DMA((terms, steps)),
    ]
    flops = 2 * experts * rows * (stop - start) * (hidden * terms + count)
    kernel = functools.partial(back_kernel, terms, start, steps)
    grid = steps + (0 if extra is None else 1)
    return call(kernel, grid, ins, args, outs, shapes, scratch, flops)


def grad_call(x, *lefts):
    experts, rows, width = x.shape
    hidden = lefts[0].shape[1]
    shapes = [bf16(experts, hidden, width)] * len(lefts)
    ins = [each(x)] + [each(left) for left in lefts]
    flops = 2 * experts * rows * hidden * width * len(lefts)
    return call(grad_kernel, experts, ins, (x, *lefts), [each(s) for s in shapes], shapes, flops=flops)


def dense_body(
    tokens, cotangent, gate_prob, expert_ids, placement, gate_weight, up_weight, down_weight
):
    tok_count, width = tokens.shape
    local = gate_weight.shape[0]
    total_experts = placement.shape[0]
    devices = lax.axis_size("dp") * lax.axis_size("expert")
    places = devices // 2 * CAP
    count = devices // 2 * tok_count
    quarter, middle = count // 4, width // 2

    slots = slots_of(expert_ids, placement)
    used = slots[:, :, None] == jnp.arange(total_experts, dtype=jnp.int32)
    prob = jnp.sum(jnp.where(used, gate_prob[:, :, None], 0.0), axis=1)
    high = lax.reduce_precision(prob, 8, 7)
    extended = jnp.concatenate(
        [tokens, high.astype(jnp.bfloat16), (prob - high).astype(jnp.bfloat16)], axis=1
    )

    slot = lax.axis_index("expert") * local + jnp.arange(local * places, dtype=jnp.int32) // places
    spots = jnp.arange(2 * total_experts, dtype=jnp.int32)
    mine = (slot[:, None] == spots[None, :]).astype(jnp.bfloat16)
    both = (slot[:, None] == spots[None, :] % total_experts).astype(jnp.float32)
    maps = ((slot[None, :] == spots[:, None]).astype(jnp.bfloat16), mine, both)

    near, far = swap(extended, Z1), swap(extended, Z2)
    last = swap(far, Z1)
    cotangent, last = together(cotangent, last)
    own, other = [], []
    for rows in (extended, jnp.concatenate([near, far]), last):
        rows = jnp.concatenate([rows, swap(rows, X, Y)])
        rows = jnp.concatenate([rows, swap(rows, Y, X)])
        own.append(rows)
        other.append(swap(rows, CORE))

    grads = jnp.concatenate([cotangent] + [swap(cotangent, bit) for bit in (Z1, Z2, Z3)])
    grads = jnp.concatenate([grads, swap(grads, X, Y)])
    *rows, grads = together(*own, *other, grads)
    far_grads = swap(grads, Y, X)
    grads_other = swap(grads, CORE)

    x, put, pick, prob_rows, g, u, h, ht = up_call(
        rows[:3], rows[3:], maps, gate_weight, up_weight, tok_count
    )
    h, far_grads = together(h, far_grads)
    far_grads_other = swap(far_grads, CORE)
    mixed, mixed_other = back_call(put, [h], [down_weight], 0, width)
    mixed_other, far_grads_other = together(mixed_other, far_grads_other)
    mixed = [mixed, swap(mixed_other, CORE)]

    c, dg, du, dgt, dut, share = slope_call(
        (grads, far_grads),
        (grads_other, far_grads_other),
        pick,
        put,
        prob_rows,
        mine.reshape(local, places, -1),
        down_weight,
        g,
        u,
    )

    def leaving(parts, start, stop):
        return add(*(part[start:stop] for part in parts))

    def by_second(parts):
        return parts + [swap(leaving(parts, 2 * quarter, 4 * quarter), Y, X)]

    def by_first(parts):
        return parts + [swap(leaving(parts, quarter, 2 * quarter), X, Y)]

    def by_far(parts):
        return parts + [swap(leaving(parts, 2 * tok_count, 4 * tok_count), Z2)]

    def by_near(parts):
        return parts + [swap(leaving(parts, tok_count, 2 * tok_count), Z1)]

    weights = [gate_weight, up_weight]
    mixed[1], dg, du = together(mixed[1], dg, du)
    mixed = by_second(mixed)
    left, left_other = back_call(put, [dg, du], weights, 0, middle)
    left = [left, swap(left_other, CORE)]
    left[0], dg, du = together(left[0], dg, du)
    right, right_other = back_call(put, [dg, du], weights, middle, width, share)
    right = [right, swap(right_other, CORE)]

    right[0], left[1] = together(right[0], left[1])
    left = by_second(left)
    mixed[2], ht = together(mixed[2], ht)
    mixed = by_first(mixed)
    (down_weight_grad,) = grad_call(c, ht)

    right[1], left[2], mixed[3], down_weight_grad = together(
        right[1], left[2], mixed[3], down_weight_grad
    )
    right, left, mixed = by_second(right), by_first(left), by_far(mixed)
    right[0], dgt, dut = together(right[0], dgt, dut)
    gate_weight_grad, up_weight_grad = grad_call(x, dgt, dut)

    right[2], left[3], mixed[4], gate_weight_grad = together(
        right[2], left[3], mixed[4], gate_weight_grad
    )
    right, left, mixed = by_first(right), by_far(left), by_near(mixed)
    right, left = by_far(right), by_near(left)
    right = by_near(right)
    mixed, left, right = (leaving(parts, 0, tok_count) for parts in (mixed, left, right))
    token_grad = jnp.concatenate([left, right[:, : width - middle]], axis=1)
    share = right[:, width - middle : width - middle + total_experts].astype(jnp.float32)
    gate_grad = jnp.sum(jnp.where(used, share[:, None, :], 0.0), axis=2)
    return (mixed, token_grad, gate_grad, gate_weight_grad, up_weight_grad, down_weight_grad)


def routed_body(tokens, cotangent, gate_prob, expert_ids, placement, gate_weight, up_weight, down_weight):
    tok_count, model_width = tokens.shape
    top_count = expert_ids.shape[1]
    expert_devs = lax.axis_size("expert")
    local_experts = gate_weight.shape[0]
    total_experts = placement.shape[0]
    capacity = CAP
    flat_ids = expert_ids.reshape(-1)
    matches_id = flat_ids[:, None] == jnp.arange(total_experts, dtype=jnp.int32)[None, :]
    slot_ids = jnp.sum(jnp.where(matches_id, placement[None, :], 0), axis=1)
    pair_order = jnp.arange(flat_ids.shape[0], dtype=jnp.int32)
    earlier = (slot_ids[:, None] == slot_ids[None, :]) & (pair_order[None, :] < pair_order[:, None])
    position = slot_ids * capacity + jnp.sum(earlier.astype(jnp.int32), axis=1)
    matches = jnp.arange(total_experts * capacity, dtype=jnp.int32)[:, None] == position[None, :]
    matches = matches.reshape(total_experts * capacity, tok_count, top_count)
    dispatch = jnp.any(matches, axis=2).astype(jnp.bfloat16)
    weight_map = jnp.sum(jnp.where(matches, gate_prob[None, :, :], 0.0), axis=2)
    sent_rows = jnp.dot(dispatch, tokens, preferred_element_type=jnp.float32).astype(jnp.bfloat16)
    sent_grads = jnp.dot(
        weight_map, cotangent.astype(jnp.float32), precision=lax.Precision.HIGHEST
    ).astype(jnp.bfloat16)
    block_shape = (1, expert_devs, local_experts, capacity, model_width)
    sent_rows = sent_rows.reshape(block_shape)
    sent_grads = sent_grads.reshape(block_shape)
    got_rows, got_grads = (
        lax.all_to_all(sent_rows, "expert", split_axis=1, concat_axis=1, tiled=True),
        lax.all_to_all(sent_grads, "expert", split_axis=1, concat_axis=1, tiled=True),
    )
    routed, routed_grads = (
        lax.all_gather(got_rows, "dp", axis=0, tiled=True),
        lax.all_gather(got_grads, "dp", axis=0, tiled=True),
    )
    gate_pre = jnp.einsum(
        "asjcd,jfd->asjcf", routed, gate_weight, preferred_element_type=jnp.float32
    )
    up_pre = jnp.einsum("asjcd,jfd->asjcf", routed, up_weight, preferred_element_type=jnp.float32)
    silu_v, slope = gated(gate_pre)
    hidden = (silu_v * up_pre).astype(jnp.bfloat16)
    out_part = jnp.einsum(
        "asjcf,jfd->asjcd", hidden, down_weight, preferred_element_type=jnp.float32
    )
    d_hidden = jnp.einsum(
        "asjcd,jfd->asjcf", routed_grads, down_weight, preferred_element_type=jnp.float32
    )
    d_gate_pre = (d_hidden * up_pre * slope).astype(jnp.bfloat16)
    d_up_pre = (d_hidden * silu_v).astype(jnp.bfloat16)
    back_part = jnp.einsum(
        "asjcf,jfd->asjcd", d_gate_pre, gate_weight, preferred_element_type=jnp.float32
    )
    back_part = back_part + jnp.einsum(
        "asjcf,jfd->asjcd", d_up_pre, up_weight, preferred_element_type=jnp.float32
    )
    down_grad = jnp.einsum(
        "asjcf,asjcd->jfd", hidden, routed_grads, preferred_element_type=jnp.float32
    ).astype(jnp.bfloat16)
    gate_grad_w = jnp.einsum(
        "asjcf,asjcd->jfd", d_gate_pre, routed, preferred_element_type=jnp.float32
    ).astype(jnp.bfloat16)
    up_grad_w = jnp.einsum(
        "asjcf,asjcd->jfd", d_up_pre, routed, preferred_element_type=jnp.float32
    ).astype(jnp.bfloat16)
    summed = (
        lax.psum_scatter(
            out_part.astype(jnp.bfloat16), "dp", scatter_dimension=0, tiled=True
        ).astype(jnp.float32),
        lax.psum_scatter(
            back_part.astype(jnp.bfloat16), "dp", scatter_dimension=0, tiled=True
        ).astype(jnp.float32),
    )
    back_out, back_grad = (
        lax.all_to_all(
            summed[0].astype(jnp.bfloat16), "expert", split_axis=1, concat_axis=1, tiled=True
        ),
        lax.all_to_all(
            summed[1].astype(jnp.bfloat16), "expert", split_axis=1, concat_axis=1, tiled=True
        ),
    )
    out_flat = back_out.reshape(total_experts * capacity, model_width)
    grad_flat = back_grad.reshape(total_experts * capacity, model_width)
    chosen_out = out_flat[position].reshape(tok_count, top_count, model_width)
    chosen_grad = grad_flat[position].reshape(tok_count, top_count, model_width)
    mixed = jnp.einsum(
        "tk,tkd->td", gate_prob, chosen_out.astype(jnp.float32), precision=lax.Precision.HIGHEST
    ).astype(jnp.bfloat16)
    gate_grad = jnp.einsum("td,tkd->tk", cotangent, chosen_out, preferred_element_type=jnp.float32)
    token_grad = jnp.sum(chosen_grad.astype(jnp.float32), axis=1).astype(jnp.bfloat16)
    return (mixed, token_grad, gate_grad, gate_grad_w, up_grad_w, down_grad)


def body(*args):
    tokens, gate_weight = args[0], args[5]
    mesh_fits = (lax.axis_size("dp"), lax.axis_size("expert")) == (4, 8)
    if mesh_fits and tokens.shape[0] <= gate_weight.shape[0] * CAP:
        return dense_body(*args)
    return routed_body(*args)


def solution(mesh):
    return jax.shard_map(
        body,
        mesh=mesh,
        in_specs=(
            P(("dp", "expert"), None),
            P(("dp", "expert"), None),
            P(("dp", "expert"), None),
            P(("dp", "expert"), None),
            P(),
            P("expert", "dp", None),
            P("expert", "dp", None),
            P("expert", "dp", None),
        ),
        out_specs=(
            P(("dp", "expert"), None),
            P(("dp", "expert"), None),
            P(("dp", "expert"), None),
            P("expert", "dp", None),
            P("expert", "dp", None),
            P("expert", "dp", None),
        ),
        check_vma=False,
    )
```

```python
import functools

import jax
import jax.numpy as jnp
from jax import lax
from jax.experimental import pallas as pl
from jax.experimental.pallas import tpu as pltpu
from jax.sharding import PartitionSpec as P

CAP = 3
AXES = ("dp", "expert")
CORE, Z1, Z2, Z3, X, Y = 1, 2, 4, 6, 8, 16
GROUPS = ((0,), (1, 2), (3,))
CHUNK = 512
WIDE = 1024
MIB = 1 << 20

NT = (((1,), (1,)), ((), ()))
NN = (((1,), (0,)), ((), ()))


def gated(values):
    sigmoid_v = jax.nn.sigmoid(values)
    return (values * sigmoid_v, sigmoid_v * (1.0 + values * (1.0 - sigmoid_v)))


def swap(values, even, odd=None):
    odd = even if odd is None else odd
    count = lax.axis_size("dp") * lax.axis_size("expert")
    pairs = [(i, i ^ (odd if i & CORE else even)) for i in range(count)]
    return lax.ppermute(values, AXES, pairs)


def add(*parts):
    total = parts[0].astype(jnp.float32)
    for part in parts[1:]:
        total = total + part.astype(jnp.float32)
    return total.astype(jnp.bfloat16)


def together(*values):
    return lax.optimization_barrier(values)


def slots_of(expert_ids, placement):
    total = placement.shape[0]
    matches = expert_ids[:, :, None] == jnp.arange(total, dtype=jnp.int32)
    return jnp.sum(jnp.where(matches, placement, 0), axis=2)


def dot(a, b, dims=NN):
    return lax.dot_general(a, b, dims, preferred_element_type=jnp.float32)


def iota(shape, axis):
    return lax.broadcasted_iota(jnp.int32, shape, axis)


def dispatch(pick, rows_ref, half, x_ref):
    experts, both, width = x_ref.shape
    places = both // 2
    for at in range(0, width, WIDE):
        rows = dot(pick, rows_ref[half, :, at : at + WIDE]).astype(jnp.bfloat16)
        for e in range(experts):
            x_ref[e, half * places : (half + 1) * places, at : at + WIDE] = rows[
                e * places : (e + 1) * places
            ]


def join_groups(pieces, rows_ref, half, tok_count):
    for piece, group in zip(pieces, GROUPS):
        size = len(group) * tok_count
        for quarter in range(4):
            at = (quarter * 4 + group[0]) * tok_count
            rows_ref[half, at : at + size] = piece[quarter * size : (quarter + 1) * size]


def up_kernel(tok_count, own0, own1, own2, other0, other1, other2, mine_ref, mine_t_ref, both_ref,
              gate_ref, up_ref, x_out, put_ref, pick_ref, prob_ref, g_ref, u_ref, h_ref, ht_ref,
              rows_ref, x_ref, held_ref, held_sems, sem):
    e = pl.program_id(0)
    experts, both, width = x_ref.shape
    places = both // 2
    hidden = gate_ref.shape[1]
    count = rows_ref.shape[1]

    def copies(i):
        return (
            pltpu.make_async_copy(gate_ref.at[i], held_ref.at[i, :hidden], held_sems.at[0, i]),
            pltpu.make_async_copy(up_ref.at[i], held_ref.at[i, hidden:], held_sems.at[1, i]),
        )

    @pl.when(e == 0)
    def _():
        for i in range(experts):
            for copy in copies(i):
                copy.start()
        join_groups((own0, own1, own2), rows_ref, 0, tok_count)
        join_groups((other0, other1, other2), rows_ref, 1, tok_count)
        row, col = iota((count, count), 0), iota((count, count), 1)
        block = lax.div(row, tok_count)
        before = ((col < row) & (lax.div(col, tok_count) == block)).astype(jnp.bfloat16)
        columns = mine_ref.shape[0]
        first = (lax.div(iota((count, columns), 0), tok_count) * CAP).astype(jnp.float32)
        spot = lax.rem(iota((count, experts * places), 1), places).astype(jnp.float32)
        spot_t = lax.rem(iota((experts * places, count), 0), places).astype(jnp.float32)
        for half in range(2):
            prob = rows_ref[half, :, width:]
            taken = prob.astype(jnp.float32) > 0.0
            rank = dot(before, jnp.where(taken, 1.0, 0.0).astype(jnp.bfloat16))
            place = jnp.where(taken, rank + first, -1.0).astype(jnp.bfloat16)
            put = jnp.where(dot(place, mine_ref[...]) == spot, 1.0, 0.0)
            pick = dot(mine_t_ref[...], place, NT) == spot_t
            pick = jnp.where(pick, 1.0, 0.0).astype(jnp.bfloat16)
            put_ref[half] = put.astype(jnp.bfloat16)
            pick_ref[half] = pick
            weight = jnp.sum(put * dot(prob, both_ref[...]), axis=0, keepdims=True)
            for i in range(experts):
                prob_ref[i, :, half * places : (half + 1) * places] = weight[
                    :, i * places : (i + 1) * places
                ]
            dispatch(pick, rows_ref, half, x_ref)
        pltpu.make_async_copy(x_ref, x_out, sem).start()

    for copy in copies(e):
        copy.wait()
    product = dot(held_ref[e], x_ref[e], NT)
    g, u = product[:hidden], product[hidden:]
    g_ref[0] = g
    u_ref[0] = u
    silu_v, _ = gated(g)
    scaled = silu_v * u * prob_ref[e]
    ht_ref[0] = scaled.astype(jnp.bfloat16)
    h_ref[0] = scaled.T.astype(jnp.bfloat16)

    @pl.when(e == pl.num_programs(0) - 1)
    def _():
        pltpu.make_async_copy(x_ref, x_out, sem).wait()


def slope_kernel(own0, own1, other0, other1, pick_ref, put_ref, prob_ref, mine_ref, down_ref, g_ref, u_ref,
                 x_out, dg_ref, du_ref, dgt_ref, dut_ref, share_ref, rows_ref, x_ref, shares_ref, terms_ref,
                 held_ref, held_sems, sem):
    e = pl.program_id(0)
    experts = x_ref.shape[0]
    places = x_ref.shape[1] // 2

    def copy(i):
        return pltpu.make_async_copy(down_ref.at[i], held_ref.at[i], held_sems.at[i])

    @pl.when(e == 0)
    def _():
        for i in range(experts):
            copy(i).start()
        for half, pieces in enumerate(((own0, own1), (other0, other1))):
            size = own0.shape[0]
            rows_ref[half, :size] = pieces[0][...]
            rows_ref[half, size:] = pieces[1][...]
            dispatch(pick_ref[half], rows_ref, half, x_ref)
        pltpu.make_async_copy(x_ref, x_out, sem).start()

    copy(e).wait()
    plain = dot(held_ref[e], x_ref[e], NT)
    g, u = g_ref[0], u_ref[0]
    silu_v, slope = gated(g)
    shares_ref[pl.ds(e, 1), :] = jnp.sum(silu_v * u * plain, axis=0, keepdims=True)
    scaled = plain * prob_ref[e]
    dg = scaled * u * slope
    du = scaled * silu_v
    dgt_ref[0] = dg.astype(jnp.bfloat16)
    dut_ref[0] = du.astype(jnp.bfloat16)
    dg_ref[0] = dg.T.astype(jnp.bfloat16)
    du_ref[0] = du.T.astype(jnp.bfloat16)

    @pl.when(e == pl.num_programs(0) - 1)
    def _():
        shares = shares_ref[...].T
        for half in range(2):
            for i in range(experts):
                share = shares[half * places : (half + 1) * places, i : i + 1]
                share = (share * mine_ref[i].astype(jnp.float32)).astype(jnp.bfloat16)
                terms_ref[i * places : (i + 1) * places] = share
            share_ref[half] = dot(put_ref[half], terms_ref[...]).astype(jnp.bfloat16)
        pltpu.make_async_copy(x_ref, x_out, sem).wait()


def back_kernel(terms, start, steps, put_ref, *refs):
    lefts, rights = refs[:terms], refs[terms : 2 * terms]
    extra_ref = refs[2 * terms] if len(refs) > 2 * terms + 5 else None
    own_ref, other_ref, rows_ref, held_ref, sems = refs[-5:]
    experts, places = rights[0].shape[0], put_ref.shape[2] // rights[0].shape[0]
    step = pl.program_id(0)

    def copy(i, at):
        columns = pl.ds(pl.multiple_of(start + at * CHUNK, CHUNK), CHUNK)
        return pltpu.make_async_copy(rights[i].at[:, :, columns], held_ref.at[i, at], sems.at[i, at])

    @pl.when(step == 0)
    def _():
        for at in range(steps):
            for i in range(terms):
                copy(i, at).start()

    @pl.when(step < steps)
    def _():
        for i in range(terms):
            copy(i, step).wait()
        for e in range(experts):
            rows = dot(lefts[0][e], held_ref[0, step, e])
            for i in range(1, terms):
                rows = rows + dot(lefts[i][e], held_ref[i, step, e])
            rows = rows.astype(jnp.bfloat16)
            for half in range(2):
                rows_ref[half, e * places : (e + 1) * places] = rows[half * places : (half + 1) * places]
        own_ref[...] = dot(put_ref[0], rows_ref[0]).astype(jnp.bfloat16)
        other_ref[...] = dot(put_ref[1], rows_ref[1]).astype(jnp.bfloat16)

    if extra_ref is not None:

        @pl.when(step == steps)
        def _():
            columns = extra_ref.shape[2]
            own_ref[:, :columns] = extra_ref[0]
            other_ref[:, :columns] = extra_ref[1]


def grad_kernel(x_ref, left, out):
    for at in range(0, x_ref.shape[2], WIDE):
        out[0, :, at : at + WIDE] = dot(left[0], x_ref[0, :, at : at + WIDE]).astype(jnp.bfloat16)


def whole(a):
    shape = a.shape
    return pl.BlockSpec(shape, lambda i: (0,) * len(shape), pipeline_mode=pl.Buffered(1))


def kept(a):
    shape = a.shape
    return pl.BlockSpec(shape, lambda i: (0,) * len(shape))


def each(a):
    shape = a.shape
    return pl.BlockSpec((1, *shape[1:]), lambda i: (i,) + (0,) * (len(shape) - 1))


def bf16(*shape):
    return jax.ShapeDtypeStruct(shape, jnp.bfloat16)


def f32(*shape):
    return jax.ShapeDtypeStruct(shape, jnp.float32)


def call(kernel, grid, ins, args, outs, shapes, scratch=(), flops=0):
    moved = sum(a.size * a.dtype.itemsize for a in (*args, *shapes))
    return pl.pallas_call(
        kernel,
        grid=(grid,),
        in_specs=ins,
        out_specs=outs,
        out_shape=shapes,
        scratch_shapes=scratch,
        compiler_params=pltpu.CompilerParams(vmem_limit_bytes=56 * MIB),
        cost_estimate=pl.CostEstimate(flops=flops, bytes_accessed=moved, transcendentals=0),
    )(*args)


def up_call(own, other, maps, w_gate, w_up, tok_count):
    experts, hidden, width = w_gate.shape
    held = own[0].shape[1]
    count = sum(piece.shape[0] for piece in own)
    places = count // tok_count * CAP
    rows = 2 * places
    args = (*own, *other, *maps, w_gate, w_up)
    shapes = [
        bf16(experts, rows, width),
        bf16(2, count, experts * places),
        bf16(2, experts * places, count),
        f32(experts, 1, rows),
        f32(experts, hidden, rows),
        f32(experts, hidden, rows),
        bf16(experts, rows, hidden),
        bf16(experts, hidden, rows),
    ]
    ins = [whole(a) for a in args[:-2]] + [pl.BlockSpec(memory_space=pl.ANY)] * 2
    outs = [pl.BlockSpec(memory_space=pl.ANY)]
    outs += [kept(s) for s in shapes[1:4]] + [each(s) for s in shapes[4:]]
    scratch = [
        pltpu.VMEM((2, count, held), jnp.bfloat16),
        pltpu.VMEM((experts, rows, width), jnp.bfloat16),
        pltpu.VMEM((experts, 2 * hidden, width), jnp.bfloat16),
        pltpu.SemaphoreType.DMA((2, experts)),
        pltpu.SemaphoreType.DMA,
    ]
    flops = 4 * experts * rows * hidden * width + 2 * experts * rows * count * width
    return call(
        functools.partial(up_kernel, tok_count), experts, ins, args, outs, shapes, scratch, flops
    )


def slope_call(own, other, pick, put, prob, mine, w_down, g, u):
    experts, hidden, width = w_down.shape
    count, rows, columns = pick.shape[2], prob.shape[2], mine.shape[2]
    places = rows // 2
    args = (*own, *other, pick, put, prob, mine, w_down, g, u)
    shapes = [
        bf16(experts, rows, width),
        bf16(experts, rows, hidden),
        bf16(experts, rows, hidden),
        bf16(experts, hidden, rows),
        bf16(experts, hidden, rows),
        bf16(2, count, columns),
    ]
    ins = [whole(a) for a in args[:-3]] + [pl.BlockSpec(memory_space=pl.ANY), each(g), each(u)]
    outs = [pl.BlockSpec(memory_space=pl.ANY)]
    outs += [each(s) for s in shapes[1:5]] + [kept(shapes[5])]
    scratch = [
        pltpu.VMEM((2, count, width), jnp.bfloat16),
        pltpu.VMEM((experts, rows, width), jnp.bfloat16),
        pltpu.VMEM((experts, rows), jnp.float32),
        pltpu.VMEM((experts * places, columns), jnp.bfloat16),
        pltpu.VMEM(w_down.shape, jnp.bfloat16),
        pltpu.SemaphoreType.DMA((experts,)),
        pltpu.SemaphoreType.DMA,
    ]
    flops = 2 * experts * rows * hidden * width + 2 * experts * rows * count * width
    return call(slope_kernel, experts, ins, args, outs, shapes, scratch, flops)


def back_call(put, lefts, rights, start, stop, extra=None):
    experts, hidden, _ = rights[0].shape
    rows = lefts[0].shape[1]
    count = put.shape[1]
    terms = len(lefts)
    steps = (stop - start) // CHUNK
    columns = stop - start + (0 if extra is None else extra.shape[2])
    args = (put, *lefts, *rights) + (() if extra is None else (extra,))
    shapes = [bf16(count, columns)] * 2
    ins = [whole(put)] + [whole(a) for a in lefts]
    ins += [pl.BlockSpec(memory_space=pl.ANY)] * terms
    ins += [] if extra is None else [whole(extra)]
    outs = [pl.BlockSpec((count, CHUNK), lambda i: (0, i))] * 2
    scratch = [
        pltpu.VMEM((2, put.shape[2], CHUNK), jnp.bfloat16),
        pltpu.VMEM((terms, steps, experts, hidden, CHUNK), jnp.bfloat16),
        pltpu.SemaphoreType.DMA((terms, steps)),
    ]
    flops = 2 * experts * rows * (stop - start) * (hidden * terms + count)
    kernel = functools.partial(back_kernel, terms, start, steps)
    grid = steps + (0 if extra is None else 1)
    return call(kernel, grid, ins, args, outs, shapes, scratch, flops)


def grad_call(x, left):
    experts, rows, width = x.shape
    hidden = left.shape[1]
    shape = bf16(experts, hidden, width)
    flops = 2 * experts * rows * hidden * width
    ins, outs = [each(x), each(left)], [each(shape)]
    return call(grad_kernel, experts, ins, (x, left), outs, [shape], flops=flops)[0]


def dense_body(
    tokens, cotangent, gate_prob, expert_ids, placement, gate_weight, up_weight, down_weight
):
    tok_count, width = tokens.shape
    local = gate_weight.shape[0]
    total_experts = placement.shape[0]
    devices = lax.axis_size("dp") * lax.axis_size("expert")
    places = devices // 2 * CAP
    count = devices // 2 * tok_count
    quarter, middle = count // 4, width // 2

    slots = slots_of(expert_ids, placement)
    used = slots[:, :, None] == jnp.arange(total_experts, dtype=jnp.int32)
    prob = jnp.sum(jnp.where(used, gate_prob[:, :, None], 0.0), axis=1)
    high = lax.reduce_precision(prob, 8, 7)
    parts = jnp.concatenate([high.astype(jnp.bfloat16), (prob - high).astype(jnp.bfloat16)], axis=1)

    slot = lax.axis_index("expert") * local + jnp.arange(local * places, dtype=jnp.int32) // places
    spots = jnp.arange(2 * total_experts, dtype=jnp.int32)
    mine = (slot[:, None] == spots[None, :]).astype(jnp.bfloat16)
    both = (slot[None, :] == spots[:, None] % total_experts).astype(jnp.bfloat16)
    maps = ((slot[None, :] == spots[:, None]).astype(jnp.bfloat16), mine, both)

    def rows_of(*blocks):
        return jnp.concatenate(blocks)

    def wide(values, extra):
        return jnp.concatenate([values, extra], axis=1)

    near, far = swap(tokens, Z1), swap(tokens, Z2)
    near_parts, far_parts = swap(parts, Z1), swap(parts, Z2)
    zero = wide(tokens, parts)
    first0 = swap(zero, X, Y)
    near, far, near_parts, far_parts = together(near, far, near_parts, far_parts)

    last, last_parts = swap(far, Z1), swap(far_parts, Z1)
    middle_rows = wide(rows_of(near, far), rows_of(near_parts, far_parts))
    first1 = swap(middle_rows, X, Y)
    zero = rows_of(zero, first0)
    second0 = swap(zero, Y, X)
    cotangent, last_parts = together(cotangent, last_parts)
    grads = [swap(cotangent, bit) for bit in (Z1, Z2, Z3)]
    last, last_parts, first1, second0 = together(last, last_parts, first1, second0)

    last = wide(last, last_parts)
    first2 = swap(last, X, Y)
    middle_rows = rows_of(middle_rows, first1)
    second1 = swap(middle_rows, Y, X)
    zero = rows_of(zero, second0)
    zero_other = swap(zero, CORE)
    first2, second1, cotangent = together(first2, second1, cotangent)

    last = rows_of(last, first2)
    second2 = swap(last, Y, X)
    middle_rows = rows_of(middle_rows, second1)
    middle_other = swap(middle_rows, CORE)
    grads = rows_of(cotangent, *grads)
    grads = rows_of(grads, swap(grads, X, Y))
    last = rows_of(last, second2)
    last_other = swap(last, CORE)
    *rows, grads = together(
        zero, middle_rows, last, zero_other, middle_other, last_other, grads
    )
    far_grads = swap(grads, Y, X)
    grads_other = swap(grads, CORE)

    x, put, pick, prob_rows, g, u, h, ht = up_call(
        rows[:3], rows[3:], maps, gate_weight, up_weight, tok_count
    )
    h, far_grads, grads_other = together(h, far_grads, grads_other)
    far_grads_other = swap(far_grads, CORE)
    mixed, mixed_other = back_call(put, [h], [down_weight], 0, width)
    mixed_other, far_grads_other = together(mixed_other, far_grads_other)
    mixed = [mixed, swap(mixed_other, CORE)]

    c, dg, du, dgt, dut, share = slope_call(
        (grads, far_grads),
        (grads_other, far_grads_other),
        pick,
        put,
        prob_rows,
        mine.reshape(local, places, -1),
        down_weight,
        g,
        u,
    )

    def leaving(parts, start, stop):
        return add(*(part[start:stop] for part in parts))

    def by_second(parts):
        return parts + [swap(leaving(parts, 2 * quarter, 4 * quarter), Y, X)]

    def by_first(parts):
        return parts + [swap(leaving(parts, quarter, 2 * quarter), X, Y)]

    def by_far(parts):
        return parts + [swap(leaving(parts, 2 * tok_count, 4 * tok_count), Z2)]

    def by_near(parts):
        return parts + [swap(leaving(parts, tok_count, 2 * tok_count), Z1)]

    weights = [gate_weight, up_weight]
    mixed[1], dg, du = together(mixed[1], dg, du)
    mixed = by_second(mixed)
    left, left_other = back_call(put, [dg, du], weights, 0, middle)
    left = [left, swap(left_other, CORE)]
    left[0], dg, du = together(left[0], dg, du)
    right, right_other = back_call(put, [dg, du], weights, middle, width, share)
    right = [right, swap(right_other, CORE)]

    right[0], left[1] = together(right[0], left[1])
    left = by_second(left)
    mixed[2], ht = together(mixed[2], ht)
    mixed = by_first(mixed)
    down_weight_grad = grad_call(c, ht)

    right[1], left[2], mixed[3], down_weight_grad = together(
        right[1], left[2], mixed[3], down_weight_grad
    )
    right, left, mixed = by_second(right), by_first(left), by_far(mixed)
    right[0], dgt = together(right[0], dgt)
    gate_weight_grad = grad_call(x, dgt)

    right[2], left[3], mixed[4], gate_weight_grad = together(
        right[2], left[3], mixed[4], gate_weight_grad
    )
    right, left, mixed = by_first(right), by_far(left), by_near(mixed)
    right[0], dut = together(right[0], dut)
    up_weight_grad = grad_call(x, dut)

    right[3], left[4], mixed[5], up_weight_grad = together(
        right[3], left[4], mixed[5], up_weight_grad
    )
    right, left = by_far(right), by_near(left)
    right = by_near(right)
    mixed, left, right = (leaving(parts, 0, tok_count) for parts in (mixed, left, right))
    token_grad = jnp.concatenate([left, right[:, : width - middle]], axis=1)
    share = right[:, width - middle : width - middle + total_experts].astype(jnp.float32)
    gate_grad = jnp.sum(jnp.where(used, share[:, None, :], 0.0), axis=2)
    return (mixed, token_grad, gate_grad, gate_weight_grad, up_weight_grad, down_weight_grad)


def routed_body(tokens, cotangent, gate_prob, expert_ids, placement, gate_weight, up_weight, down_weight):
    tok_count, model_width = tokens.shape
    top_count = expert_ids.shape[1]
    expert_devs = lax.axis_size("expert")
    local_experts = gate_weight.shape[0]
    total_experts = placement.shape[0]
    capacity = CAP
    flat_ids = expert_ids.reshape(-1)
    matches_id = flat_ids[:, None] == jnp.arange(total_experts, dtype=jnp.int32)[None, :]
    slot_ids = jnp.sum(jnp.where(matches_id, placement[None, :], 0), axis=1)
    pair_order = jnp.arange(flat_ids.shape[0], dtype=jnp.int32)
    earlier = (slot_ids[:, None] == slot_ids[None, :]) & (pair_order[None, :] < pair_order[:, None])
    position = slot_ids * capacity + jnp.sum(earlier.astype(jnp.int32), axis=1)
    matches = jnp.arange(total_experts * capacity, dtype=jnp.int32)[:, None] == position[None, :]
    matches = matches.reshape(total_experts * capacity, tok_count, top_count)
    dispatch = jnp.any(matches, axis=2).astype(jnp.bfloat16)
    weight_map = jnp.sum(jnp.where(matches, gate_prob[None, :, :], 0.0), axis=2)
    sent_rows = jnp.dot(dispatch, tokens, preferred_element_type=jnp.float32).astype(jnp.bfloat16)
    sent_grads = jnp.dot(
        weight_map, cotangent.astype(jnp.float32), precision=lax.Precision.HIGHEST
    ).astype(jnp.bfloat16)
    block_shape = (1, expert_devs, local_experts, capacity, model_width)
    sent_rows = sent_rows.reshape(block_shape)
    sent_grads = sent_grads.reshape(block_shape)
    got_rows, got_grads = (
        lax.all_to_all(sent_rows, "expert", split_axis=1, concat_axis=1, tiled=True),
        lax.all_to_all(sent_grads, "expert", split_axis=1, concat_axis=1, tiled=True),
    )
    routed, routed_grads = (
        lax.all_gather(got_rows, "dp", axis=0, tiled=True),
        lax.all_gather(got_grads, "dp", axis=0, tiled=True),
    )
    gate_pre = jnp.einsum(
        "asjcd,jfd->asjcf", routed, gate_weight, preferred_element_type=jnp.float32
    )
    up_pre = jnp.einsum("asjcd,jfd->asjcf", routed, up_weight, preferred_element_type=jnp.float32)
    silu_v, slope = gated(gate_pre)
    hidden = (silu_v * up_pre).astype(jnp.bfloat16)
    out_part = jnp.einsum(
        "asjcf,jfd->asjcd", hidden, down_weight, preferred_element_type=jnp.float32
    )
    d_hidden = jnp.einsum(
        "asjcd,jfd->asjcf", routed_grads, down_weight, preferred_element_type=jnp.float32
    )
    d_gate_pre = (d_hidden * up_pre * slope).astype(jnp.bfloat16)
    d_up_pre = (d_hidden * silu_v).astype(jnp.bfloat16)
    back_part = jnp.einsum(
        "asjcf,jfd->asjcd", d_gate_pre, gate_weight, preferred_element_type=jnp.float32
    )
    back_part = back_part + jnp.einsum(
        "asjcf,jfd->asjcd", d_up_pre, up_weight, preferred_element_type=jnp.float32
    )
    down_grad = jnp.einsum(
        "asjcf,asjcd->jfd", hidden, routed_grads, preferred_element_type=jnp.float32
    ).astype(jnp.bfloat16)
    gate_grad_w = jnp.einsum(
        "asjcf,asjcd->jfd", d_gate_pre, routed, preferred_element_type=jnp.float32
    ).astype(jnp.bfloat16)
    up_grad_w = jnp.einsum(
        "asjcf,asjcd->jfd", d_up_pre, routed, preferred_element_type=jnp.float32
    ).astype(jnp.bfloat16)
    summed = (
        lax.psum_scatter(
            out_part.astype(jnp.bfloat16), "dp", scatter_dimension=0, tiled=True
        ).astype(jnp.float32),
        lax.psum_scatter(
            back_part.astype(jnp.bfloat16), "dp", scatter_dimension=0, tiled=True
        ).astype(jnp.float32),
    )
    back_out, back_grad = (
        lax.all_to_all(
            summed[0].astype(jnp.bfloat16), "expert", split_axis=1, concat_axis=1, tiled=True
        ),
        lax.all_to_all(
            summed[1].astype(jnp.bfloat16), "expert", split_axis=1, concat_axis=1, tiled=True
        ),
    )
    out_flat = back_out.reshape(total_experts * capacity, model_width)
    grad_flat = back_grad.reshape(total_experts * capacity, model_width)
    chosen_out = out_flat[position].reshape(tok_count, top_count, model_width)
    chosen_grad = grad_flat[position].reshape(tok_count, top_count, model_width)
    mixed = jnp.einsum(
        "tk,tkd->td", gate_prob, chosen_out.astype(jnp.float32), precision=lax.Precision.HIGHEST
    ).astype(jnp.bfloat16)
    gate_grad = jnp.einsum("td,tkd->tk", cotangent, chosen_out, preferred_element_type=jnp.float32)
    token_grad = jnp.sum(chosen_grad.astype(jnp.float32), axis=1).astype(jnp.bfloat16)
    return (mixed, token_grad, gate_grad, gate_grad_w, up_grad_w, down_grad)


def body(*args):
    tokens, gate_weight = args[0], args[5]
    mesh_fits = (lax.axis_size("dp"), lax.axis_size("expert")) == (4, 8)
    if mesh_fits and tokens.shape[0] <= gate_weight.shape[0] * CAP:
        return dense_body(*args)
    return routed_body(*args)


def solution(mesh):
    return jax.shard_map(
        body,
        mesh=mesh,
        in_specs=(
            P(("dp", "expert"), None),
            P(("dp", "expert"), None),
            P(("dp", "expert"), None),
            P(("dp", "expert"), None),
            P(),
            P("expert", "dp", None),
            P("expert", "dp", None),
            P("expert", "dp", None),
        ),
        out_specs=(
            P(("dp", "expert"), None),
            P(("dp", "expert"), None),
            P(("dp", "expert"), None),
            P("expert", "dp", None),
            P("expert", "dp", None),
            P("expert", "dp", None),
        ),
        check_vma=False,
    )
```

```python
import functools

import jax
import jax.numpy as jnp
from jax import lax
from jax.experimental import pallas as pl
from jax.experimental.pallas import tpu as pltpu
from jax.sharding import PartitionSpec as P

CAP = 3
AXES = ("dp", "expert")
CORE, Z1, Z2, Z3, X, Y = 1, 2, 4, 6, 8, 16
GROUPS = ((0,), (1, 2), (3,))
CHUNK = 512
WIDE = 1024
PAIR = 2
MIB = 1 << 20

NT = (((1,), (1,)), ((), ()))
NN = (((1,), (0,)), ((), ()))


def gated(values):
    sigmoid_v = jax.nn.sigmoid(values)
    return (values * sigmoid_v, sigmoid_v * (1.0 + values * (1.0 - sigmoid_v)))


def swap(values, even, odd=None):
    odd = even if odd is None else odd
    count = lax.axis_size("dp") * lax.axis_size("expert")
    pairs = [(i, i ^ (odd if i & CORE else even)) for i in range(count)]
    return lax.ppermute(values, AXES, pairs)


def add(*parts):
    total = parts[0].astype(jnp.float32)
    for part in parts[1:]:
        total = total + part.astype(jnp.float32)
    return total.astype(jnp.bfloat16)


def together(*values):
    return lax.optimization_barrier(values)


def slots_of(expert_ids, placement):
    total = placement.shape[0]
    matches = expert_ids[:, :, None] == jnp.arange(total, dtype=jnp.int32)
    return jnp.sum(jnp.where(matches, placement, 0), axis=2)


def dot(a, b, dims=NN):
    return lax.dot_general(a, b, dims, preferred_element_type=jnp.float32)


def iota(shape, axis):
    return lax.broadcasted_iota(jnp.int32, shape, axis)


def dispatch(pick, rows_ref, half, x_ref):
    experts, both, width = x_ref.shape
    places = both // 2
    for at in range(0, width, WIDE):
        rows = dot(pick, rows_ref[half, :, at : at + WIDE]).astype(jnp.bfloat16)
        for e in range(experts):
            x_ref[e, half * places : (half + 1) * places, at : at + WIDE] = rows[
                e * places : (e + 1) * places
            ]


def join_groups(pieces, rows_ref, half, tok_count):
    for piece, group in zip(pieces, GROUPS):
        size = len(group) * tok_count
        for quarter in range(4):
            at = (quarter * 4 + group[0]) * tok_count
            rows_ref[half, at : at + size] = piece[quarter * size : (quarter + 1) * size]


def up_kernel(tok_count, own0, own1, own2, other0, other1, other2, mine_ref, mine_t_ref, both_ref,
              gate_ref, up_ref, x_out, put_ref, pick_ref, prob_ref, g_ref, u_ref, h_ref, ht_ref,
              rows_ref, x_ref, held_ref, held_sems, sem):
    e = pl.program_id(0)
    experts, both, width = x_ref.shape
    places = both // 2
    hidden = gate_ref.shape[1]
    count = rows_ref.shape[1]

    def copies(i):
        return (
            pltpu.make_async_copy(gate_ref.at[i], held_ref.at[i, :hidden], held_sems.at[0, i]),
            pltpu.make_async_copy(up_ref.at[i], held_ref.at[i, hidden:], held_sems.at[1, i]),
        )

    @pl.when(e == 0)
    def _():
        for i in range(experts):
            for copy in copies(i):
                copy.start()
        join_groups((own0, own1, own2), rows_ref, 0, tok_count)
        join_groups((other0, other1, other2), rows_ref, 1, tok_count)
        row, col = iota((count, count), 0), iota((count, count), 1)
        block = lax.div(row, tok_count)
        before = ((col < row) & (lax.div(col, tok_count) == block)).astype(jnp.bfloat16)
        columns = mine_ref.shape[0]
        first = (lax.div(iota((count, columns), 0), tok_count) * CAP).astype(jnp.float32)
        spot = lax.rem(iota((count, experts * places), 1), places).astype(jnp.float32)
        spot_t = lax.rem(iota((experts * places, count), 0), places).astype(jnp.float32)
        for half in range(2):
            prob = rows_ref[half, :, width:]
            taken = prob.astype(jnp.float32) > 0.0
            rank = dot(before, jnp.where(taken, 1.0, 0.0).astype(jnp.bfloat16))
            place = jnp.where(taken, rank + first, -1.0).astype(jnp.bfloat16)
            put = jnp.where(dot(place, mine_ref[...]) == spot, 1.0, 0.0)
            pick = dot(mine_t_ref[...], place, NT) == spot_t
            pick = jnp.where(pick, 1.0, 0.0).astype(jnp.bfloat16)
            put_ref[half] = put.astype(jnp.bfloat16)
            pick_ref[half] = pick
            weight = jnp.sum(put * dot(prob, both_ref[...]), axis=0, keepdims=True)
            for i in range(experts):
                prob_ref[i, :, half * places : (half + 1) * places] = weight[
                    :, i * places : (i + 1) * places
                ]
            dispatch(pick, rows_ref, half, x_ref)
        pltpu.make_async_copy(x_ref, x_out, sem).start()

    pair = pl.ds(PAIR * e, PAIR)
    for i in range(PAIR):
        for copy in copies(PAIR * e + i):
            copy.wait()
    product = dot(
        held_ref[pair].reshape(PAIR * 2 * hidden, width), x_ref[pair].reshape(PAIR * both, width), NT
    )
    for i in range(PAIR):
        own = product[2 * hidden * i : 2 * hidden * (i + 1), both * i : both * (i + 1)]
        g, u = own[:hidden], own[hidden:]
        g_ref[i] = g
        u_ref[i] = u
        silu_v, _ = gated(g)
        scaled = silu_v * u * prob_ref[PAIR * e + i]
        ht_ref[i] = scaled.astype(jnp.bfloat16)
        h_ref[i] = scaled.T.astype(jnp.bfloat16)

    @pl.when(e == pl.num_programs(0) - 1)
    def _():
        pltpu.make_async_copy(x_ref, x_out, sem).wait()


def place_kernel(own0, own1, other0, other1, pick_ref, x_ref):
    experts, both = x_ref.shape[:2]
    places = both // 2
    for half, pieces in enumerate(((own0, own1), (other0, other1))):
        rows = jnp.concatenate([pieces[0][...], pieces[1][...]], axis=0)
        rows = dot(pick_ref[half], rows).astype(jnp.bfloat16)
        for e in range(experts):
            x_ref[e, half * places : (half + 1) * places] = rows[e * places : (e + 1) * places]


def slope_kernel(x_ref, put_ref, prob_ref, mine_ref, down_ref, g_ref, u_ref,
                 dg_ref, du_ref, dt_ref, share_ref, shares_ref, terms_ref):
    e = pl.program_id(0)
    experts, both = shares_ref.shape
    places = both // 2
    _, hidden, width = down_ref.shape
    product = dot(
        down_ref[...].reshape(PAIR * hidden, width), x_ref[...].reshape(PAIR * both, width), NT
    )
    for i in range(PAIR):
        plain = product[hidden * i : hidden * (i + 1), both * i : both * (i + 1)]
        g, u = g_ref[i], u_ref[i]
        silu_v, slope = gated(g)
        shares_ref[pl.ds(PAIR * e + i, 1), :] = jnp.sum(silu_v * u * plain, axis=0, keepdims=True)
        scaled = plain * prob_ref[i]
        dg = scaled * u * slope
        du = scaled * silu_v
        dt_ref[i, :hidden] = dg.astype(jnp.bfloat16)
        dt_ref[i, hidden:] = du.astype(jnp.bfloat16)
        dg_ref[i] = dg.T.astype(jnp.bfloat16)
        du_ref[i] = du.T.astype(jnp.bfloat16)

    @pl.when(e == pl.num_programs(0) - 1)
    def _():
        shares = shares_ref[...].T
        for half in range(2):
            for i in range(experts):
                share = shares[half * places : (half + 1) * places, i : i + 1]
                share = (share * mine_ref[i].astype(jnp.float32)).astype(jnp.bfloat16)
                terms_ref[i * places : (i + 1) * places] = share
            share_ref[half] = dot(put_ref[half], terms_ref[...]).astype(jnp.bfloat16)


def back_kernel(terms, start, steps, put_ref, *refs):
    lefts, rights = refs[:terms], refs[terms : 2 * terms]
    extra_ref = refs[2 * terms] if len(refs) > 2 * terms + 5 else None
    own_ref, other_ref, rows_ref, held_ref, sems = refs[-5:]
    experts, places = rights[0].shape[0], put_ref.shape[2] // rights[0].shape[0]
    step = pl.program_id(0)

    def copy(i, at):
        columns = pl.ds(pl.multiple_of(start + at * CHUNK, CHUNK), CHUNK)
        return pltpu.make_async_copy(rights[i].at[:, :, columns], held_ref.at[i, at], sems.at[i, at])

    @pl.when(step == 0)
    def _():
        for at in range(steps):
            for i in range(terms):
                copy(i, at).start()

    @pl.when(step < steps)
    def _():
        for i in range(terms):
            copy(i, step).wait()
        for e in range(experts):
            rows = dot(lefts[0][e], held_ref[0, step, e])
            for i in range(1, terms):
                rows = rows + dot(lefts[i][e], held_ref[i, step, e])
            rows = rows.astype(jnp.bfloat16)
            for half in range(2):
                rows_ref[half, e * places : (e + 1) * places] = rows[half * places : (half + 1) * places]
        own_ref[...] = dot(put_ref[0], rows_ref[0]).astype(jnp.bfloat16)
        other_ref[...] = dot(put_ref[1], rows_ref[1]).astype(jnp.bfloat16)

    if extra_ref is not None:

        @pl.when(step == steps)
        def _():
            columns = extra_ref.shape[2]
            own_ref[:, :columns] = extra_ref[0]
            other_ref[:, :columns] = extra_ref[1]


def grad_kernel(x_ref, left, *outs):
    hidden = outs[0].shape[1]
    for at in range(0, x_ref.shape[2], WIDE):
        product = dot(left[0], x_ref[0, :, at : at + WIDE]).astype(jnp.bfloat16)
        for i, out in enumerate(outs):
            out[0, :, at : at + WIDE] = product[hidden * i : hidden * (i + 1)]


def whole(a):
    shape = a.shape
    return pl.BlockSpec(shape, lambda i: (0,) * len(shape), pipeline_mode=pl.Buffered(1))


def kept(a):
    shape = a.shape
    return pl.BlockSpec(shape, lambda i: (0,) * len(shape))


def each(a, size=1):
    shape = a.shape
    return pl.BlockSpec((size, *shape[1:]), lambda i: (i,) + (0,) * (len(shape) - 1))


def bf16(*shape):
    return jax.ShapeDtypeStruct(shape, jnp.bfloat16)


def f32(*shape):
    return jax.ShapeDtypeStruct(shape, jnp.float32)


def call(kernel, grid, ins, args, outs, shapes, scratch=(), flops=0):
    moved = sum(a.size * a.dtype.itemsize for a in (*args, *shapes))
    return pl.pallas_call(
        kernel,
        grid=(grid,),
        in_specs=ins,
        out_specs=outs,
        out_shape=shapes,
        scratch_shapes=scratch,
        compiler_params=pltpu.CompilerParams(vmem_limit_bytes=56 * MIB),
        cost_estimate=pl.CostEstimate(flops=flops, bytes_accessed=moved, transcendentals=0),
    )(*args)


def up_call(own, other, maps, w_gate, w_up, tok_count):
    experts, hidden, width = w_gate.shape
    held = own[0].shape[1]
    count = sum(piece.shape[0] for piece in own)
    places = count // tok_count * CAP
    rows = 2 * places
    args = (*own, *other, *maps, w_gate, w_up)
    shapes = [
        bf16(experts, rows, width),
        bf16(2, count, experts * places),
        bf16(2, experts * places, count),
        f32(experts, 1, rows),
        f32(experts, hidden, rows),
        f32(experts, hidden, rows),
        bf16(experts, rows, hidden),
        bf16(experts, hidden, rows),
    ]
    ins = [whole(a) for a in args[:-2]] + [pl.BlockSpec(memory_space=pl.ANY)] * 2
    outs = [pl.BlockSpec(memory_space=pl.ANY)]
    outs += [kept(s) for s in shapes[1:4]] + [each(s, PAIR) for s in shapes[4:]]
    scratch = [
        pltpu.VMEM((2, count, held), jnp.bfloat16),
        pltpu.VMEM((experts, rows, width), jnp.bfloat16),
        pltpu.VMEM((experts, 2 * hidden, width), jnp.bfloat16),
        pltpu.SemaphoreType.DMA((2, experts)),
        pltpu.SemaphoreType.DMA,
    ]
    flops = 4 * experts * rows * hidden * width + 2 * experts * rows * count * width
    return call(
        functools.partial(up_kernel, tok_count), experts // PAIR, ins, args, outs, shapes, scratch, flops
    )


def place_call(pieces, pick, experts):
    _, rows, count = pick.shape
    size, width = pieces[0].shape
    shape = bf16(experts, 2 * rows // experts, width)
    ins = [pl.BlockSpec((size, WIDE), lambda i: (0, i))] * len(pieces) + [whole(pick)]
    outs = [pl.BlockSpec((*shape.shape[:2], WIDE), lambda i: (0, 0, i))]
    flops = 4 * rows * count * width
    return call(place_kernel, width // WIDE, ins, (*pieces, pick), outs, [shape], flops=flops)[0]


def slope_call(x, put, prob, mine, w_down, g, u):
    experts, hidden, width = w_down.shape
    rows, count, columns = x.shape[1], put.shape[1], mine.shape[2]
    args = (x, put, prob, mine, w_down, g, u)
    shapes = [
        bf16(experts, rows, hidden),
        bf16(experts, rows, hidden),
        bf16(experts, 2 * hidden, rows),
        bf16(2, count, columns),
    ]
    ins = [each(x, PAIR), whole(put), each(prob, PAIR), whole(mine)]
    ins += [each(a, PAIR) for a in (w_down, g, u)]
    outs = [each(s, PAIR) for s in shapes[:3]] + [kept(shapes[3])]
    scratch = [
        pltpu.VMEM((experts, rows), jnp.float32),
        pltpu.VMEM((put.shape[2], columns), jnp.bfloat16),
    ]
    flops = 2 * experts * rows * hidden * width
    return call(slope_kernel, experts // PAIR, ins, args, outs, shapes, scratch, flops)


def back_call(put, lefts, rights, start, stop, extra=None):
    experts, hidden, _ = rights[0].shape
    rows = lefts[0].shape[1]
    count = put.shape[1]
    terms = len(lefts)
    steps = (stop - start) // CHUNK
    columns = stop - start + (0 if extra is None else extra.shape[2])
    args = (put, *lefts, *rights) + (() if extra is None else (extra,))
    shapes = [bf16(count, columns)] * 2
    ins = [whole(put)] + [whole(a) for a in lefts]
    ins += [pl.BlockSpec(memory_space=pl.ANY)] * terms
    ins += [] if extra is None else [whole(extra)]
    outs = [pl.BlockSpec((count, CHUNK), lambda i: (0, i))] * 2
    scratch = [
        pltpu.VMEM((2, put.shape[2], CHUNK), jnp.bfloat16),
        pltpu.VMEM((terms, steps, experts, hidden, CHUNK), jnp.bfloat16),
        pltpu.SemaphoreType.DMA((terms, steps)),
    ]
    flops = 2 * experts * rows * (stop - start) * (hidden * terms + count)
    kernel = functools.partial(back_kernel, terms, start, steps)
    grid = steps + (0 if extra is None else 1)
    return call(kernel, grid, ins, args, outs, shapes, scratch, flops)


def grad_call(x, left, hidden):
    experts, rows, width = x.shape
    shapes = [bf16(experts, hidden, width)] * (left.shape[1] // hidden)
    flops = 2 * experts * rows * left.shape[1] * width
    ins, outs = [each(x), each(left)], [each(s) for s in shapes]
    return call(grad_kernel, experts, ins, (x, left), outs, shapes, flops=flops)


def dense_body(
    tokens, cotangent, gate_prob, expert_ids, placement, gate_weight, up_weight, down_weight
):
    tok_count, width = tokens.shape
    local = gate_weight.shape[0]
    total_experts = placement.shape[0]
    devices = lax.axis_size("dp") * lax.axis_size("expert")
    places = devices // 2 * CAP
    count = devices // 2 * tok_count
    quarter, middle = count // 4, width // 2

    slots = slots_of(expert_ids, placement)
    used = slots[:, :, None] == jnp.arange(total_experts, dtype=jnp.int32)
    prob = jnp.sum(jnp.where(used, gate_prob[:, :, None], 0.0), axis=1)
    high = lax.reduce_precision(prob, 8, 7)
    parts = jnp.concatenate([high.astype(jnp.bfloat16), (prob - high).astype(jnp.bfloat16)], axis=1)

    slot = lax.axis_index("expert") * local + jnp.arange(local * places, dtype=jnp.int32) // places
    spots = jnp.arange(2 * total_experts, dtype=jnp.int32)
    mine = (slot[:, None] == spots[None, :]).astype(jnp.bfloat16)
    both = (slot[None, :] == spots[:, None] % total_experts).astype(jnp.bfloat16)
    maps = ((slot[None, :] == spots[:, None]).astype(jnp.bfloat16), mine, both)

    def rows_of(*blocks):
        return jnp.concatenate(blocks)

    def wide(values, extra):
        return jnp.concatenate([values, extra], axis=1)

    near, far = swap(tokens, Z1), swap(tokens, Z2)
    near_parts, far_parts = swap(parts, Z1), swap(parts, Z2)
    zero = wide(tokens, parts)
    first0 = swap(zero, X, Y)
    near, far, near_parts, far_parts = together(near, far, near_parts, far_parts)

    last, last_parts = swap(far, Z1), swap(far_parts, Z1)
    middle_rows = wide(rows_of(near, far), rows_of(near_parts, far_parts))
    first1 = swap(middle_rows, X, Y)
    zero = rows_of(zero, first0)
    second0 = swap(zero, Y, X)
    cotangent, last_parts = together(cotangent, last_parts)
    grads = [swap(cotangent, bit) for bit in (Z1, Z2, Z3)]
    last, last_parts, first1, second0 = together(last, last_parts, first1, second0)

    last = wide(last, last_parts)
    first2 = swap(last, X, Y)
    middle_rows = rows_of(middle_rows, first1)
    second1 = swap(middle_rows, Y, X)
    zero = rows_of(zero, second0)
    zero_other = swap(zero, CORE)
    first2, second1, cotangent = together(first2, second1, cotangent)

    last = rows_of(last, first2)
    second2 = swap(last, Y, X)
    middle_rows = rows_of(middle_rows, second1)
    middle_other = swap(middle_rows, CORE)
    grads = rows_of(cotangent, *grads)
    grads = rows_of(grads, swap(grads, X, Y))
    last = rows_of(last, second2)
    last_other = swap(last, CORE)
    *rows, grads = together(
        zero, middle_rows, last, zero_other, middle_other, last_other, grads
    )
    far_grads = swap(grads, Y, X)
    grads_other = swap(grads, CORE)

    x, put, pick, prob_rows, g, u, h, ht = up_call(
        rows[:3], rows[3:], maps, gate_weight, up_weight, tok_count
    )
    h, far_grads, grads_other = together(h, far_grads, grads_other)
    far_grads_other = swap(far_grads, CORE)
    mixed, mixed_other = back_call(put, [h], [down_weight], 0, width)
    mixed_other, far_grads_other = together(mixed_other, far_grads_other)
    mixed = [mixed, swap(mixed_other, CORE)]

    c = place_call((grads, far_grads, grads_other, far_grads_other), pick, local)

    def leaving(parts, start, stop):
        return add(*(part[start:stop] for part in parts))

    def by_second(parts):
        return parts + [swap(leaving(parts, 2 * quarter, 4 * quarter), Y, X)]

    def by_first(parts):
        return parts + [swap(leaving(parts, quarter, 2 * quarter), X, Y)]

    def by_far(parts):
        return parts + [swap(leaving(parts, 2 * tok_count, 4 * tok_count), Z2)]

    def by_near(parts):
        return parts + [swap(leaving(parts, tok_count, 2 * tok_count), Z1)]

    weights = [gate_weight, up_weight]
    mixed[1], c = together(mixed[1], c)
    mixed = by_second(mixed)
    dg, du, dt, share = slope_call(
        c, put, prob_rows, mine.reshape(local, places, -1), down_weight, g, u
    )
    left, left_other = back_call(put, [dg, du], weights, 0, middle)
    left = [left, swap(left_other, CORE)]
    left[0], mixed[2], dg, du = together(left[0], mixed[2], dg, du)
    mixed = by_first(mixed)
    right, right_other = back_call(put, [dg, du], weights, middle, width, share)
    right = [right, swap(right_other, CORE)]

    right[0], left[1], mixed[3] = together(right[0], left[1], mixed[3])
    left, mixed = by_second(left), by_far(mixed)
    left[0], ht = together(left[0], ht)
    (down_weight_grad,) = grad_call(c, ht, ht.shape[1])

    right[1], left[2], mixed[4], down_weight_grad = together(
        right[1], left[2], mixed[4], down_weight_grad
    )
    right, left, mixed = by_second(right), by_first(left), by_near(mixed)
    right[0], dt = together(right[0], dt)
    gate_weight_grad, up_weight_grad = grad_call(x, dt, ht.shape[1])

    right[2], left[3], mixed[5], gate_weight_grad = together(
        right[2], left[3], mixed[5], gate_weight_grad
    )
    right, left = by_first(right), by_far(left)
    right, left = by_far(right), by_near(left)
    right = by_near(right)
    mixed, left, right = (leaving(parts, 0, tok_count) for parts in (mixed, left, right))
    token_grad = jnp.concatenate([left, right[:, : width - middle]], axis=1)
    share = right[:, width - middle : width - middle + total_experts].astype(jnp.float32)
    gate_grad = jnp.sum(jnp.where(used, share[:, None, :], 0.0), axis=2)
    return (mixed, token_grad, gate_grad, gate_weight_grad, up_weight_grad, down_weight_grad)


def routed_body(tokens, cotangent, gate_prob, expert_ids, placement, gate_weight, up_weight, down_weight):
    tok_count, model_width = tokens.shape
    top_count = expert_ids.shape[1]
    expert_devs = lax.axis_size("expert")
    local_experts = gate_weight.shape[0]
    total_experts = placement.shape[0]
    capacity = CAP
    flat_ids = expert_ids.reshape(-1)
    matches_id = flat_ids[:, None] == jnp.arange(total_experts, dtype=jnp.int32)[None, :]
    slot_ids = jnp.sum(jnp.where(matches_id, placement[None, :], 0), axis=1)
    pair_order = jnp.arange(flat_ids.shape[0], dtype=jnp.int32)
    earlier = (slot_ids[:, None] == slot_ids[None, :]) & (pair_order[None, :] < pair_order[:, None])
    position = slot_ids * capacity + jnp.sum(earlier.astype(jnp.int32), axis=1)
    matches = jnp.arange(total_experts * capacity, dtype=jnp.int32)[:, None] == position[None, :]
    matches = matches.reshape(total_experts * capacity, tok_count, top_count)
    dispatch = jnp.any(matches, axis=2).astype(jnp.bfloat16)
    weight_map = jnp.sum(jnp.where(matches, gate_prob[None, :, :], 0.0), axis=2)
    sent_rows = jnp.dot(dispatch, tokens, preferred_element_type=jnp.float32).astype(jnp.bfloat16)
    sent_grads = jnp.dot(
        weight_map, cotangent.astype(jnp.float32), precision=lax.Precision.HIGHEST
    ).astype(jnp.bfloat16)
    block_shape = (1, expert_devs, local_experts, capacity, model_width)
    sent_rows = sent_rows.reshape(block_shape)
    sent_grads = sent_grads.reshape(block_shape)
    got_rows, got_grads = (
        lax.all_to_all(sent_rows, "expert", split_axis=1, concat_axis=1, tiled=True),
        lax.all_to_all(sent_grads, "expert", split_axis=1, concat_axis=1, tiled=True),
    )
    routed, routed_grads = (
        lax.all_gather(got_rows, "dp", axis=0, tiled=True),
        lax.all_gather(got_grads, "dp", axis=0, tiled=True),
    )
    gate_pre = jnp.einsum(
        "asjcd,jfd->asjcf", routed, gate_weight, preferred_element_type=jnp.float32
    )
    up_pre = jnp.einsum("asjcd,jfd->asjcf", routed, up_weight, preferred_element_type=jnp.float32)
    silu_v, slope = gated(gate_pre)
    hidden = (silu_v * up_pre).astype(jnp.bfloat16)
    out_part = jnp.einsum(
        "asjcf,jfd->asjcd", hidden, down_weight, preferred_element_type=jnp.float32
    )
    d_hidden = jnp.einsum(
        "asjcd,jfd->asjcf", routed_grads, down_weight, preferred_element_type=jnp.float32
    )
    d_gate_pre = (d_hidden * up_pre * slope).astype(jnp.bfloat16)
    d_up_pre = (d_hidden * silu_v).astype(jnp.bfloat16)
    back_part = jnp.einsum(
        "asjcf,jfd->asjcd", d_gate_pre, gate_weight, preferred_element_type=jnp.float32
    )
    back_part = back_part + jnp.einsum(
        "asjcf,jfd->asjcd", d_up_pre, up_weight, preferred_element_type=jnp.float32
    )
    down_grad = jnp.einsum(
        "asjcf,asjcd->jfd", hidden, routed_grads, preferred_element_type=jnp.float32
    ).astype(jnp.bfloat16)
    gate_grad_w = jnp.einsum(
        "asjcf,asjcd->jfd", d_gate_pre, routed, preferred_element_type=jnp.float32
    ).astype(jnp.bfloat16)
    up_grad_w = jnp.einsum(
        "asjcf,asjcd->jfd", d_up_pre, routed, preferred_element_type=jnp.float32
    ).astype(jnp.bfloat16)
    summed = (
        lax.psum_scatter(
            out_part.astype(jnp.bfloat16), "dp", scatter_dimension=0, tiled=True
        ).astype(jnp.float32),
        lax.psum_scatter(
            back_part.astype(jnp.bfloat16), "dp", scatter_dimension=0, tiled=True
        ).astype(jnp.float32),
    )
    back_out, back_grad = (
        lax.all_to_all(
            summed[0].astype(jnp.bfloat16), "expert", split_axis=1, concat_axis=1, tiled=True
        ),
        lax.all_to_all(
            summed[1].astype(jnp.bfloat16), "expert", split_axis=1, concat_axis=1, tiled=True
        ),
    )
    out_flat = back_out.reshape(total_experts * capacity, model_width)
    grad_flat = back_grad.reshape(total_experts * capacity, model_width)
    chosen_out = out_flat[position].reshape(tok_count, top_count, model_width)
    chosen_grad = grad_flat[position].reshape(tok_count, top_count, model_width)
    mixed = jnp.einsum(
        "tk,tkd->td", gate_prob, chosen_out.astype(jnp.float32), precision=lax.Precision.HIGHEST
    ).astype(jnp.bfloat16)
    gate_grad = jnp.einsum("td,tkd->tk", cotangent, chosen_out, preferred_element_type=jnp.float32)
    token_grad = jnp.sum(chosen_grad.astype(jnp.float32), axis=1).astype(jnp.bfloat16)
    return (mixed, token_grad, gate_grad, gate_grad_w, up_grad_w, down_grad)


def body(*args):
    tokens, gate_weight = args[0], args[5]
    mesh_fits = (lax.axis_size("dp"), lax.axis_size("expert")) == (4, 8)
    if mesh_fits and tokens.shape[0] <= gate_weight.shape[0] * CAP:
        return dense_body(*args)
    return routed_body(*args)


def solution(mesh):
    return jax.shard_map(
        body,
        mesh=mesh,
        in_specs=(
            P(("dp", "expert"), None),
            P(("dp", "expert"), None),
            P(("dp", "expert"), None),
            P(("dp", "expert"), None),
            P(),
            P("expert", "dp", None),
            P("expert", "dp", None),
            P("expert", "dp", None),
        ),
        out_specs=(
            P(("dp", "expert"), None),
            P(("dp", "expert"), None),
            P(("dp", "expert"), None),
            P("expert", "dp", None),
            P("expert", "dp", None),
            P("expert", "dp", None),
        ),
        check_vma=False,
    )
```

```python
import functools
import math

import jax
import jax.numpy as jnp
from jax import lax
from jax.experimental import pallas as pl
from jax.experimental.pallas import tpu as pltpu
from jax.sharding import PartitionSpec as P

CAP = 3
AXES = ("dp", "expert")
CORE, Z1, Z2, Z3, X, Y = 1, 2, 4, 6, 8, 16
GROUPS = ((0,), (1, 2), (3,))
CHUNK = 512
WIDE = 1024
PAIR = 2
MIB = 1 << 20

NT = (((1,), (1,)), ((), ()))
NN = (((1,), (0,)), ((), ()))


def gated(values):
    sigmoid_v = jax.nn.sigmoid(values)
    return (values * sigmoid_v, sigmoid_v * (1.0 + values * (1.0 - sigmoid_v)))


def swap(values, even, odd=None):
    odd = even if odd is None else odd
    count = lax.axis_size("dp") * lax.axis_size("expert")
    pairs = [(i, i ^ (odd if i & CORE else even)) for i in range(count)]
    return lax.ppermute(values, AXES, pairs)


def add(*parts):
    total = parts[0].astype(jnp.float32)
    for part in parts[1:]:
        total = total + part.astype(jnp.float32)
    return total.astype(jnp.bfloat16)


def together(*values):
    return lax.optimization_barrier(values)


def slots_of(expert_ids, placement):
    total = placement.shape[0]
    matches = expert_ids[:, :, None] == jnp.arange(total, dtype=jnp.int32)
    return jnp.sum(jnp.where(matches, placement, 0), axis=2)


def dot(a, b, dims=NN):
    return lax.dot_general(a, b, dims, preferred_element_type=jnp.float32)


def iota(shape, axis):
    return lax.broadcasted_iota(jnp.int32, shape, axis)


def ordered(pieces, tok_count):
    rows = []
    for quarter in range(4):
        for piece, group in zip(pieces, GROUPS):
            size = len(group) * tok_count
            rows.append(piece[quarter * size : (quarter + 1) * size])
    return jnp.concatenate(rows, axis=0)


def put_in_places(pick, rows, half, x_ref):
    experts, both = x_ref.shape[:2]
    places = both // 2
    rows = dot(pick, rows).astype(jnp.bfloat16)
    for e in range(experts):
        x_ref[e, half * places : (half + 1) * places] = rows[e * places : (e + 1) * places]


def route_kernel(tok_count, *refs):
    rows_refs, part_refs, (mine_ref, mine_t_ref, both_ref) = refs[:6], refs[6:12], refs[12:15]
    x_ref, put_ref, pick_ref, prob_ref = refs[16:]
    experts, both = x_ref.shape[:2]
    places = both // 2
    count = pick_ref.shape[2]

    @pl.when(pl.program_id(0) == 0)
    def _():
        row, col = iota((count, count), 0), iota((count, count), 1)
        block = lax.div(row, tok_count)
        before = ((col < row) & (lax.div(col, tok_count) == block)).astype(jnp.bfloat16)
        columns = mine_ref.shape[0]
        first = (lax.div(iota((count, columns), 0), tok_count) * CAP).astype(jnp.float32)
        spot = lax.rem(iota((count, experts * places), 1), places).astype(jnp.float32)
        spot_t = lax.rem(iota((experts * places, count), 0), places).astype(jnp.float32)
        for half in range(2):
            prob = ordered(part_refs[3 * half : 3 * half + 3], tok_count)
            taken = prob.astype(jnp.float32) > 0.0
            rank = dot(before, jnp.where(taken, 1.0, 0.0).astype(jnp.bfloat16))
            place = jnp.where(taken, rank + first, -1.0).astype(jnp.bfloat16)
            put = jnp.where(dot(place, mine_ref[...]) == spot, 1.0, 0.0)
            pick = dot(mine_t_ref[...], place, NT) == spot_t
            put_ref[half] = put.astype(jnp.bfloat16)
            pick_ref[half] = jnp.where(pick, 1.0, 0.0).astype(jnp.bfloat16)
            weight = jnp.sum(put * dot(prob, both_ref[...]), axis=0, keepdims=True)
            for i in range(experts):
                prob_ref[i, :, half * places : (half + 1) * places] = weight[
                    :, i * places : (i + 1) * places
                ]

    for half in range(2):
        rows = ordered(rows_refs[3 * half : 3 * half + 3], tok_count)
        put_in_places(pick_ref[half], rows, half, x_ref)


def up_kernel(x_ref, prob_ref, gate_ref, up_ref, g_ref, u_ref, h_ref, ht_ref, held_ref, sems):
    step = pl.program_id(0)
    both, width = x_ref.shape[1:]
    hidden = gate_ref.shape[1]

    def copies(at):
        slot = lax.rem(at, 2)
        for i in range(PAIR):
            e = PAIR * at + i
            for j, source in enumerate((gate_ref, up_ref)):
                held = held_ref.at[slot, i, hidden * j : hidden * (j + 1)]
                yield pltpu.make_async_copy(source.at[e], held, sems.at[slot, 2 * i + j])

    @pl.when(step == 0)
    def _():
        for copy in copies(step):
            copy.start()

    @pl.when(step + 1 < pl.num_programs(0))
    def _():
        for copy in copies(step + 1):
            copy.start()

    for copy in copies(step):
        copy.wait()
    weights = held_ref[lax.rem(step, 2)].reshape(PAIR * 2 * hidden, width)
    product = dot(weights, x_ref[...].reshape(PAIR * both, width), NT)
    for i in range(PAIR):
        own = product[2 * hidden * i : 2 * hidden * (i + 1), both * i : both * (i + 1)]
        g, u = own[:hidden], own[hidden:]
        g_ref[i] = g
        u_ref[i] = u
        silu_v, _ = gated(g)
        scaled = silu_v * u * prob_ref[i]
        ht_ref[i] = scaled.astype(jnp.bfloat16)
        h_ref[i] = scaled.T.astype(jnp.bfloat16)


def place_kernel(own0, own1, other0, other1, pick_ref, x_ref):
    for half, pieces in enumerate(((own0, own1), (other0, other1))):
        rows = jnp.concatenate([pieces[0][...], pieces[1][...]], axis=0)
        put_in_places(pick_ref[half], rows, half, x_ref)


def slope_kernel(x_ref, put_ref, prob_ref, mine_ref, down_ref, g_ref, u_ref,
                 dg_ref, du_ref, dt_ref, share_ref, shares_ref, terms_ref):
    e = pl.program_id(0)
    experts, both = shares_ref.shape
    places = both // 2
    _, hidden, width = down_ref.shape
    product = dot(
        down_ref[...].reshape(PAIR * hidden, width), x_ref[...].reshape(PAIR * both, width), NT
    )
    for i in range(PAIR):
        plain = product[hidden * i : hidden * (i + 1), both * i : both * (i + 1)]
        g, u = g_ref[i], u_ref[i]
        silu_v, slope = gated(g)
        shares_ref[pl.ds(PAIR * e + i, 1), :] = jnp.sum(silu_v * u * plain, axis=0, keepdims=True)
        scaled = plain * prob_ref[i]
        dg = scaled * u * slope
        du = scaled * silu_v
        dt_ref[i, :hidden] = dg.astype(jnp.bfloat16)
        dt_ref[i, hidden:] = du.astype(jnp.bfloat16)
        dg_ref[i] = dg.T.astype(jnp.bfloat16)
        du_ref[i] = du.T.astype(jnp.bfloat16)

    @pl.when(e == pl.num_programs(0) - 1)
    def _():
        shares = shares_ref[...].T
        for half in range(2):
            for i in range(experts):
                share = shares[half * places : (half + 1) * places, i : i + 1]
                share = (share * mine_ref[i].astype(jnp.float32)).astype(jnp.bfloat16)
                terms_ref[i * places : (i + 1) * places] = share
            share_ref[half] = dot(put_ref[half], terms_ref[...]).astype(jnp.bfloat16)


def back_kernel(terms, start, steps, put_ref, *refs):
    lefts, rights = refs[:terms], refs[terms : 2 * terms]
    extra_ref = refs[2 * terms] if len(refs) > 2 * terms + 5 else None
    own_ref, other_ref, rows_ref, held_ref, sems = refs[-5:]
    experts, places = rights[0].shape[0], put_ref.shape[2] // rights[0].shape[0]
    step = pl.program_id(0)

    def copy(i, at):
        columns = pl.ds(pl.multiple_of(start + at * CHUNK, CHUNK), CHUNK)
        return pltpu.make_async_copy(rights[i].at[:, :, columns], held_ref.at[i, at], sems.at[i, at])

    @pl.when(step == 0)
    def _():
        for at in range(steps):
            for i in range(terms):
                copy(i, at).start()

    @pl.when(step < steps)
    def _():
        for i in range(terms):
            copy(i, step).wait()
        for e in range(experts):
            rows = dot(lefts[0][e], held_ref[0, step, e])
            for i in range(1, terms):
                rows = rows + dot(lefts[i][e], held_ref[i, step, e])
            rows = rows.astype(jnp.bfloat16)
            for half in range(2):
                rows_ref[half, e * places : (e + 1) * places] = rows[half * places : (half + 1) * places]
        own_ref[...] = dot(put_ref[0], rows_ref[0]).astype(jnp.bfloat16)
        other_ref[...] = dot(put_ref[1], rows_ref[1]).astype(jnp.bfloat16)

    if extra_ref is not None:

        @pl.when(step == steps)
        def _():
            columns = extra_ref.shape[2]
            own_ref[:, :columns] = extra_ref[0]
            other_ref[:, :columns] = extra_ref[1]


def grad_kernel(x_ref, left, *outs):
    hidden = outs[0].shape[1]
    for at in range(0, x_ref.shape[2], WIDE):
        product = dot(left[0], x_ref[0, :, at : at + WIDE]).astype(jnp.bfloat16)
        for i, out in enumerate(outs):
            out[0, :, at : at + WIDE] = product[hidden * i : hidden * (i + 1)]


def whole(a):
    shape = a.shape
    return pl.BlockSpec(shape, lambda i: (0,) * len(shape), pipeline_mode=pl.Buffered(1))


def kept(a):
    shape = a.shape
    return pl.BlockSpec(shape, lambda i: (0,) * len(shape))


def each(a, size=1):
    shape = a.shape
    return pl.BlockSpec((size, *shape[1:]), lambda i: (i,) + (0,) * (len(shape) - 1))


def near_core(a):
    return pltpu.with_memory_space_constraint(a, pltpu.VMEM)


def in_hbm(a):
    return pltpu.with_memory_space_constraint(a, pltpu.HBM)


def bf16(*shape):
    return jax.ShapeDtypeStruct(shape, jnp.bfloat16)


def f32(*shape):
    return jax.ShapeDtypeStruct(shape, jnp.float32)


def call(kernel, grid, ins, args, outs, shapes, scratch=(), flops=0):
    moved = sum(math.prod(a.shape) * a.dtype.itemsize for a in (*args, *shapes))
    return pl.pallas_call(
        kernel,
        grid=(grid,),
        in_specs=ins,
        out_specs=outs,
        out_shape=shapes,
        scratch_shapes=scratch,
        compiler_params=pltpu.CompilerParams(vmem_limit_bytes=24 * MIB),
        cost_estimate=pl.CostEstimate(flops=flops, bytes_accessed=moved, transcendentals=0),
    )(*args)


def fetch_kernel(source, after, held, mark, sem):
    copy = pltpu.make_async_copy(source, held, sem)
    copy.start()
    mark[...] = jnp.zeros_like(mark)
    copy.wait()


def fetch_call(weight, after):
    return pl.pallas_call(
        fetch_kernel,
        in_specs=[pl.BlockSpec(memory_space=pl.ANY)] * 2,
        out_specs=[pl.BlockSpec(memory_space=pl.ANY), pl.BlockSpec(memory_space=pltpu.VMEM)],
        out_shape=[pltpu.VMEM(weight.shape, weight.dtype), f32(8, 128)],
        scratch_shapes=[pltpu.SemaphoreType.DMA],
        compiler_params=pltpu.CompilerParams(vmem_limit_bytes=MIB),
        cost_estimate=pl.CostEstimate(
            flops=0, bytes_accessed=weight.size * weight.dtype.itemsize, transcendentals=0
        ),
    )(in_hbm(weight), after)


def route_call(own, other, maps, mark, experts, width, tok_count):
    count = sum(piece.shape[0] for piece in own)
    places = count // tok_count * CAP
    columns = own[0].shape[1] - width
    pieces = (*own, *other)
    shapes = [
        pltpu.HBM((experts, 2 * places, width), jnp.bfloat16),
        bf16(2, count, experts * places),
        bf16(2, experts * places, count),
        f32(experts, 1, 2 * places),
    ]
    ins = [pl.BlockSpec((piece.shape[0], WIDE), lambda i: (0, i)) for piece in pieces]
    ins += [pl.BlockSpec((piece.shape[0], columns), lambda i: (0, width // columns)) for piece in pieces]
    ins += [whole(a) for a in (*maps, mark)]
    outs = [pl.BlockSpec((experts, 2 * places, WIDE), lambda i: (0, 0, i))]
    outs += [kept(s) for s in shapes[1:]]
    flops = 4 * experts * places * count * width
    kernel = functools.partial(route_kernel, tok_count)
    return call(kernel, width // WIDE, ins, (*pieces, *pieces, *maps, mark), outs, shapes, flops=flops)


def up_call(x, prob, w_gate, w_up):
    experts, hidden, width = w_gate.shape
    rows = x.shape[1]
    args = (in_hbm(x), prob, near_core(w_gate), near_core(w_up))
    shapes = [
        f32(experts, hidden, rows),
        f32(experts, hidden, rows),
        bf16(experts, rows, hidden),
        bf16(experts, hidden, rows),
    ]
    ins = [each(x, PAIR), each(prob, PAIR)] + [pl.BlockSpec(memory_space=pl.ANY)] * 2
    outs = [each(s, PAIR) for s in shapes]
    scratch = [
        pltpu.VMEM((2, PAIR, 2 * hidden, width), jnp.bfloat16),
        pltpu.SemaphoreType.DMA((2, 2 * PAIR)),
    ]
    flops = 4 * experts * rows * hidden * width
    return call(up_kernel, experts // PAIR, ins, args, outs, shapes, scratch, flops)


def place_call(pieces, pick, experts):
    _, rows, count = pick.shape
    size, width = pieces[0].shape
    shape = pltpu.HBM((experts, 2 * rows // experts, width), jnp.bfloat16)
    ins = [pl.BlockSpec((size, WIDE), lambda i: (0, i))] * len(pieces) + [whole(pick)]
    outs = [pl.BlockSpec((*shape.shape[:2], WIDE), lambda i: (0, 0, i))]
    flops = 4 * rows * count * width
    return call(place_kernel, width // WIDE, ins, (*pieces, pick), outs, [shape], flops=flops)[0]


def slope_call(x, put, prob, mine, w_down, g, u):
    experts, hidden, width = w_down.shape
    rows, count, columns = x.shape[1], put.shape[1], mine.shape[2]
    args = (in_hbm(x), put, prob, mine, in_hbm(w_down), g, u)
    shapes = [
        bf16(experts, rows, hidden),
        bf16(experts, rows, hidden),
        bf16(experts, 2 * hidden, rows),
        bf16(2, count, columns),
    ]
    ins = [each(x, PAIR), whole(put), each(prob, PAIR), whole(mine)]
    ins += [each(a, PAIR) for a in (w_down, g, u)]
    outs = [each(s, PAIR) for s in shapes[:3]] + [kept(shapes[3])]
    scratch = [
        pltpu.VMEM((experts, rows), jnp.float32),
        pltpu.VMEM((put.shape[2], columns), jnp.bfloat16),
    ]
    flops = 2 * experts * rows * hidden * width
    return call(slope_kernel, experts // PAIR, ins, args, outs, shapes, scratch, flops)


def back_call(put, lefts, rights, start, stop, extra=None):
    experts, hidden, _ = rights[0].shape
    rows = lefts[0].shape[1]
    count = put.shape[1]
    terms = len(lefts)
    steps = (stop - start) // CHUNK
    columns = stop - start + (0 if extra is None else extra.shape[2])
    args = (put, *lefts, *rights) + (() if extra is None else (extra,))
    shapes = [bf16(count, columns)] * 2
    ins = [whole(put)] + [whole(a) for a in lefts]
    ins += [pl.BlockSpec(memory_space=pl.ANY)] * terms
    ins += [] if extra is None else [whole(extra)]
    outs = [pl.BlockSpec((count, CHUNK), lambda i: (0, i))] * 2
    scratch = [
        pltpu.VMEM((2, put.shape[2], CHUNK), jnp.bfloat16),
        pltpu.VMEM((terms, steps, experts, hidden, CHUNK), jnp.bfloat16),
        pltpu.SemaphoreType.DMA((terms, steps)),
    ]
    flops = 2 * experts * rows * (stop - start) * (hidden * terms + count)
    kernel = functools.partial(back_kernel, terms, start, steps)
    grid = steps + (0 if extra is None else 1)
    return call(kernel, grid, ins, args, outs, shapes, scratch, flops)


def grad_call(x, left, hidden):
    experts, rows, width = x.shape
    shapes = [bf16(experts, hidden, width)] * (left.shape[1] // hidden)
    flops = 2 * experts * rows * left.shape[1] * width
    ins, outs = [each(x), each(left)], [each(s) for s in shapes]
    return call(grad_kernel, experts, ins, (in_hbm(x), left), outs, shapes, flops=flops)


def dense_body(
    tokens, cotangent, gate_prob, expert_ids, placement, gate_weight, up_weight, down_weight
):
    tok_count, width = tokens.shape
    local = gate_weight.shape[0]
    total_experts = placement.shape[0]
    devices = lax.axis_size("dp") * lax.axis_size("expert")
    places = devices // 2 * CAP
    count = devices // 2 * tok_count
    quarter, middle = count // 4, width // 2

    slots = slots_of(expert_ids, placement)
    used = slots[:, :, None] == jnp.arange(total_experts, dtype=jnp.int32)
    prob = jnp.sum(jnp.where(used, gate_prob[:, :, None], 0.0), axis=1)
    high = lax.reduce_precision(prob, 8, 7)
    parts = jnp.concatenate([high.astype(jnp.bfloat16), (prob - high).astype(jnp.bfloat16)], axis=1)

    slot = lax.axis_index("expert") * local + jnp.arange(local * places, dtype=jnp.int32) // places
    spots = jnp.arange(2 * total_experts, dtype=jnp.int32)
    mine = (slot[:, None] == spots[None, :]).astype(jnp.bfloat16)
    both = (slot[None, :] == spots[:, None] % total_experts).astype(jnp.bfloat16)
    maps = ((slot[None, :] == spots[:, None]).astype(jnp.bfloat16), mine, both)

    def rows_of(*blocks):
        return jnp.concatenate(blocks)

    def wide(values, extra):
        return jnp.concatenate([values, extra], axis=1)

    near, far = swap(tokens, Z1), swap(tokens, Z2)
    near_parts, far_parts = swap(parts, Z1), swap(parts, Z2)
    zero = wide(tokens, parts)
    first0 = swap(zero, X, Y)
    near, far, near_parts, far_parts = together(near, far, near_parts, far_parts)

    last, last_parts = swap(far, Z1), swap(far_parts, Z1)
    middle_rows = wide(rows_of(near, far), rows_of(near_parts, far_parts))
    first1 = swap(middle_rows, X, Y)
    zero = rows_of(zero, first0)
    second0 = swap(zero, Y, X)
    cotangent, last_parts = together(cotangent, last_parts)
    grads = [swap(cotangent, bit) for bit in (Z1, Z2, Z3)]
    last, last_parts, first1, second0, gate_weight = together(
        last, last_parts, first1, second0, gate_weight
    )
    gate_weight, mark = fetch_call(gate_weight, last_parts)

    last = wide(last, last_parts)
    first2 = swap(last, X, Y)
    middle_rows = rows_of(middle_rows, first1)
    second1 = swap(middle_rows, Y, X)
    zero = rows_of(zero, second0)
    zero_other = swap(zero, CORE)
    first2, second1, cotangent, mark, up_weight = together(
        first2, second1, cotangent, mark, up_weight
    )
    up_weight, mark = fetch_call(up_weight, mark)

    last = rows_of(last, first2)
    second2 = swap(last, Y, X)
    middle_rows = rows_of(middle_rows, second1)
    middle_other = swap(middle_rows, CORE)
    grads = rows_of(cotangent, *grads)
    grads = rows_of(grads, swap(grads, X, Y))
    last = rows_of(last, second2)
    last_other = swap(last, CORE)
    last, last_other, mark = together(last, last_other, mark)
    x, put, pick, prob_rows = route_call(
        (zero, middle_rows, last),
        (zero_other, middle_other, last_other),
        maps,
        mark,
        local,
        width,
        tok_count,
    )
    x, grads = together(x, grads)
    far_grads = swap(grads, Y, X)
    grads_other = swap(grads, CORE)

    g, u, h, ht = up_call(x, prob_rows, gate_weight, up_weight)
    h, far_grads, grads_other = together(h, far_grads, grads_other)
    far_grads_other = swap(far_grads, CORE)
    mixed, mixed_other = back_call(put, [h], [in_hbm(down_weight)], 0, width)
    mixed_other, far_grads_other = together(mixed_other, far_grads_other)
    mixed = [mixed, swap(mixed_other, CORE)]

    c = place_call((grads, far_grads, grads_other, far_grads_other), pick, local)

    def leaving(parts, start, stop):
        return add(*(part[start:stop] for part in parts))

    def by_second(parts):
        return parts + [swap(leaving(parts, 2 * quarter, 4 * quarter), Y, X)]

    def by_first(parts):
        return parts + [swap(leaving(parts, quarter, 2 * quarter), X, Y)]

    def by_far(parts):
        return parts + [swap(leaving(parts, 2 * tok_count, 4 * tok_count), Z2)]

    def by_near(parts):
        return parts + [swap(leaving(parts, tok_count, 2 * tok_count), Z1)]

    weights = [near_core(gate_weight), near_core(up_weight)]
    mixed[1], c = together(mixed[1], c)
    mixed = by_second(mixed)
    dg, du, dt, share = slope_call(
        c, put, prob_rows, mine.reshape(local, places, -1), down_weight, g, u
    )
    left, left_other = back_call(put, [dg, du], weights, 0, middle)
    left = [left, swap(left_other, CORE)]
    left[0], mixed[2], dg, du = together(left[0], mixed[2], dg, du)
    mixed = by_first(mixed)
    right, right_other = back_call(put, [dg, du], weights, middle, width, share)
    right = [right, swap(right_other, CORE)]

    right[0], left[1], mixed[3] = together(right[0], left[1], mixed[3])
    left, mixed = by_second(left), by_far(mixed)
    left[0], ht = together(left[0], ht)
    (down_weight_grad,) = grad_call(c, ht, ht.shape[1])

    right[1], left[2], mixed[4], down_weight_grad = together(
        right[1], left[2], mixed[4], down_weight_grad
    )
    right, left, mixed = by_second(right), by_first(left), by_near(mixed)
    right[0], dt = together(right[0], dt)
    gate_weight_grad, up_weight_grad = grad_call(x, dt, ht.shape[1])

    right[2], left[3], mixed[5], gate_weight_grad = together(
        right[2], left[3], mixed[5], gate_weight_grad
    )
    right, left = by_first(right), by_far(left)
    right, left = by_far(right), by_near(left)
    right = by_near(right)
    mixed, left, right = (leaving(parts, 0, tok_count) for parts in (mixed, left, right))
    token_grad = jnp.concatenate([left, right[:, : width - middle]], axis=1)
    share = right[:, width - middle : width - middle + total_experts].astype(jnp.float32)
    gate_grad = jnp.sum(jnp.where(used, share[:, None, :], 0.0), axis=2)
    return (mixed, token_grad, gate_grad, gate_weight_grad, up_weight_grad, down_weight_grad)


def routed_body(tokens, cotangent, gate_prob, expert_ids, placement, gate_weight, up_weight, down_weight):
    tok_count, model_width = tokens.shape
    top_count = expert_ids.shape[1]
    expert_devs = lax.axis_size("expert")
    local_experts = gate_weight.shape[0]
    total_experts = placement.shape[0]
    capacity = CAP
    flat_ids = expert_ids.reshape(-1)
    matches_id = flat_ids[:, None] == jnp.arange(total_experts, dtype=jnp.int32)[None, :]
    slot_ids = jnp.sum(jnp.where(matches_id, placement[None, :], 0), axis=1)
    pair_order = jnp.arange(flat_ids.shape[0], dtype=jnp.int32)
    earlier = (slot_ids[:, None] == slot_ids[None, :]) & (pair_order[None, :] < pair_order[:, None])
    position = slot_ids * capacity + jnp.sum(earlier.astype(jnp.int32), axis=1)
    matches = jnp.arange(total_experts * capacity, dtype=jnp.int32)[:, None] == position[None, :]
    matches = matches.reshape(total_experts * capacity, tok_count, top_count)
    dispatch = jnp.any(matches, axis=2).astype(jnp.bfloat16)
    weight_map = jnp.sum(jnp.where(matches, gate_prob[None, :, :], 0.0), axis=2)
    sent_rows = jnp.dot(dispatch, tokens, preferred_element_type=jnp.float32).astype(jnp.bfloat16)
    sent_grads = jnp.dot(
        weight_map, cotangent.astype(jnp.float32), precision=lax.Precision.HIGHEST
    ).astype(jnp.bfloat16)
    block_shape = (1, expert_devs, local_experts, capacity, model_width)
    sent_rows = sent_rows.reshape(block_shape)
    sent_grads = sent_grads.reshape(block_shape)
    got_rows, got_grads = (
        lax.all_to_all(sent_rows, "expert", split_axis=1, concat_axis=1, tiled=True),
        lax.all_to_all(sent_grads, "expert", split_axis=1, concat_axis=1, tiled=True),
    )
    routed, routed_grads = (
        lax.all_gather(got_rows, "dp", axis=0, tiled=True),
        lax.all_gather(got_grads, "dp", axis=0, tiled=True),
    )
    gate_pre = jnp.einsum(
        "asjcd,jfd->asjcf", routed, gate_weight, preferred_element_type=jnp.float32
    )
    up_pre = jnp.einsum("asjcd,jfd->asjcf", routed, up_weight, preferred_element_type=jnp.float32)
    silu_v, slope = gated(gate_pre)
    hidden = (silu_v * up_pre).astype(jnp.bfloat16)
    out_part = jnp.einsum(
        "asjcf,jfd->asjcd", hidden, down_weight, preferred_element_type=jnp.float32
    )
    d_hidden = jnp.einsum(
        "asjcd,jfd->asjcf", routed_grads, down_weight, preferred_element_type=jnp.float32
    )
    d_gate_pre = (d_hidden * up_pre * slope).astype(jnp.bfloat16)
    d_up_pre = (d_hidden * silu_v).astype(jnp.bfloat16)
    back_part = jnp.einsum(
        "asjcf,jfd->asjcd", d_gate_pre, gate_weight, preferred_element_type=jnp.float32
    )
    back_part = back_part + jnp.einsum(
        "asjcf,jfd->asjcd", d_up_pre, up_weight, preferred_element_type=jnp.float32
    )
    down_grad = jnp.einsum(
        "asjcf,asjcd->jfd", hidden, routed_grads, preferred_element_type=jnp.float32
    ).astype(jnp.bfloat16)
    gate_grad_w = jnp.einsum(
        "asjcf,asjcd->jfd", d_gate_pre, routed, preferred_element_type=jnp.float32
    ).astype(jnp.bfloat16)
    up_grad_w = jnp.einsum(
        "asjcf,asjcd->jfd", d_up_pre, routed, preferred_element_type=jnp.float32
    ).astype(jnp.bfloat16)
    summed = (
        lax.psum_scatter(
            out_part.astype(jnp.bfloat16), "dp", scatter_dimension=0, tiled=True
        ).astype(jnp.float32),
        lax.psum_scatter(
            back_part.astype(jnp.bfloat16), "dp", scatter_dimension=0, tiled=True
        ).astype(jnp.float32),
    )
    back_out, back_grad = (
        lax.all_to_all(
            summed[0].astype(jnp.bfloat16), "expert", split_axis=1, concat_axis=1, tiled=True
        ),
        lax.all_to_all(
            summed[1].astype(jnp.bfloat16), "expert", split_axis=1, concat_axis=1, tiled=True
        ),
    )
    out_flat = back_out.reshape(total_experts * capacity, model_width)
    grad_flat = back_grad.reshape(total_experts * capacity, model_width)
    chosen_out = out_flat[position].reshape(tok_count, top_count, model_width)
    chosen_grad = grad_flat[position].reshape(tok_count, top_count, model_width)
    mixed = jnp.einsum(
        "tk,tkd->td", gate_prob, chosen_out.astype(jnp.float32), precision=lax.Precision.HIGHEST
    ).astype(jnp.bfloat16)
    gate_grad = jnp.einsum("td,tkd->tk", cotangent, chosen_out, preferred_element_type=jnp.float32)
    token_grad = jnp.sum(chosen_grad.astype(jnp.float32), axis=1).astype(jnp.bfloat16)
    return (mixed, token_grad, gate_grad, gate_grad_w, up_grad_w, down_grad)


def body(*args):
    tokens, gate_weight = args[0], args[5]
    mesh_fits = (lax.axis_size("dp"), lax.axis_size("expert")) == (4, 8)
    if mesh_fits and tokens.shape[0] <= gate_weight.shape[0] * CAP:
        return dense_body(*args)
    return routed_body(*args)


def solution(mesh):
    return jax.shard_map(
        body,
        mesh=mesh,
        in_specs=(
            P(("dp", "expert"), None),
            P(("dp", "expert"), None),
            P(("dp", "expert"), None),
            P(("dp", "expert"), None),
            P(),
            P("expert", "dp", None),
            P("expert", "dp", None),
            P("expert", "dp", None),
        ),
        out_specs=(
            P(("dp", "expert"), None),
            P(("dp", "expert"), None),
            P(("dp", "expert"), None),
            P("expert", "dp", None),
            P("expert", "dp", None),
            P("expert", "dp", None),
        ),
        check_vma=False,
    )
```

```python
import functools
import math

import jax
import jax.numpy as jnp
from jax import lax
from jax.experimental import pallas as pl
from jax.experimental.pallas import tpu as pltpu
from jax.sharding import PartitionSpec as P

CAP = 3
AXES = ("dp", "expert")
CORE, Z1, Z2, Z3, X, Y = 1, 2, 4, 6, 8, 16
GROUPS = ((0,), (1, 2), (3,))
CHUNK = 512
WIDE = 1024
PAIR = 2
MIB = 1 << 20

NT = (((1,), (1,)), ((), ()))
NN = (((1,), (0,)), ((), ()))


def gated(values):
    sigmoid_v = jax.nn.sigmoid(values)
    return (values * sigmoid_v, sigmoid_v * (1.0 + values * (1.0 - sigmoid_v)))


def swap(values, even, odd=None):
    odd = even if odd is None else odd
    count = lax.axis_size("dp") * lax.axis_size("expert")
    pairs = [(i, i ^ (odd if i & CORE else even)) for i in range(count)]
    return lax.ppermute(values, AXES, pairs)


def add(*parts):
    total = parts[0].astype(jnp.float32)
    for part in parts[1:]:
        total = total + part.astype(jnp.float32)
    return total.astype(jnp.bfloat16)


def together(*values):
    return lax.optimization_barrier(values)


def slots_of(expert_ids, placement):
    total = placement.shape[0]
    matches = expert_ids[:, :, None] == jnp.arange(total, dtype=jnp.int32)
    return jnp.sum(jnp.where(matches, placement, 0), axis=2)


def dot(a, b, dims=NN):
    return lax.dot_general(a, b, dims, preferred_element_type=jnp.float32)


def iota(shape, axis):
    return lax.broadcasted_iota(jnp.int32, shape, axis)


def ordered(pieces, tok_count):
    rows = []
    for quarter in range(4):
        for piece, group in zip(pieces, GROUPS):
            size = len(group) * tok_count
            rows.append(piece[quarter * size : (quarter + 1) * size])
    return jnp.concatenate(rows, axis=0)


def put_in_places(pick, rows, half, x_ref):
    experts, both = x_ref.shape[:2]
    places = both // 2
    rows = dot(pick, rows).astype(jnp.bfloat16)
    for e in range(experts):
        x_ref[e, half * places : (half + 1) * places] = rows[e * places : (e + 1) * places]


def route_kernel(tok_count, *refs):
    rows_refs, part_refs, (mine_ref, mine_t_ref, both_ref) = refs[:6], refs[6:12], refs[12:15]
    x_ref, put_ref, pick_ref, prob_ref = refs[16:]
    experts, both = x_ref.shape[:2]
    places = both // 2
    count = pick_ref.shape[2]

    @pl.when(pl.program_id(0) == 0)
    def _():
        row, col = iota((count, count), 0), iota((count, count), 1)
        block = lax.div(row, tok_count)
        before = ((col < row) & (lax.div(col, tok_count) == block)).astype(jnp.bfloat16)
        columns = mine_ref.shape[0]
        first = (lax.div(iota((count, columns), 0), tok_count) * CAP).astype(jnp.float32)
        spot = lax.rem(iota((count, experts * places), 1), places).astype(jnp.float32)
        spot_t = lax.rem(iota((experts * places, count), 0), places).astype(jnp.float32)
        for half in range(2):
            prob = ordered(part_refs[3 * half : 3 * half + 3], tok_count)
            taken = prob.astype(jnp.float32) > 0.0
            rank = dot(before, jnp.where(taken, 1.0, 0.0).astype(jnp.bfloat16))
            place = jnp.where(taken, rank + first, -1.0).astype(jnp.bfloat16)
            put = jnp.where(dot(place, mine_ref[...]) == spot, 1.0, 0.0)
            pick = dot(mine_t_ref[...], place, NT) == spot_t
            put_ref[half] = put.astype(jnp.bfloat16)
            pick_ref[half] = jnp.where(pick, 1.0, 0.0).astype(jnp.bfloat16)
            weight = jnp.sum(put * dot(prob, both_ref[...]), axis=0, keepdims=True)
            for i in range(experts):
                prob_ref[i, :, half * places : (half + 1) * places] = weight[
                    :, i * places : (i + 1) * places
                ]

    for half in range(2):
        rows = ordered(rows_refs[3 * half : 3 * half + 3], tok_count)
        put_in_places(pick_ref[half], rows, half, x_ref)


def up_kernel(x_ref, prob_ref, gate_ref, up_ref, g_ref, u_ref, h_ref, ht_ref, held_ref, sems):
    step = pl.program_id(0)
    hidden = gate_ref.shape[1]

    def copies(e):
        slot = lax.rem(e, 2)
        for j, source in enumerate((gate_ref, up_ref)):
            held = held_ref.at[slot, hidden * j : hidden * (j + 1)]
            yield pltpu.make_async_copy(source.at[e], held, sems.at[slot, j])

    @pl.when(step == 0)
    def _():
        for copy in copies(step):
            copy.start()

    @pl.when(step + 1 < pl.num_programs(0))
    def _():
        for copy in copies(step + 1):
            copy.start()

    for copy in copies(step):
        copy.wait()
    product = dot(held_ref[lax.rem(step, 2)], x_ref[0], NT)
    g, u = product[:hidden], product[hidden:]
    g_ref[0] = g
    u_ref[0] = u
    silu_v, _ = gated(g)
    scaled = silu_v * u * prob_ref[0]
    ht_ref[0] = scaled.astype(jnp.bfloat16)
    h_ref[0] = scaled.T.astype(jnp.bfloat16)


def place_kernel(own0, own1, other0, other1, pick_ref, x_ref, kept_ref):
    for half, pieces in enumerate(((own0, own1), (other0, other1))):
        rows = jnp.concatenate([pieces[0][...], pieces[1][...]], axis=0)
        put_in_places(pick_ref[half], rows, half, x_ref)
    kept_ref[...] = x_ref[...]


def slope_kernel(x_ref, put_ref, prob_ref, mine_ref, down_ref, g_ref, u_ref,
                 dg_ref, du_ref, dgt_ref, dut_ref, share_ref, shares_ref, terms_ref):
    e = pl.program_id(0)
    experts, both = shares_ref.shape
    places = both // 2
    _, hidden, width = down_ref.shape
    product = dot(
        down_ref[...].reshape(PAIR * hidden, width), x_ref[...].reshape(PAIR * both, width), NT
    )
    for i in range(PAIR):
        plain = product[hidden * i : hidden * (i + 1), both * i : both * (i + 1)]
        g, u = g_ref[i], u_ref[i]
        silu_v, slope = gated(g)
        shares_ref[pl.ds(PAIR * e + i, 1), :] = jnp.sum(silu_v * u * plain, axis=0, keepdims=True)
        scaled = plain * prob_ref[i]
        dg = scaled * u * slope
        du = scaled * silu_v
        dgt_ref[i] = dg.astype(jnp.bfloat16)
        dut_ref[i] = du.astype(jnp.bfloat16)
        dg_ref[i] = dg.T.astype(jnp.bfloat16)
        du_ref[i] = du.T.astype(jnp.bfloat16)

    @pl.when(e == pl.num_programs(0) - 1)
    def _():
        shares = shares_ref[...].T
        for half in range(2):
            for i in range(experts):
                share = shares[half * places : (half + 1) * places, i : i + 1]
                share = (share * mine_ref[i].astype(jnp.float32)).astype(jnp.bfloat16)
                terms_ref[i * places : (i + 1) * places] = share
            share_ref[half] = dot(put_ref[half], terms_ref[...]).astype(jnp.bfloat16)


def back_kernel(terms, steps, put_ref, *refs):
    lefts, rights = refs[:terms], refs[terms : 2 * terms]
    extra_ref = refs[2 * terms] if len(refs) > 2 * terms + 3 else None
    own_ref, other_ref, rows_ref = refs[-3:]
    experts, places = rights[0].shape[0], put_ref.shape[2] // rights[0].shape[0]

    @pl.when(pl.program_id(0) < steps)
    def _():
        for e in range(experts):
            rows = dot(lefts[0][e], rights[0][e])
            for left, right in zip(lefts[1:], rights[1:]):
                rows = rows + dot(left[e], right[e])
            rows = rows.astype(jnp.bfloat16)
            for half in range(2):
                rows_ref[half, e * places : (e + 1) * places] = rows[half * places : (half + 1) * places]
        own_ref[...] = dot(put_ref[0], rows_ref[0]).astype(jnp.bfloat16)
        other_ref[...] = dot(put_ref[1], rows_ref[1]).astype(jnp.bfloat16)

    if extra_ref is not None:

        @pl.when(pl.program_id(0) == steps)
        def _():
            columns = extra_ref.shape[2]
            own_ref[:, :columns] = extra_ref[0]
            other_ref[:, :columns] = extra_ref[1]


def grad_kernel(x_ref, left, *outs):
    hidden = outs[0].shape[1]
    for at in range(0, x_ref.shape[2], WIDE):
        product = dot(left[0], x_ref[0, :, at : at + WIDE]).astype(jnp.bfloat16)
        for i, out in enumerate(outs):
            out[0, :, at : at + WIDE] = product[hidden * i : hidden * (i + 1)]


def whole(a):
    shape = a.shape
    return pl.BlockSpec(shape, lambda i: (0,) * len(shape), pipeline_mode=pl.Buffered(1))


def kept(a):
    shape = a.shape
    return pl.BlockSpec(shape, lambda i: (0,) * len(shape))


def each(a, size=1):
    shape = a.shape
    return pl.BlockSpec((size, *shape[1:]), lambda i: (i,) + (0,) * (len(shape) - 1))


def near_core(a):
    return pltpu.with_memory_space_constraint(a, pltpu.VMEM)


def in_hbm(a):
    return pltpu.with_memory_space_constraint(a, pltpu.HBM)


def bf16(*shape):
    return jax.ShapeDtypeStruct(shape, jnp.bfloat16)


def f32(*shape):
    return jax.ShapeDtypeStruct(shape, jnp.float32)


def call(kernel, grid, ins, args, outs, shapes, scratch=(), flops=0):
    moved = sum(math.prod(a.shape) * a.dtype.itemsize for a in (*args, *shapes))
    return pl.pallas_call(
        kernel,
        grid=(grid,),
        in_specs=ins,
        out_specs=outs,
        out_shape=shapes,
        scratch_shapes=scratch,
        compiler_params=pltpu.CompilerParams(vmem_limit_bytes=14 * MIB),
        cost_estimate=pl.CostEstimate(flops=flops, bytes_accessed=moved, transcendentals=0),
    )(*args)


def fetch_kernel(source, after, held, mark, sem):
    copy = pltpu.make_async_copy(source, held, sem)
    copy.start()
    mark[...] = jnp.zeros_like(mark)
    copy.wait()


def fetch_call(weight, after):
    return pl.pallas_call(
        fetch_kernel,
        in_specs=[pl.BlockSpec(memory_space=pl.ANY)] * 2,
        out_specs=[pl.BlockSpec(memory_space=pl.ANY), pl.BlockSpec(memory_space=pltpu.VMEM)],
        out_shape=[pltpu.VMEM(weight.shape, weight.dtype), f32(8, 128)],
        scratch_shapes=[pltpu.SemaphoreType.DMA],
        compiler_params=pltpu.CompilerParams(vmem_limit_bytes=MIB),
        cost_estimate=pl.CostEstimate(
            flops=0, bytes_accessed=weight.size * weight.dtype.itemsize, transcendentals=0
        ),
    )(in_hbm(weight), after)


def route_call(own, other, maps, mark, experts, width, tok_count):
    count = sum(piece.shape[0] for piece in own)
    places = count // tok_count * CAP
    columns = own[0].shape[1] - width
    pieces = (*own, *other)
    shapes = [
        pltpu.VMEM((experts, 2 * places, width), jnp.bfloat16),
        bf16(2, count, experts * places),
        bf16(2, experts * places, count),
        f32(experts, 1, 2 * places),
    ]
    ins = [pl.BlockSpec((piece.shape[0], WIDE), lambda i: (0, i)) for piece in pieces]
    ins += [pl.BlockSpec((piece.shape[0], columns), lambda i: (0, width // columns)) for piece in pieces]
    ins += [whole(a) for a in (*maps, mark)]
    outs = [pl.BlockSpec((experts, 2 * places, WIDE), lambda i: (0, 0, i))]
    outs += [kept(s) for s in shapes[1:]]
    flops = 4 * experts * places * count * width
    kernel = functools.partial(route_kernel, tok_count)
    return call(kernel, width // WIDE, ins, (*pieces, *pieces, *maps, mark), outs, shapes, flops=flops)


def up_call(x, prob, w_gate, w_up):
    experts, hidden, width = w_gate.shape
    rows = x.shape[1]
    args = (near_core(x), prob, near_core(w_gate), near_core(w_up))
    shapes = [
        f32(experts, hidden, rows),
        f32(experts, hidden, rows),
        bf16(experts, rows, hidden),
        bf16(experts, hidden, rows),
    ]
    ins = [each(x), each(prob)] + [pl.BlockSpec(memory_space=pl.ANY)] * 2
    outs = [each(s) for s in shapes]
    scratch = [
        pltpu.VMEM((2, 2 * hidden, width), jnp.bfloat16),
        pltpu.SemaphoreType.DMA((2, 2)),
    ]
    flops = 4 * experts * rows * hidden * width
    return call(up_kernel, experts, ins, args, outs, shapes, scratch, flops)


def place_call(pieces, pick, experts):
    _, rows, count = pick.shape
    size, width = pieces[0].shape
    shape = (experts, 2 * rows // experts, width)
    shapes = [pltpu.VMEM(shape, jnp.bfloat16), pltpu.HBM(shape, jnp.bfloat16)]
    ins = [pl.BlockSpec((size, WIDE), lambda i: (0, i))] * len(pieces) + [whole(pick)]
    outs = [pl.BlockSpec((*shape[:2], WIDE), lambda i: (0, 0, i))] * 2
    flops = 4 * rows * count * width
    return call(place_kernel, width // WIDE, ins, (*pieces, pick), outs, shapes, flops=flops)


def slope_call(x, put, prob, mine, w_down, g, u):
    experts, hidden, width = w_down.shape
    rows, count, columns = x.shape[1], put.shape[1], mine.shape[2]
    args = (near_core(x), put, prob, mine, in_hbm(w_down), g, u)
    shapes = [
        bf16(experts, rows, hidden),
        bf16(experts, rows, hidden),
        bf16(experts, hidden, rows),
        bf16(experts, hidden, rows),
        bf16(2, count, columns),
    ]
    ins = [each(x, PAIR), whole(put), each(prob, PAIR), whole(mine)]
    ins += [each(a, PAIR) for a in (w_down, g, u)]
    outs = [each(s, PAIR) for s in shapes[:4]] + [kept(shapes[4])]
    scratch = [
        pltpu.VMEM((experts, rows), jnp.float32),
        pltpu.VMEM((put.shape[2], columns), jnp.bfloat16),
    ]
    flops = 2 * experts * rows * hidden * width
    return call(slope_kernel, experts // PAIR, ins, args, outs, shapes, scratch, flops)


def back_call(put, lefts, rights, start, stop, extra=None):
    experts, hidden, _ = rights[0].shape
    rows = lefts[0].shape[1]
    count = put.shape[1]
    terms = len(lefts)
    steps = (stop - start) // CHUNK
    columns = stop - start + (0 if extra is None else extra.shape[2])
    args = (put, *lefts, *rights) + (() if extra is None else (extra,))
    shapes = [bf16(count, columns)] * 2
    ins = [whole(put)] + [whole(a) for a in lefts]
    first, last = start // CHUNK, stop // CHUNK - 1
    ins += [
        pl.BlockSpec((experts, hidden, CHUNK), lambda i: (0, 0, jnp.minimum(first + i, last)))
    ] * terms
    ins += [] if extra is None else [whole(extra)]
    outs = [pl.BlockSpec((count, CHUNK), lambda i: (0, i))] * 2
    scratch = [
        pltpu.VMEM((2, put.shape[2], CHUNK), jnp.bfloat16),
    ]
    flops = 2 * experts * rows * (stop - start) * (hidden * terms + count)
    kernel = functools.partial(back_kernel, terms, steps)
    grid = steps + (0 if extra is None else 1)
    return call(kernel, grid, ins, args, outs, shapes, scratch, flops)


def grad_call(x, left, hidden):
    experts, rows, width = x.shape
    shapes = [bf16(experts, hidden, width)] * (left.shape[1] // hidden)
    flops = 2 * experts * rows * left.shape[1] * width
    ins, outs = [each(x), each(left)], [each(s) for s in shapes]
    return call(grad_kernel, experts, ins, (x, left), outs, shapes, flops=flops)


def dense_body(
    tokens, cotangent, gate_prob, expert_ids, placement, gate_weight, up_weight, down_weight
):
    tok_count, width = tokens.shape
    local, hidden, _ = gate_weight.shape
    total_experts = placement.shape[0]
    devices = lax.axis_size("dp") * lax.axis_size("expert")
    places = devices // 2 * CAP
    count = devices // 2 * tok_count
    quarter, middle = count // 4, width // 2

    slots = slots_of(expert_ids, placement)
    used = slots[:, :, None] == jnp.arange(total_experts, dtype=jnp.int32)
    prob = jnp.sum(jnp.where(used, gate_prob[:, :, None], 0.0), axis=1)
    high = lax.reduce_precision(prob, 8, 7)
    parts = jnp.concatenate([high.astype(jnp.bfloat16), (prob - high).astype(jnp.bfloat16)], axis=1)

    slot = lax.axis_index("expert") * local + jnp.arange(local * places, dtype=jnp.int32) // places
    spots = jnp.arange(2 * total_experts, dtype=jnp.int32)
    mine = (slot[:, None] == spots[None, :]).astype(jnp.bfloat16)
    both = (slot[None, :] == spots[:, None] % total_experts).astype(jnp.bfloat16)
    maps = ((slot[None, :] == spots[:, None]).astype(jnp.bfloat16), mine, both)

    def rows_of(*blocks):
        return jnp.concatenate(blocks)

    def wide(values, extra):
        return jnp.concatenate([values, extra], axis=1)

    near, far = swap(tokens, Z1), swap(tokens, Z2)
    near_parts, far_parts = swap(parts, Z1), swap(parts, Z2)
    zero = wide(tokens, parts)
    first0 = swap(zero, X, Y)
    near, far = together(near, far)

    last, last_parts = swap(far, Z1), swap(far_parts, Z1)
    middle_rows = wide(rows_of(near, far), rows_of(near_parts, far_parts))
    first1 = swap(middle_rows, X, Y)
    zero = rows_of(zero, first0)
    second0 = swap(zero, Y, X)
    cotangent, last_parts = together(cotangent, last_parts)
    grads = [swap(cotangent, bit) for bit in (Z1, Z2, Z3)]
    last, last_parts, first1, second0, gate_weight = together(
        last, last_parts, first1, second0, gate_weight
    )
    gate_weight, mark = fetch_call(gate_weight, gate_prob)

    last = wide(last, last_parts)
    first2 = swap(last, X, Y)
    middle_rows = rows_of(middle_rows, first1)
    second1 = swap(middle_rows, Y, X)
    zero = rows_of(zero, second0)
    zero_other = swap(zero, CORE)
    first2, second1, cotangent, mark, up_weight = together(
        first2, second1, cotangent, mark, up_weight
    )
    up_weight, mark = fetch_call(up_weight, mark)

    last = rows_of(last, first2)
    second2 = swap(last, Y, X)
    second2, mark = together(second2, mark)
    middle_rows = rows_of(middle_rows, second1)
    middle_other = swap(middle_rows, CORE)
    grads = rows_of(cotangent, *grads)
    grads = rows_of(grads, swap(grads, X, Y))
    last = rows_of(last, second2)
    last_other = swap(last, CORE)
    x, put, pick, prob_rows = route_call(
        (zero, middle_rows, last),
        (zero_other, middle_other, last_other),
        maps,
        mark,
        local,
        width,
        tok_count,
    )
    x, grads = together(x, grads)
    far_grads = swap(grads, Y, X)
    grads_other = swap(grads, CORE)

    g, u, h, ht = up_call(x, prob_rows, gate_weight, up_weight)
    h, far_grads, grads_other = together(h, far_grads, grads_other)
    far_grads_other = swap(far_grads, CORE)
    mixed, mixed_other = back_call(put, [h], [in_hbm(down_weight)], 0, width)
    mixed_other, far_grads_other = together(mixed_other, far_grads_other)
    mixed = [mixed, swap(mixed_other, CORE)]

    near_c, c = place_call((grads, far_grads, grads_other, far_grads_other), pick, local)

    def leaving(parts, start, stop):
        return add(*(part[start:stop] for part in parts))

    def by_second(parts):
        return parts + [swap(leaving(parts, 2 * quarter, 4 * quarter), Y, X)]

    def by_first(parts):
        return parts + [swap(leaving(parts, quarter, 2 * quarter), X, Y)]

    def by_far(parts):
        return parts + [swap(leaving(parts, 2 * tok_count, 4 * tok_count), Z2)]

    def by_near(parts):
        return parts + [swap(leaving(parts, tok_count, 2 * tok_count), Z1)]

    weights = [near_core(gate_weight), near_core(up_weight)]
    mixed[1], far_c = together(mixed[1], c)
    rows, g = together(leaving(mixed, 2 * quarter, 4 * quarter), g)
    mixed.append(swap(rows, Y, X))
    dg, du, dgt, dut, share = slope_call(
        near_c, put, prob_rows, mine.reshape(local, places, -1), down_weight, g, u
    )
    left, left_other = back_call(put, [dg, du], weights, 0, middle)
    left = [left, swap(left_other, CORE)]
    left[0], mixed[2], dg, du = together(left[0], mixed[2], dg, du)
    mixed = by_first(mixed)
    right, right_other = back_call(put, [dg, du], weights, middle, width, share)
    right = [right, swap(right_other, CORE)]

    right[0], left[1], mixed[3] = together(right[0], left[1], mixed[3])
    rows, ht = together(leaving(left, 2 * quarter, 4 * quarter), ht)
    left.append(swap(rows, Y, X))
    mixed = by_far(mixed)
    (down_weight_grad,) = grad_call(far_c, ht, hidden)

    right[1], mixed[4], down_weight_grad = together(right[1], mixed[4], down_weight_grad)
    rows, dgt = together(leaving(right, 2 * quarter, 4 * quarter), dgt)
    right.append(swap(rows, Y, X))
    mixed = by_near(mixed)
    (gate_weight_grad,) = grad_call(x, dgt, hidden)

    def joined(parts, start, stop):
        halves = [
            sum(part[start:stop].astype(jnp.float32) for part in half) for half in (left, right)
        ]
        total = jnp.concatenate(halves, axis=1)
        return sum((part[start:stop].astype(jnp.float32) for part in parts), total)

    def sent(parts, start, stop):
        return joined(parts, start, stop).astype(jnp.bfloat16)

    right[2], left[2], gate_weight_grad = together(right[2], left[2], gate_weight_grad)
    rows, dut = together(sent([], quarter, 2 * quarter), dut)
    parts = [swap(rows, X, Y)]
    (up_weight_grad,) = grad_call(x, dut, hidden)

    parts[0], mixed[5], up_weight_grad = together(parts[0], mixed[5], up_weight_grad)
    parts.append(swap(sent(parts, 2 * tok_count, 4 * tok_count), Z2))
    mixed = leaving(mixed, 0, tok_count)
    parts.append(swap(sent(parts, tok_count, 2 * tok_count), Z1))
    total = sent(parts, 0, tok_count)
    token_grad = total[:, :width]
    share = total[:, width : width + total_experts].astype(jnp.float32)
    gate_grad = jnp.sum(jnp.where(used, share[:, None, :], 0.0), axis=2)
    return (mixed, token_grad, gate_grad, gate_weight_grad, up_weight_grad, down_weight_grad)


def routed_body(tokens, cotangent, gate_prob, expert_ids, placement, gate_weight, up_weight, down_weight):
    tok_count, model_width = tokens.shape
    top_count = expert_ids.shape[1]
    expert_devs = lax.axis_size("expert")
    local_experts = gate_weight.shape[0]
    total_experts = placement.shape[0]
    capacity = CAP
    flat_ids = expert_ids.reshape(-1)
    matches_id = flat_ids[:, None] == jnp.arange(total_experts, dtype=jnp.int32)[None, :]
    slot_ids = jnp.sum(jnp.where(matches_id, placement[None, :], 0), axis=1)
    pair_order = jnp.arange(flat_ids.shape[0], dtype=jnp.int32)
    earlier = (slot_ids[:, None] == slot_ids[None, :]) & (pair_order[None, :] < pair_order[:, None])
    position = slot_ids * capacity + jnp.sum(earlier.astype(jnp.int32), axis=1)
    matches = jnp.arange(total_experts * capacity, dtype=jnp.int32)[:, None] == position[None, :]
    matches = matches.reshape(total_experts * capacity, tok_count, top_count)
    dispatch = jnp.any(matches, axis=2).astype(jnp.bfloat16)
    weight_map = jnp.sum(jnp.where(matches, gate_prob[None, :, :], 0.0), axis=2)
    sent_rows = jnp.dot(dispatch, tokens, preferred_element_type=jnp.float32).astype(jnp.bfloat16)
    sent_grads = jnp.dot(
        weight_map, cotangent.astype(jnp.float32), precision=lax.Precision.HIGHEST
    ).astype(jnp.bfloat16)
    block_shape = (1, expert_devs, local_experts, capacity, model_width)
    sent_rows = sent_rows.reshape(block_shape)
    sent_grads = sent_grads.reshape(block_shape)
    got_rows, got_grads = (
        lax.all_to_all(sent_rows, "expert", split_axis=1, concat_axis=1, tiled=True),
        lax.all_to_all(sent_grads, "expert", split_axis=1, concat_axis=1, tiled=True),
    )
    routed, routed_grads = (
        lax.all_gather(got_rows, "dp", axis=0, tiled=True),
        lax.all_gather(got_grads, "dp", axis=0, tiled=True),
    )
    gate_pre = jnp.einsum(
        "asjcd,jfd->asjcf", routed, gate_weight, preferred_element_type=jnp.float32
    )
    up_pre = jnp.einsum("asjcd,jfd->asjcf", routed, up_weight, preferred_element_type=jnp.float32)
    silu_v, slope = gated(gate_pre)
    hidden = (silu_v * up_pre).astype(jnp.bfloat16)
    out_part = jnp.einsum(
        "asjcf,jfd->asjcd", hidden, down_weight, preferred_element_type=jnp.float32
    )
    d_hidden = jnp.einsum(
        "asjcd,jfd->asjcf", routed_grads, down_weight, preferred_element_type=jnp.float32
    )
    d_gate_pre = (d_hidden * up_pre * slope).astype(jnp.bfloat16)
    d_up_pre = (d_hidden * silu_v).astype(jnp.bfloat16)
    back_part = jnp.einsum(
        "asjcf,jfd->asjcd", d_gate_pre, gate_weight, preferred_element_type=jnp.float32
    )
    back_part = back_part + jnp.einsum(
        "asjcf,jfd->asjcd", d_up_pre, up_weight, preferred_element_type=jnp.float32
    )
    down_grad = jnp.einsum(
        "asjcf,asjcd->jfd", hidden, routed_grads, preferred_element_type=jnp.float32
    ).astype(jnp.bfloat16)
    gate_grad_w = jnp.einsum(
        "asjcf,asjcd->jfd", d_gate_pre, routed, preferred_element_type=jnp.float32
    ).astype(jnp.bfloat16)
    up_grad_w = jnp.einsum(
        "asjcf,asjcd->jfd", d_up_pre, routed, preferred_element_type=jnp.float32
    ).astype(jnp.bfloat16)
    summed = (
        lax.psum_scatter(
            out_part.astype(jnp.bfloat16), "dp", scatter_dimension=0, tiled=True
        ).astype(jnp.float32),
        lax.psum_scatter(
            back_part.astype(jnp.bfloat16), "dp", scatter_dimension=0, tiled=True
        ).astype(jnp.float32),
    )
    back_out, back_grad = (
        lax.all_to_all(
            summed[0].astype(jnp.bfloat16), "expert", split_axis=1, concat_axis=1, tiled=True
        ),
        lax.all_to_all(
            summed[1].astype(jnp.bfloat16), "expert", split_axis=1, concat_axis=1, tiled=True
        ),
    )
    out_flat = back_out.reshape(total_experts * capacity, model_width)
    grad_flat = back_grad.reshape(total_experts * capacity, model_width)
    chosen_out = out_flat[position].reshape(tok_count, top_count, model_width)
    chosen_grad = grad_flat[position].reshape(tok_count, top_count, model_width)
    mixed = jnp.einsum(
        "tk,tkd->td", gate_prob, chosen_out.astype(jnp.float32), precision=lax.Precision.HIGHEST
    ).astype(jnp.bfloat16)
    gate_grad = jnp.einsum("td,tkd->tk", cotangent, chosen_out, preferred_element_type=jnp.float32)
    token_grad = jnp.sum(chosen_grad.astype(jnp.float32), axis=1).astype(jnp.bfloat16)
    return (mixed, token_grad, gate_grad, gate_grad_w, up_grad_w, down_grad)


def body(*args):
    tokens, gate_weight = args[0], args[5]
    mesh_fits = (lax.axis_size("dp"), lax.axis_size("expert")) == (4, 8)
    if mesh_fits and tokens.shape[0] <= gate_weight.shape[0] * CAP:
        return dense_body(*args)
    return routed_body(*args)


def solution(mesh):
    return jax.shard_map(
        body,
        mesh=mesh,
        in_specs=(
            P(("dp", "expert"), None),
            P(("dp", "expert"), None),
            P(("dp", "expert"), None),
            P(("dp", "expert"), None),
            P(),
            P("expert", "dp", None),
            P("expert", "dp", None),
            P("expert", "dp", None),
        ),
        out_specs=(
            P(("dp", "expert"), None),
            P(("dp", "expert"), None),
            P(("dp", "expert"), None),
            P("expert", "dp", None),
            P("expert", "dp", None),
            P("expert", "dp", None),
        ),
        check_vma=False,
    )
```

```python
import functools
import math

import jax
import jax.numpy as jnp
from jax import lax
from jax.experimental import pallas as pl
from jax.experimental.pallas import tpu as pltpu
from jax.sharding import PartitionSpec as P

CAP = 3
AXES = ("dp", "expert")
CORE, Z1, Z2, Z3, X, Y = 1, 2, 4, 6, 8, 16
GROUPS = ((0,), (1, 2), (3,))
CHUNK = 512
WIDE = 1024
PAIR = 2
MIB = 1 << 20

NT = (((1,), (1,)), ((), ()))
NN = (((1,), (0,)), ((), ()))


def gated(values):
    sigmoid_v = jax.nn.sigmoid(values)
    return (values * sigmoid_v, sigmoid_v * (1.0 + values * (1.0 - sigmoid_v)))


def swap(values, even, odd=None):
    odd = even if odd is None else odd
    count = lax.axis_size("dp") * lax.axis_size("expert")
    pairs = [(i, i ^ (odd if i & CORE else even)) for i in range(count)]
    return lax.ppermute(values, AXES, pairs)


def add(*parts):
    total = parts[0].astype(jnp.float32)
    for part in parts[1:]:
        total = total + part.astype(jnp.float32)
    return total.astype(jnp.bfloat16)


def together(*values):
    return lax.optimization_barrier(values)


def slots_of(expert_ids, placement):
    total = placement.shape[0]
    matches = expert_ids[:, :, None] == jnp.arange(total, dtype=jnp.int32)
    return jnp.sum(jnp.where(matches, placement, 0), axis=2)


def dot(a, b, dims=NN):
    return lax.dot_general(a, b, dims, preferred_element_type=jnp.float32)


def iota(shape, axis):
    return lax.broadcasted_iota(jnp.int32, shape, axis)


def ordered(pieces, tok_count):
    rows = []
    for quarter in range(4):
        for piece, group in zip(pieces, GROUPS):
            size = len(group) * tok_count
            rows.append(piece[quarter * size : (quarter + 1) * size])
    return jnp.concatenate(rows, axis=0)


def put_in_places(pick, rows, half, x_ref):
    experts, both = x_ref.shape[:2]
    places = both // 2
    rows = dot(pick, rows).astype(jnp.bfloat16)
    for e in range(experts):
        x_ref[e, half * places : (half + 1) * places] = rows[e * places : (e + 1) * places]


def route_kernel(tok_count, *refs):
    rows_refs, part_refs, (mine_ref, mine_t_ref, both_ref) = refs[:6], refs[6:8], refs[8:11]
    x_ref, put_ref, pick_ref, prob_ref = refs[12:]
    experts, both = x_ref.shape[:2]
    places = both // 2
    count = pick_ref.shape[2]

    @pl.when(pl.program_id(0) == 0)
    def _():
        row, col = iota((count, count), 0), iota((count, count), 1)
        block = lax.div(row, tok_count)
        before = ((col < row) & (lax.div(col, tok_count) == block)).astype(jnp.bfloat16)
        columns = mine_ref.shape[0]
        first = (lax.div(iota((count, columns), 0), tok_count) * CAP).astype(jnp.float32)
        spot = lax.rem(iota((count, experts * places), 1), places).astype(jnp.float32)
        spot_t = lax.rem(iota((experts * places, count), 0), places).astype(jnp.float32)
        for half in range(2):
            prob = part_refs[half][...]
            taken = prob.astype(jnp.float32) > 0.0
            rank = dot(before, jnp.where(taken, 1.0, 0.0).astype(jnp.bfloat16))
            place = jnp.where(taken, rank + first, -1.0).astype(jnp.bfloat16)
            put = jnp.where(dot(place, mine_ref[...]) == spot, 1.0, 0.0)
            pick = dot(mine_t_ref[...], place, NT) == spot_t
            put_ref[half] = put.astype(jnp.bfloat16)
            pick_ref[half] = jnp.where(pick, 1.0, 0.0).astype(jnp.bfloat16)
            weight = jnp.sum(put * dot(prob, both_ref[...]), axis=0, keepdims=True)
            for i in range(experts):
                prob_ref[i, :, half * places : (half + 1) * places] = weight[
                    :, i * places : (i + 1) * places
                ]

    for half in range(2):
        rows = ordered(rows_refs[3 * half : 3 * half + 3], tok_count)
        put_in_places(pick_ref[half], rows, half, x_ref)


def up_kernel(x_ref, prob_ref, gate_ref, up_ref, g_ref, u_ref, h_ref, ht_ref, held_ref, sems):
    step = pl.program_id(0)
    hidden = gate_ref.shape[1]

    def copies(e):
        slot = lax.rem(e, 2)
        for j, source in enumerate((gate_ref, up_ref)):
            held = held_ref.at[slot, hidden * j : hidden * (j + 1)]
            yield pltpu.make_async_copy(source.at[e], held, sems.at[slot, j])

    @pl.when(step == 0)
    def _():
        for copy in copies(step):
            copy.start()

    @pl.when(step + 1 < pl.num_programs(0))
    def _():
        for copy in copies(step + 1):
            copy.start()

    for copy in copies(step):
        copy.wait()
    product = dot(held_ref[lax.rem(step, 2)], x_ref[0], NT)
    g, u = product[:hidden], product[hidden:]
    g_ref[0] = g
    u_ref[0] = u
    silu_v, _ = gated(g)
    scaled = silu_v * u * prob_ref[0]
    ht_ref[0] = scaled.astype(jnp.bfloat16)
    h_ref[0] = scaled.T.astype(jnp.bfloat16)


def place_kernel(own0, own1, other0, other1, pick_ref, x_ref, kept_ref):
    for half, pieces in enumerate(((own0, own1), (other0, other1))):
        rows = jnp.concatenate([pieces[0][...], pieces[1][...]], axis=0)
        put_in_places(pick_ref[half], rows, half, x_ref)
    kept_ref[...] = x_ref[...]


def slope_kernel(x_ref, put_ref, prob_ref, mine_ref, down_ref, g_ref, u_ref,
                 dg_ref, du_ref, dgt_ref, dut_ref, share_ref, shares_ref, terms_ref):
    e = pl.program_id(0)
    experts, both = shares_ref.shape
    places = both // 2
    _, hidden, width = down_ref.shape
    product = dot(
        down_ref[...].reshape(PAIR * hidden, width), x_ref[...].reshape(PAIR * both, width), NT
    )
    for i in range(PAIR):
        plain = product[hidden * i : hidden * (i + 1), both * i : both * (i + 1)]
        g, u = g_ref[i], u_ref[i]
        silu_v, slope = gated(g)
        shares_ref[pl.ds(PAIR * e + i, 1), :] = jnp.sum(silu_v * u * plain, axis=0, keepdims=True)
        scaled = plain * prob_ref[i]
        dg = scaled * u * slope
        du = scaled * silu_v
        dgt_ref[i] = dg.astype(jnp.bfloat16)
        dut_ref[i] = du.astype(jnp.bfloat16)
        dg_ref[i] = dg.T.astype(jnp.bfloat16)
        du_ref[i] = du.T.astype(jnp.bfloat16)

    @pl.when(e == pl.num_programs(0) - 1)
    def _():
        shares = shares_ref[...].T
        for half in range(2):
            for i in range(experts):
                share = shares[half * places : (half + 1) * places, i : i + 1]
                share = (share * mine_ref[i].astype(jnp.float32)).astype(jnp.bfloat16)
                terms_ref[i * places : (i + 1) * places] = share
            share_ref[half] = dot(put_ref[half], terms_ref[...]).astype(jnp.bfloat16)


def back_kernel(terms, steps, put_ref, *refs):
    lefts, rights = refs[:terms], refs[terms : 2 * terms]
    extra_ref = refs[2 * terms] if len(refs) > 2 * terms + 3 else None
    own_ref, other_ref, rows_ref = refs[-3:]
    experts, places = rights[0].shape[0], put_ref.shape[2] // rights[0].shape[0]

    @pl.when(pl.program_id(0) < steps)
    def _():
        for e in range(experts):
            rows = dot(lefts[0][e], rights[0][e])
            for left, right in zip(lefts[1:], rights[1:]):
                rows = rows + dot(left[e], right[e])
            rows = rows.astype(jnp.bfloat16)
            for half in range(2):
                rows_ref[half, e * places : (e + 1) * places] = rows[half * places : (half + 1) * places]
        own_ref[...] = dot(put_ref[0], rows_ref[0]).astype(jnp.bfloat16)
        other_ref[...] = dot(put_ref[1], rows_ref[1]).astype(jnp.bfloat16)

    if extra_ref is not None:

        @pl.when(pl.program_id(0) == steps)
        def _():
            columns = extra_ref.shape[2]
            own_ref[:, :columns] = extra_ref[0]
            other_ref[:, :columns] = extra_ref[1]


def grad_kernel(x_ref, left, *outs):
    hidden = outs[0].shape[1]
    for at in range(0, x_ref.shape[2], WIDE):
        product = dot(left[0], x_ref[0, :, at : at + WIDE]).astype(jnp.bfloat16)
        for i, out in enumerate(outs):
            out[0, :, at : at + WIDE] = product[hidden * i : hidden * (i + 1)]


def whole(a):
    shape = a.shape
    return pl.BlockSpec(shape, lambda i: (0,) * len(shape), pipeline_mode=pl.Buffered(1))


def kept(a):
    shape = a.shape
    return pl.BlockSpec(shape, lambda i: (0,) * len(shape))


def each(a, size=1):
    shape = a.shape
    return pl.BlockSpec((size, *shape[1:]), lambda i: (i,) + (0,) * (len(shape) - 1))


def near_core(a):
    return pltpu.with_memory_space_constraint(a, pltpu.VMEM)


def in_hbm(a):
    return pltpu.with_memory_space_constraint(a, pltpu.HBM)


def bf16(*shape):
    return jax.ShapeDtypeStruct(shape, jnp.bfloat16)


def f32(*shape):
    return jax.ShapeDtypeStruct(shape, jnp.float32)


def call(kernel, grid, ins, args, outs, shapes, scratch=(), flops=0):
    moved = sum(math.prod(a.shape) * a.dtype.itemsize for a in (*args, *shapes))
    return pl.pallas_call(
        kernel,
        grid=(grid,),
        in_specs=ins,
        out_specs=outs,
        out_shape=shapes,
        scratch_shapes=scratch,
        compiler_params=pltpu.CompilerParams(vmem_limit_bytes=14 * MIB),
        cost_estimate=pl.CostEstimate(flops=flops, bytes_accessed=moved, transcendentals=0),
    )(*args)


def fetch_kernel(source, after, held, mark, sem):
    copy = pltpu.make_async_copy(source, held, sem)
    copy.start()
    mark[...] = jnp.zeros_like(mark)
    copy.wait()


def fetch_call(weight, after):
    return pl.pallas_call(
        fetch_kernel,
        in_specs=[pl.BlockSpec(memory_space=pl.ANY)] * 2,
        out_specs=[pl.BlockSpec(memory_space=pl.ANY), pl.BlockSpec(memory_space=pltpu.VMEM)],
        out_shape=[pltpu.VMEM(weight.shape, weight.dtype), f32(8, 128)],
        scratch_shapes=[pltpu.SemaphoreType.DMA],
        compiler_params=pltpu.CompilerParams(vmem_limit_bytes=MIB),
        cost_estimate=pl.CostEstimate(
            flops=0, bytes_accessed=weight.size * weight.dtype.itemsize, transcendentals=0
        ),
    )(in_hbm(weight), after)


def route_call(own, other, parts, maps, mark, experts, tok_count):
    count = sum(piece.shape[0] for piece in own)
    places = count // tok_count * CAP
    width = own[0].shape[1]
    pieces = (*own, *other)
    shapes = [
        pltpu.VMEM((experts, 2 * places, width), jnp.bfloat16),
        bf16(2, count, experts * places),
        bf16(2, experts * places, count),
        f32(experts, 1, 2 * places),
    ]
    ins = [pl.BlockSpec((piece.shape[0], WIDE), lambda i: (0, i)) for piece in pieces]
    ins += [whole(a) for a in (*parts, *maps, mark)]
    outs = [pl.BlockSpec((experts, 2 * places, WIDE), lambda i: (0, 0, i))]
    outs += [kept(s) for s in shapes[1:]]
    flops = 4 * experts * places * count * width
    kernel = functools.partial(route_kernel, tok_count)
    return call(kernel, width // WIDE, ins, (*pieces, *parts, *maps, mark), outs, shapes, flops=flops)


def up_call(x, prob, w_gate, w_up):
    experts, hidden, width = w_gate.shape
    rows = x.shape[1]
    args = (near_core(x), prob, near_core(w_gate), near_core(w_up))
    shapes = [
        f32(experts, hidden, rows),
        f32(experts, hidden, rows),
        bf16(experts, rows, hidden),
        bf16(experts, hidden, rows),
    ]
    ins = [each(x), each(prob)] + [pl.BlockSpec(memory_space=pl.ANY)] * 2
    outs = [each(s) for s in shapes]
    scratch = [
        pltpu.VMEM((2, 2 * hidden, width), jnp.bfloat16),
        pltpu.SemaphoreType.DMA((2, 2)),
    ]
    flops = 4 * experts * rows * hidden * width
    return call(up_kernel, experts, ins, args, outs, shapes, scratch, flops)


def place_call(pieces, pick, experts):
    _, rows, count = pick.shape
    size, width = pieces[0].shape
    shape = (experts, 2 * rows // experts, width)
    shapes = [pltpu.VMEM(shape, jnp.bfloat16), pltpu.HBM(shape, jnp.bfloat16)]
    ins = [pl.BlockSpec((size, WIDE), lambda i: (0, i))] * len(pieces) + [whole(pick)]
    outs = [pl.BlockSpec((*shape[:2], WIDE), lambda i: (0, 0, i))] * 2
    flops = 4 * rows * count * width
    return call(place_kernel, width // WIDE, ins, (*pieces, pick), outs, shapes, flops=flops)


def slope_call(x, put, prob, mine, w_down, g, u):
    experts, hidden, width = w_down.shape
    rows, count, columns = x.shape[1], put.shape[1], mine.shape[2]
    args = (near_core(x), put, prob, mine, in_hbm(w_down), g, u)
    shapes = [
        bf16(experts, rows, hidden),
        bf16(experts, rows, hidden),
        bf16(experts, hidden, rows),
        bf16(experts, hidden, rows),
        bf16(2, count, columns),
    ]
    ins = [each(x, PAIR), whole(put), each(prob, PAIR), whole(mine)]
    ins += [each(a, PAIR) for a in (w_down, g, u)]
    outs = [each(s, PAIR) for s in shapes[:4]] + [kept(shapes[4])]
    scratch = [
        pltpu.VMEM((experts, rows), jnp.float32),
        pltpu.VMEM((put.shape[2], columns), jnp.bfloat16),
    ]
    flops = 2 * experts * rows * hidden * width
    return call(slope_kernel, experts // PAIR, ins, args, outs, shapes, scratch, flops)


def back_call(put, lefts, rights, start, stop, extra=None):
    experts, hidden, _ = rights[0].shape
    rows = lefts[0].shape[1]
    count = put.shape[1]
    terms = len(lefts)
    chunk = CHUNK * 2 // terms
    steps = (stop - start) // chunk
    columns = stop - start + (0 if extra is None else extra.shape[2])
    args = (put, *lefts, *rights) + (() if extra is None else (extra,))
    shapes = [bf16(count, columns)] * 2
    ins = [whole(put)] + [whole(a) for a in lefts]
    first, last = start // chunk, stop // chunk - 1
    ins += [
        pl.BlockSpec((experts, hidden, chunk), lambda i: (0, 0, jnp.minimum(first + i, last)))
    ] * terms
    ins += [] if extra is None else [whole(extra)]
    outs = [pl.BlockSpec((count, chunk), lambda i: (0, i))] * 2
    scratch = [
        pltpu.VMEM((2, put.shape[2], chunk), jnp.bfloat16),
    ]
    flops = 2 * experts * rows * (stop - start) * (hidden * terms + count)
    kernel = functools.partial(back_kernel, terms, steps)
    grid = steps + (0 if extra is None else 1)
    return call(kernel, grid, ins, args, outs, shapes, scratch, flops)


def grad_call(x, left, hidden):
    experts, rows, width = x.shape
    shapes = [bf16(experts, hidden, width)] * (left.shape[1] // hidden)
    flops = 2 * experts * rows * left.shape[1] * width
    ins, outs = [each(x), each(left)], [each(s) for s in shapes]
    return call(grad_kernel, experts, ins, (x, left), outs, shapes, flops=flops)


def dense_body(
    tokens, cotangent, gate_prob, expert_ids, placement, gate_weight, up_weight, down_weight
):
    tok_count, width = tokens.shape
    local, hidden, _ = gate_weight.shape
    total_experts = placement.shape[0]
    devices = lax.axis_size("dp") * lax.axis_size("expert")
    places = devices // 2 * CAP
    count = devices // 2 * tok_count
    quarter, middle = count // 4, width // 2

    slots = slots_of(expert_ids, placement)
    used = slots[:, :, None] == jnp.arange(total_experts, dtype=jnp.int32)
    prob = jnp.sum(jnp.where(used, gate_prob[:, :, None], 0.0), axis=1)
    high = lax.reduce_precision(prob, 8, 7)
    parts = jnp.concatenate([high.astype(jnp.bfloat16), (prob - high).astype(jnp.bfloat16)], axis=1)

    slot = lax.axis_index("expert") * local + jnp.arange(local * places, dtype=jnp.int32) // places
    spots = jnp.arange(2 * total_experts, dtype=jnp.int32)
    mine = (slot[:, None] == spots[None, :]).astype(jnp.bfloat16)
    both = (slot[None, :] == spots[:, None] % total_experts).astype(jnp.bfloat16)
    maps = ((slot[None, :] == spots[:, None]).astype(jnp.bfloat16), mine, both)

    def rows_of(*blocks):
        return jnp.concatenate(blocks)

    near, far = swap(tokens, Z1), swap(tokens, Z2)
    first0 = swap(tokens, X, Y)
    near, far = together(near, far)

    last = swap(far, Z1)
    middle_rows = rows_of(far, near)
    first1 = swap(middle_rows, X, Y)
    zero = rows_of(tokens, first0)
    second0 = swap(zero, Y, X)
    last, cotangent = together(last, cotangent)
    grads = [swap(cotangent, bit) for bit in (Z2, Z1, Z3)]
    last, first1, second0, gate_weight = together(last, first1, second0, gate_weight)
    gate_weight, mark = fetch_call(gate_weight, last)

    first2 = swap(last, X, Y)
    middle_rows = rows_of(middle_rows, first1)
    second1 = swap(middle_rows, Y, X)
    zero = rows_of(zero, second0)
    zero_other = swap(zero, CORE)
    first2, second1, cotangent, mark, up_weight = together(
        first2, second1, cotangent, mark, up_weight
    )
    up_weight, mark = fetch_call(up_weight, mark)

    parts = rows_of(parts, *(swap(parts, bit) for bit in (Z2, Z1, Z3)))
    parts = rows_of(parts, swap(parts, X, Y))
    parts = rows_of(parts, swap(parts, Y, X))
    parts = (parts, swap(parts, CORE))

    last = rows_of(last, first2)
    second2 = swap(last, Y, X)
    second2, mark = together(second2, mark)
    middle_rows = rows_of(middle_rows, second1)
    middle_other = swap(middle_rows, CORE)
    second2, cotangent = together(second2, cotangent)
    grads = rows_of(cotangent, *grads)
    grads = rows_of(grads, swap(grads, X, Y))
    last = rows_of(last, second2)
    last_other = swap(last, CORE)
    x, put, pick, prob_rows = route_call(
        (zero, middle_rows, last),
        (zero_other, middle_other, last_other),
        parts,
        maps,
        mark,
        local,
        tok_count,
    )
    x, grads = together(x, grads)
    far_grads = swap(grads, Y, X)
    grads_other = swap(grads, CORE)

    g, u, h, ht = up_call(x, prob_rows, gate_weight, up_weight)
    h, far_grads, grads_other = together(h, far_grads, grads_other)
    far_grads_other = swap(far_grads, CORE)
    mixed, mixed_other = back_call(put, [h], [in_hbm(down_weight)], 0, width)
    mixed_other, far_grads_other = together(mixed_other, far_grads_other)
    mixed = [mixed, swap(mixed_other, CORE)]

    near_c, c = place_call((grads, far_grads, grads_other, far_grads_other), pick, local)

    def leaving(parts, start, stop):
        return add(*(part[start:stop] for part in parts))

    def by_second(parts):
        return parts + [swap(leaving(parts, 2 * quarter, 4 * quarter), Y, X)]

    def by_first(parts):
        return parts + [swap(leaving(parts, quarter, 2 * quarter), X, Y)]

    def by_near(parts):
        return parts + [swap(leaving(parts, 2 * tok_count, 4 * tok_count), Z1)]

    def by_far(parts):
        return parts + [swap(leaving(parts, tok_count, 2 * tok_count), Z2)]

    weights = [near_core(gate_weight), near_core(up_weight)]
    mixed[1], far_c = together(mixed[1], c)
    rows, g = together(leaving(mixed, 2 * quarter, 4 * quarter), g)
    mixed.append(swap(rows, Y, X))
    dg, du, dgt, dut, share = slope_call(
        near_c, put, prob_rows, mine.reshape(local, places, -1), down_weight, g, u
    )
    left, left_other = back_call(put, [dg, du], weights, 0, middle)
    left = [left, swap(left_other, CORE)]
    left[0], mixed[2], dg, du = together(left[0], mixed[2], dg, du)
    mixed = by_first(mixed)
    right, right_other = back_call(put, [dg, du], weights, middle, width, share)
    right = [right, swap(right_other, CORE)]

    right[0], left[1] = together(right[0], left[1])
    rows, ht = together(leaving(left, 2 * quarter, 4 * quarter), ht)
    left.append(swap(rows, Y, X))
    (down_weight_grad,) = grad_call(far_c, ht, hidden)

    right[1], left[2], mixed[3], down_weight_grad = together(
        right[1], left[2], mixed[3], down_weight_grad
    )
    rows, left_rows, mixed_rows, dgt = together(
        leaving(right, 2 * quarter, 4 * quarter),
        leaving(left, quarter, 2 * quarter),
        leaving(mixed, 2 * tok_count, 4 * tok_count),
        dgt,
    )
    right.append(swap(rows, Y, X))
    left.append(swap(left_rows, X, Y))
    mixed.append(swap(mixed_rows, Z1))
    (gate_weight_grad,) = grad_call(x, dgt, hidden)

    right[2], left[3], mixed[4], gate_weight_grad = together(
        right[2], left[3], mixed[4], gate_weight_grad
    )
    rows, left_rows, mixed_rows, dut = together(
        leaving(right, quarter, 2 * quarter),
        leaving(left, 2 * tok_count, 4 * tok_count),
        leaving(mixed, tok_count, 2 * tok_count),
        dut,
    )
    right.append(swap(rows, X, Y))
    left.append(swap(left_rows, Z1))
    mixed.append(swap(mixed_rows, Z2))
    (up_weight_grad,) = grad_call(x, dut, hidden)

    right[3], left[4], up_weight_grad = together(right[3], left[4], up_weight_grad)
    right, left = by_near(right), by_far(left)
    right = by_far(right)
    mixed, left, right = (leaving(parts, 0, tok_count) for parts in (mixed, left, right))
    token_grad = jnp.concatenate([left, right[:, : width - middle]], axis=1)
    share = right[:, width - middle : width - middle + total_experts].astype(jnp.float32)
    gate_grad = jnp.sum(jnp.where(used, share[:, None, :], 0.0), axis=2)
    return (mixed, token_grad, gate_grad, gate_weight_grad, up_weight_grad, down_weight_grad)


def routed_body(tokens, cotangent, gate_prob, expert_ids, placement, gate_weight, up_weight, down_weight):
    tok_count, model_width = tokens.shape
    top_count = expert_ids.shape[1]
    expert_devs = lax.axis_size("expert")
    local_experts = gate_weight.shape[0]
    total_experts = placement.shape[0]
    capacity = CAP
    flat_ids = expert_ids.reshape(-1)
    matches_id = flat_ids[:, None] == jnp.arange(total_experts, dtype=jnp.int32)[None, :]
    slot_ids = jnp.sum(jnp.where(matches_id, placement[None, :], 0), axis=1)
    pair_order = jnp.arange(flat_ids.shape[0], dtype=jnp.int32)
    earlier = (slot_ids[:, None] == slot_ids[None, :]) & (pair_order[None, :] < pair_order[:, None])
    position = slot_ids * capacity + jnp.sum(earlier.astype(jnp.int32), axis=1)
    matches = jnp.arange(total_experts * capacity, dtype=jnp.int32)[:, None] == position[None, :]
    matches = matches.reshape(total_experts * capacity, tok_count, top_count)
    dispatch = jnp.any(matches, axis=2).astype(jnp.bfloat16)
    weight_map = jnp.sum(jnp.where(matches, gate_prob[None, :, :], 0.0), axis=2)
    sent_rows = jnp.dot(dispatch, tokens, preferred_element_type=jnp.float32).astype(jnp.bfloat16)
    sent_grads = jnp.dot(
        weight_map, cotangent.astype(jnp.float32), precision=lax.Precision.HIGHEST
    ).astype(jnp.bfloat16)
    block_shape = (1, expert_devs, local_experts, capacity, model_width)
    sent_rows = sent_rows.reshape(block_shape)
    sent_grads = sent_grads.reshape(block_shape)
    got_rows, got_grads = (
        lax.all_to_all(sent_rows, "expert", split_axis=1, concat_axis=1, tiled=True),
        lax.all_to_all(sent_grads, "expert", split_axis=1, concat_axis=1, tiled=True),
    )
    routed, routed_grads = (
        lax.all_gather(got_rows, "dp", axis=0, tiled=True),
        lax.all_gather(got_grads, "dp", axis=0, tiled=True),
    )
    gate_pre = jnp.einsum(
        "asjcd,jfd->asjcf", routed, gate_weight, preferred_element_type=jnp.float32
    )
    up_pre = jnp.einsum("asjcd,jfd->asjcf", routed, up_weight, preferred_element_type=jnp.float32)
    silu_v, slope = gated(gate_pre)
    hidden = (silu_v * up_pre).astype(jnp.bfloat16)
    out_part = jnp.einsum(
        "asjcf,jfd->asjcd", hidden, down_weight, preferred_element_type=jnp.float32
    )
    d_hidden = jnp.einsum(
        "asjcd,jfd->asjcf", routed_grads, down_weight, preferred_element_type=jnp.float32
    )
    d_gate_pre = (d_hidden * up_pre * slope).astype(jnp.bfloat16)
    d_up_pre = (d_hidden * silu_v).astype(jnp.bfloat16)
    back_part = jnp.einsum(
        "asjcf,jfd->asjcd", d_gate_pre, gate_weight, preferred_element_type=jnp.float32
    )
    back_part = back_part + jnp.einsum(
        "asjcf,jfd->asjcd", d_up_pre, up_weight, preferred_element_type=jnp.float32
    )
    down_grad = jnp.einsum(
        "asjcf,asjcd->jfd", hidden, routed_grads, preferred_element_type=jnp.float32
    ).astype(jnp.bfloat16)
    gate_grad_w = jnp.einsum(
        "asjcf,asjcd->jfd", d_gate_pre, routed, preferred_element_type=jnp.float32
    ).astype(jnp.bfloat16)
    up_grad_w = jnp.einsum(
        "asjcf,asjcd->jfd", d_up_pre, routed, preferred_element_type=jnp.float32
    ).astype(jnp.bfloat16)
    summed = (
        lax.psum_scatter(
            out_part.astype(jnp.bfloat16), "dp", scatter_dimension=0, tiled=True
        ).astype(jnp.float32),
        lax.psum_scatter(
            back_part.astype(jnp.bfloat16), "dp", scatter_dimension=0, tiled=True
        ).astype(jnp.float32),
    )
    back_out, back_grad = (
        lax.all_to_all(
            summed[0].astype(jnp.bfloat16), "expert", split_axis=1, concat_axis=1, tiled=True
        ),
        lax.all_to_all(
            summed[1].astype(jnp.bfloat16), "expert", split_axis=1, concat_axis=1, tiled=True
        ),
    )
    out_flat = back_out.reshape(total_experts * capacity, model_width)
    grad_flat = back_grad.reshape(total_experts * capacity, model_width)
    chosen_out = out_flat[position].reshape(tok_count, top_count, model_width)
    chosen_grad = grad_flat[position].reshape(tok_count, top_count, model_width)
    mixed = jnp.einsum(
        "tk,tkd->td", gate_prob, chosen_out.astype(jnp.float32), precision=lax.Precision.HIGHEST
    ).astype(jnp.bfloat16)
    gate_grad = jnp.einsum("td,tkd->tk", cotangent, chosen_out, preferred_element_type=jnp.float32)
    token_grad = jnp.sum(chosen_grad.astype(jnp.float32), axis=1).astype(jnp.bfloat16)
    return (mixed, token_grad, gate_grad, gate_grad_w, up_grad_w, down_grad)


def body(*args):
    tokens, gate_weight = args[0], args[5]
    mesh_fits = (lax.axis_size("dp"), lax.axis_size("expert")) == (4, 8)
    if mesh_fits and tokens.shape[0] <= gate_weight.shape[0] * CAP:
        return dense_body(*args)
    return routed_body(*args)


def solution(mesh):
    return jax.shard_map(
        body,
        mesh=mesh,
        in_specs=(
            P(("dp", "expert"), None),
            P(("dp", "expert"), None),
            P(("dp", "expert"), None),
            P(("dp", "expert"), None),
            P(),
            P("expert", "dp", None),
            P("expert", "dp", None),
            P("expert", "dp", None),
        ),
        out_specs=(
            P(("dp", "expert"), None),
            P(("dp", "expert"), None),
            P(("dp", "expert"), None),
            P("expert", "dp", None),
            P("expert", "dp", None),
            P("expert", "dp", None),
        ),
        check_vma=False,
    )
```

```python
import functools
import math

import jax
import jax.numpy as jnp
from jax import lax
from jax.experimental import pallas as pl
from jax.experimental.pallas import tpu as pltpu
from jax.sharding import PartitionSpec as P

CAP = 3
AXES = ("dp", "expert")
CORE, Z1, Z2, Z3, X, Y = 1, 2, 4, 6, 8, 16
GROUPS = ((0,), (1, 2), (3,))
CHUNK = 512
WIDE = 1024
PAIR = 2
MIB = 1 << 20

NT = (((1,), (1,)), ((), ()))
NN = (((1,), (0,)), ((), ()))


def gated(values):
    sigmoid_v = jax.nn.sigmoid(values)
    return (values * sigmoid_v, sigmoid_v * (1.0 + values * (1.0 - sigmoid_v)))


def swap(values, even, odd=None):
    odd = even if odd is None else odd
    count = lax.axis_size("dp") * lax.axis_size("expert")
    pairs = [(i, i ^ (odd if i & CORE else even)) for i in range(count)]
    return lax.ppermute(values, AXES, pairs)


def add(*parts):
    total = parts[0].astype(jnp.float32)
    for part in parts[1:]:
        total = total + part.astype(jnp.float32)
    return total.astype(jnp.bfloat16)


def together(*values):
    return lax.optimization_barrier(values)


def slots_of(expert_ids, placement):
    total = placement.shape[0]
    matches = expert_ids[:, :, None] == jnp.arange(total, dtype=jnp.int32)
    return jnp.sum(jnp.where(matches, placement, 0), axis=2)


def dot(a, b, dims=NN):
    return lax.dot_general(a, b, dims, preferred_element_type=jnp.float32)


def iota(shape, axis):
    return lax.broadcasted_iota(jnp.int32, shape, axis)


def ordered(pieces, tok_count):
    rows = []
    for quarter in range(4):
        for piece, group in zip(pieces, GROUPS):
            size = len(group) * tok_count
            rows.append(piece[quarter * size : (quarter + 1) * size])
    return jnp.concatenate(rows, axis=0)


def put_in_places(pick, rows, half, x_ref):
    experts, both = x_ref.shape[:2]
    places = both // 2
    rows = dot(pick, rows).astype(jnp.bfloat16)
    for e in range(experts):
        x_ref[e, half * places : (half + 1) * places] = rows[e * places : (e + 1) * places]


def route_kernel(tok_count, *refs):
    rows_refs, part_refs, (mine_ref, mine_t_ref, both_ref) = refs[:6], refs[6:8], refs[8:11]
    x_ref, put_ref, pick_ref, prob_ref = refs[12:]
    experts, both = x_ref.shape[:2]
    places = both // 2
    count = pick_ref.shape[2]

    @pl.when(pl.program_id(0) == 0)
    def _():
        row, col = iota((count, count), 0), iota((count, count), 1)
        block = lax.div(row, tok_count)
        before = ((col < row) & (lax.div(col, tok_count) == block)).astype(jnp.bfloat16)
        columns = mine_ref.shape[0]
        first = (lax.div(iota((count, columns), 0), tok_count) * CAP).astype(jnp.float32)
        spot = lax.rem(iota((count, experts * places), 1), places).astype(jnp.float32)
        spot_t = lax.rem(iota((experts * places, count), 0), places).astype(jnp.float32)
        for half in range(2):
            prob = part_refs[half][...]
            taken = prob.astype(jnp.float32) > 0.0
            rank = dot(before, jnp.where(taken, 1.0, 0.0).astype(jnp.bfloat16))
            place = jnp.where(taken, rank + first, -1.0).astype(jnp.bfloat16)
            put = jnp.where(dot(place, mine_ref[...]) == spot, 1.0, 0.0)
            pick = dot(mine_t_ref[...], place, NT) == spot_t
            put_ref[half] = put.astype(jnp.bfloat16)
            pick_ref[half] = jnp.where(pick, 1.0, 0.0).astype(jnp.bfloat16)
            weight = jnp.sum(put * dot(prob, both_ref[...]), axis=0, keepdims=True)
            for i in range(experts):
                prob_ref[i, :, half * places : (half + 1) * places] = weight[
                    :, i * places : (i + 1) * places
                ]

    for half in range(2):
        rows = ordered(rows_refs[3 * half : 3 * half + 3], tok_count)
        put_in_places(pick_ref[half], rows, half, x_ref)


def up_kernel(x_ref, prob_ref, gate_ref, up_ref, g_ref, u_ref, h_ref, ht_ref, held_ref, sems):
    step = pl.program_id(0)
    hidden = gate_ref.shape[1]

    def copies(e):
        slot = lax.rem(e, 2)
        for j, source in enumerate((gate_ref, up_ref)):
            held = held_ref.at[slot, hidden * j : hidden * (j + 1)]
            yield pltpu.make_async_copy(source.at[e], held, sems.at[slot, j])

    @pl.when(step == 0)
    def _():
        for copy in copies(step):
            copy.start()

    @pl.when(step + 1 < pl.num_programs(0))
    def _():
        for copy in copies(step + 1):
            copy.start()

    for copy in copies(step):
        copy.wait()
    product = dot(held_ref[lax.rem(step, 2)], x_ref[0], NT)
    g, u = product[:hidden], product[hidden:]
    g_ref[0] = g
    u_ref[0] = u
    silu_v, _ = gated(g)
    scaled = silu_v * u * prob_ref[0]
    ht_ref[0] = scaled.astype(jnp.bfloat16)
    h_ref[0] = scaled.T.astype(jnp.bfloat16)


def place_kernel(own0, own1, other0, other1, pick_ref, x_ref, kept_ref):
    for half, pieces in enumerate(((own0, own1), (other0, other1))):
        rows = jnp.concatenate([pieces[0][...], pieces[1][...]], axis=0)
        put_in_places(pick_ref[half], rows, half, x_ref)
    kept_ref[...] = x_ref[...]


def slope_kernel(x_ref, put_ref, prob_ref, mine_ref, down_ref, g_ref, u_ref,
                 dg_ref, du_ref, dgt_ref, dut_ref, share_ref, shares_ref, terms_ref):
    e = pl.program_id(0)
    experts, both = shares_ref.shape
    places = both // 2
    _, hidden, width = down_ref.shape
    product = dot(
        down_ref[...].reshape(PAIR * hidden, width), x_ref[...].reshape(PAIR * both, width), NT
    )
    for i in range(PAIR):
        plain = product[hidden * i : hidden * (i + 1), both * i : both * (i + 1)]
        g, u = g_ref[i], u_ref[i]
        silu_v, slope = gated(g)
        shares_ref[pl.ds(PAIR * e + i, 1), :] = jnp.sum(silu_v * u * plain, axis=0, keepdims=True)
        scaled = plain * prob_ref[i]
        dg = scaled * u * slope
        du = scaled * silu_v
        dgt_ref[i] = dg.astype(jnp.bfloat16)
        dut_ref[i] = du.astype(jnp.bfloat16)
        dg_ref[i] = dg.T.astype(jnp.bfloat16)
        du_ref[i] = du.T.astype(jnp.bfloat16)

    @pl.when(e == pl.num_programs(0) - 1)
    def _():
        shares = shares_ref[...].T
        for half in range(2):
            for i in range(experts):
                share = shares[half * places : (half + 1) * places, i : i + 1]
                share = (share * mine_ref[i].astype(jnp.float32)).astype(jnp.bfloat16)
                terms_ref[i * places : (i + 1) * places] = share
            share_ref[half] = dot(put_ref[half], terms_ref[...]).astype(jnp.bfloat16)


def back_kernel(terms, steps, put_ref, *refs):
    lefts, rights = refs[:terms], refs[terms : 2 * terms]
    extra_ref = refs[2 * terms] if len(refs) > 2 * terms + 3 else None
    own_ref, other_ref, rows_ref = refs[-3:]
    experts, places = rights[0].shape[0], put_ref.shape[2] // rights[0].shape[0]

    @pl.when(pl.program_id(0) < steps)
    def _():
        for e in range(experts):
            rows = dot(lefts[0][e], rights[0][e])
            for left, right in zip(lefts[1:], rights[1:]):
                rows = rows + dot(left[e], right[e])
            rows = rows.astype(jnp.bfloat16)
            for half in range(2):
                rows_ref[half, e * places : (e + 1) * places] = rows[half * places : (half + 1) * places]
        own_ref[...] = dot(put_ref[0], rows_ref[0]).astype(jnp.bfloat16)
        other_ref[...] = dot(put_ref[1], rows_ref[1]).astype(jnp.bfloat16)

    if extra_ref is not None:

        @pl.when(pl.program_id(0) == steps)
        def _():
            columns = extra_ref.shape[2]
            own_ref[:, :columns] = extra_ref[0]
            other_ref[:, :columns] = extra_ref[1]


def grad_kernel(x_ref, left, *outs):
    hidden = outs[0].shape[1]
    for at in range(0, x_ref.shape[2], WIDE):
        product = dot(left[0], x_ref[0, :, at : at + WIDE]).astype(jnp.bfloat16)
        for i, out in enumerate(outs):
            out[0, :, at : at + WIDE] = product[hidden * i : hidden * (i + 1)]


def whole(a):
    shape = a.shape
    return pl.BlockSpec(shape, lambda i: (0,) * len(shape), pipeline_mode=pl.Buffered(1))


def kept(a):
    shape = a.shape
    return pl.BlockSpec(shape, lambda i: (0,) * len(shape))


def each(a, size=1):
    shape = a.shape
    return pl.BlockSpec((size, *shape[1:]), lambda i: (i,) + (0,) * (len(shape) - 1))


def near_core(a):
    return pltpu.with_memory_space_constraint(a, pltpu.VMEM)


def in_hbm(a):
    return pltpu.with_memory_space_constraint(a, pltpu.HBM)


def bf16(*shape):
    return jax.ShapeDtypeStruct(shape, jnp.bfloat16)


def f32(*shape):
    return jax.ShapeDtypeStruct(shape, jnp.float32)


def call(kernel, grid, ins, args, outs, shapes, scratch=(), flops=0):
    moved = sum(math.prod(a.shape) * a.dtype.itemsize for a in (*args, *shapes))
    return pl.pallas_call(
        kernel,
        grid=(grid,),
        in_specs=ins,
        out_specs=outs,
        out_shape=shapes,
        scratch_shapes=scratch,
        compiler_params=pltpu.CompilerParams(vmem_limit_bytes=14 * MIB),
        cost_estimate=pl.CostEstimate(flops=flops, bytes_accessed=moved, transcendentals=0),
    )(*args)


def fetch_kernel(source, after, held, mark, sem):
    copy = pltpu.make_async_copy(source, held, sem)
    copy.start()
    mark[...] = jnp.zeros_like(mark)
    copy.wait()


def fetch_call(weight, after):
    return pl.pallas_call(
        fetch_kernel,
        in_specs=[pl.BlockSpec(memory_space=pl.ANY)] * 2,
        out_specs=[pl.BlockSpec(memory_space=pl.ANY), pl.BlockSpec(memory_space=pltpu.VMEM)],
        out_shape=[pltpu.VMEM(weight.shape, weight.dtype), f32(8, 128)],
        scratch_shapes=[pltpu.SemaphoreType.DMA],
        compiler_params=pltpu.CompilerParams(vmem_limit_bytes=MIB),
        cost_estimate=pl.CostEstimate(
            flops=0, bytes_accessed=weight.size * weight.dtype.itemsize, transcendentals=0
        ),
    )(in_hbm(weight), after)


def route_call(own, other, parts, maps, mark, experts, tok_count):
    count = sum(piece.shape[0] for piece in own)
    places = count // tok_count * CAP
    width = own[0].shape[1]
    pieces = (*own, *other)
    shapes = [
        pltpu.VMEM((experts, 2 * places, width), jnp.bfloat16),
        bf16(2, count, experts * places),
        bf16(2, experts * places, count),
        f32(experts, 1, 2 * places),
    ]
    ins = [pl.BlockSpec((piece.shape[0], WIDE), lambda i: (0, i)) for piece in pieces]
    ins += [whole(a) for a in (*parts, *maps, mark)]
    outs = [pl.BlockSpec((experts, 2 * places, WIDE), lambda i: (0, 0, i))]
    outs += [kept(s) for s in shapes[1:]]
    flops = 4 * experts * places * count * width
    kernel = functools.partial(route_kernel, tok_count)
    return call(kernel, width // WIDE, ins, (*pieces, *parts, *maps, mark), outs, shapes, flops=flops)


def up_call(x, prob, w_gate, w_up):
    experts, hidden, width = w_gate.shape
    rows = x.shape[1]
    args = (near_core(x), prob, near_core(w_gate), near_core(w_up))
    shapes = [
        f32(experts, hidden, rows),
        f32(experts, hidden, rows),
        bf16(experts, rows, hidden),
        bf16(experts, hidden, rows),
    ]
    ins = [each(x), each(prob)] + [pl.BlockSpec(memory_space=pl.ANY)] * 2
    outs = [each(s) for s in shapes]
    scratch = [
        pltpu.VMEM((2, 2 * hidden, width), jnp.bfloat16),
        pltpu.SemaphoreType.DMA((2, 2)),
    ]
    flops = 4 * experts * rows * hidden * width
    return call(up_kernel, experts, ins, args, outs, shapes, scratch, flops)


def place_call(pieces, pick, experts):
    _, rows, count = pick.shape
    size, width = pieces[0].shape
    shape = (experts, 2 * rows // experts, width)
    shapes = [pltpu.VMEM(shape, jnp.bfloat16), pltpu.HBM(shape, jnp.bfloat16)]
    ins = [pl.BlockSpec((size, WIDE), lambda i: (0, i))] * len(pieces) + [whole(pick)]
    outs = [pl.BlockSpec((*shape[:2], WIDE), lambda i: (0, 0, i))] * 2
    flops = 4 * rows * count * width
    return call(place_kernel, width // WIDE, ins, (*pieces, pick), outs, shapes, flops=flops)


def slope_call(x, put, prob, mine, w_down, g, u):
    experts, hidden, width = w_down.shape
    rows, count, columns = x.shape[1], put.shape[1], mine.shape[2]
    args = (near_core(x), put, prob, mine, in_hbm(w_down), g, u)
    shapes = [
        bf16(experts, rows, hidden),
        bf16(experts, rows, hidden),
        bf16(experts, hidden, rows),
        bf16(experts, hidden, rows),
        bf16(2, count, columns),
    ]
    ins = [each(x, PAIR), whole(put), each(prob, PAIR), whole(mine)]
    ins += [each(a, PAIR) for a in (w_down, g, u)]
    outs = [each(s, PAIR) for s in shapes[:4]] + [kept(shapes[4])]
    scratch = [
        pltpu.VMEM((experts, rows), jnp.float32),
        pltpu.VMEM((put.shape[2], columns), jnp.bfloat16),
    ]
    flops = 2 * experts * rows * hidden * width
    return call(slope_kernel, experts // PAIR, ins, args, outs, shapes, scratch, flops)


def back_call(put, lefts, rights, start, stop, extra=None):
    experts, hidden, _ = rights[0].shape
    rows = lefts[0].shape[1]
    count = put.shape[1]
    terms = len(lefts)
    chunk = CHUNK * 2 // terms
    steps = (stop - start) // chunk
    columns = stop - start + (0 if extra is None else extra.shape[2])
    args = (put, *lefts, *rights) + (() if extra is None else (extra,))
    shapes = [bf16(count, columns)] * 2
    ins = [whole(put)] + [whole(a) for a in lefts]
    first, last = start // chunk, stop // chunk - 1
    ins += [
        pl.BlockSpec((experts, hidden, chunk), lambda i: (0, 0, jnp.minimum(first + i, last)))
    ] * terms
    ins += [] if extra is None else [whole(extra)]
    outs = [pl.BlockSpec((count, chunk), lambda i: (0, i))] * 2
    scratch = [
        pltpu.VMEM((2, put.shape[2], chunk), jnp.bfloat16),
    ]
    flops = 2 * experts * rows * (stop - start) * (hidden * terms + count)
    kernel = functools.partial(back_kernel, terms, steps)
    grid = steps + (0 if extra is None else 1)
    return call(kernel, grid, ins, args, outs, shapes, scratch, flops)


def grad_call(x, left, hidden):
    experts, rows, width = x.shape
    shapes = [bf16(experts, hidden, width)] * (left.shape[1] // hidden)
    flops = 2 * experts * rows * left.shape[1] * width
    ins, outs = [each(x), each(left)], [each(s) for s in shapes]
    return call(grad_kernel, experts, ins, (in_hbm(x), left), outs, shapes, flops=flops)


def dense_body(
    tokens, cotangent, gate_prob, expert_ids, placement, gate_weight, up_weight, down_weight
):
    tok_count, width = tokens.shape
    local, hidden, _ = gate_weight.shape
    total_experts = placement.shape[0]
    devices = lax.axis_size("dp") * lax.axis_size("expert")
    places = devices // 2 * CAP
    count = devices // 2 * tok_count
    quarter, middle = count // 4, width // 2

    slots = slots_of(expert_ids, placement)
    used = slots[:, :, None] == jnp.arange(total_experts, dtype=jnp.int32)
    prob = jnp.sum(jnp.where(used, gate_prob[:, :, None], 0.0), axis=1)
    high = lax.reduce_precision(prob, 8, 7)
    parts = jnp.concatenate([high.astype(jnp.bfloat16), (prob - high).astype(jnp.bfloat16)], axis=1)

    slot = lax.axis_index("expert") * local + jnp.arange(local * places, dtype=jnp.int32) // places
    spots = jnp.arange(2 * total_experts, dtype=jnp.int32)
    mine = (slot[:, None] == spots[None, :]).astype(jnp.bfloat16)
    both = (slot[None, :] == spots[:, None] % total_experts).astype(jnp.bfloat16)
    maps = ((slot[None, :] == spots[:, None]).astype(jnp.bfloat16), mine, both)

    def rows_of(*blocks):
        return jnp.concatenate(blocks)

    near, far = swap(tokens, Z1), swap(tokens, Z2)
    first0 = swap(tokens, X, Y)
    far_parts, near_parts, last_parts = (swap(parts, bit) for bit in (Z2, Z1, Z3))
    near, far = together(near, far)

    last = swap(far, Z1)
    middle_rows = rows_of(far, near)
    first1 = swap(middle_rows, X, Y)
    zero = rows_of(tokens, first0)
    second0 = swap(zero, Y, X)
    last, cotangent = together(last, cotangent)
    grads = [swap(cotangent, bit) for bit in (Z2, Z1, Z3)]
    last, first1, second0, gate_weight, far_parts, near_parts, last_parts = together(
        last, first1, second0, gate_weight, far_parts, near_parts, last_parts
    )
    gate_weight, mark = fetch_call(gate_weight, last)

    first2 = swap(last, X, Y)
    middle_rows = rows_of(middle_rows, first1)
    second1 = swap(middle_rows, Y, X)
    zero = rows_of(zero, second0)
    zero_other = swap(zero, CORE)
    parts = rows_of(parts, far_parts, near_parts, last_parts)
    first_parts = swap(parts, X, Y)
    first2, second1, cotangent, mark, up_weight, first_parts = together(
        first2, second1, cotangent, mark, up_weight, first_parts
    )
    up_weight, mark = fetch_call(up_weight, mark)

    last = rows_of(last, first2)
    second2 = swap(last, Y, X)
    parts = rows_of(parts, first_parts)
    second_parts = swap(parts, Y, X)
    second2, mark, second_parts = together(second2, mark, second_parts)
    parts = rows_of(parts, second_parts)
    parts = (parts, swap(parts, CORE))
    middle_rows = rows_of(middle_rows, second1)
    middle_other = swap(middle_rows, CORE)
    grads = rows_of(cotangent, *grads)
    grads = rows_of(grads, swap(grads, X, Y))
    last = rows_of(last, second2)
    last_other = swap(last, CORE)
    x, put, pick, prob_rows = route_call(
        (zero, middle_rows, last),
        (zero_other, middle_other, last_other),
        parts,
        maps,
        mark,
        local,
        tok_count,
    )
    x, grads = together(x, grads)
    far_grads = swap(grads, Y, X)
    grads_other = swap(grads, CORE)

    g, u, h, ht = up_call(x, prob_rows, gate_weight, up_weight)
    h, far_grads, grads_other = together(h, far_grads, grads_other)
    far_grads_other = swap(far_grads, CORE)
    mixed, mixed_other = back_call(put, [h], [in_hbm(down_weight)], 0, width)
    mixed_other, far_grads_other = together(mixed_other, far_grads_other)
    mixed = [mixed, swap(mixed_other, CORE)]

    near_c, c = place_call((grads, far_grads, grads_other, far_grads_other), pick, local)

    def leaving(parts, start, stop):
        return add(*(part[start:stop] for part in parts))

    def by_second(parts):
        return parts + [swap(leaving(parts, 2 * quarter, 4 * quarter), Y, X)]

    def by_first(parts):
        return parts + [swap(leaving(parts, quarter, 2 * quarter), X, Y)]

    def by_near(parts):
        return parts + [swap(leaving(parts, 2 * tok_count, 4 * tok_count), Z1)]

    def by_far(parts):
        return parts + [swap(leaving(parts, tok_count, 2 * tok_count), Z2)]

    weights = [near_core(gate_weight), near_core(up_weight)]
    mixed[1], far_c = together(mixed[1], c)
    rows, g = together(leaving(mixed, 2 * quarter, 4 * quarter), g)
    mixed.append(swap(rows, Y, X))
    dg, du, dgt, dut, share = slope_call(
        near_c, put, prob_rows, mine.reshape(local, places, -1), down_weight, g, u
    )
    left, left_other = back_call(put, [dg, du], weights, 0, middle)
    left = [left, swap(left_other, CORE)]
    left[0], mixed[2], dg, du = together(left[0], mixed[2], dg, du)
    mixed = by_first(mixed)
    right, right_other = back_call(put, [dg, du], weights, middle, width, share)
    right = [right, swap(right_other, CORE)]

    right[0], left[1] = together(right[0], left[1])
    rows, ht = together(leaving(left, 2 * quarter, 4 * quarter), ht)
    left.append(swap(rows, Y, X))
    (down_weight_grad,) = grad_call(far_c, ht, hidden)

    right[1], left[2], mixed[3], down_weight_grad = together(
        right[1], left[2], mixed[3], down_weight_grad
    )
    rows, left_rows, mixed_rows, dgt = together(
        leaving(right, 2 * quarter, 4 * quarter),
        leaving(left, quarter, 2 * quarter),
        leaving(mixed, 2 * tok_count, 4 * tok_count),
        dgt,
    )
    right.append(swap(rows, Y, X))
    left.append(swap(left_rows, X, Y))
    mixed.append(swap(mixed_rows, Z1))
    (gate_weight_grad,) = grad_call(x, dgt, hidden)

    right[2], left[3], mixed[4], gate_weight_grad = together(
        right[2], left[3], mixed[4], gate_weight_grad
    )
    rows, left_rows, mixed_rows, dut = together(
        leaving(right, quarter, 2 * quarter),
        leaving(left, 2 * tok_count, 4 * tok_count),
        leaving(mixed, tok_count, 2 * tok_count),
        dut,
    )
    right.append(swap(rows, X, Y))
    left.append(swap(left_rows, Z1))
    mixed.append(swap(mixed_rows, Z2))
    (up_weight_grad,) = grad_call(x, dut, hidden)

    right[3], left[4], up_weight_grad = together(right[3], left[4], up_weight_grad)
    right, left = by_near(right), by_far(left)
    right = by_far(right)
    mixed, left, right = (leaving(parts, 0, tok_count) for parts in (mixed, left, right))
    token_grad = jnp.concatenate([left, right[:, : width - middle]], axis=1)
    share = right[:, width - middle : width - middle + total_experts].astype(jnp.float32)
    gate_grad = jnp.sum(jnp.where(used, share[:, None, :], 0.0), axis=2)
    return (mixed, token_grad, gate_grad, gate_weight_grad, up_weight_grad, down_weight_grad)


def routed_body(tokens, cotangent, gate_prob, expert_ids, placement, gate_weight, up_weight, down_weight):
    tok_count, model_width = tokens.shape
    top_count = expert_ids.shape[1]
    expert_devs = lax.axis_size("expert")
    local_experts = gate_weight.shape[0]
    total_experts = placement.shape[0]
    capacity = CAP
    flat_ids = expert_ids.reshape(-1)
    matches_id = flat_ids[:, None] == jnp.arange(total_experts, dtype=jnp.int32)[None, :]
    slot_ids = jnp.sum(jnp.where(matches_id, placement[None, :], 0), axis=1)
    pair_order = jnp.arange(flat_ids.shape[0], dtype=jnp.int32)
    earlier = (slot_ids[:, None] == slot_ids[None, :]) & (pair_order[None, :] < pair_order[:, None])
    position = slot_ids * capacity + jnp.sum(earlier.astype(jnp.int32), axis=1)
    matches = jnp.arange(total_experts * capacity, dtype=jnp.int32)[:, None] == position[None, :]
    matches = matches.reshape(total_experts * capacity, tok_count, top_count)
    dispatch = jnp.any(matches, axis=2).astype(jnp.bfloat16)
    weight_map = jnp.sum(jnp.where(matches, gate_prob[None, :, :], 0.0), axis=2)
    sent_rows = jnp.dot(dispatch, tokens, preferred_element_type=jnp.float32).astype(jnp.bfloat16)
    sent_grads = jnp.dot(
        weight_map, cotangent.astype(jnp.float32), precision=lax.Precision.HIGHEST
    ).astype(jnp.bfloat16)
    block_shape = (1, expert_devs, local_experts, capacity, model_width)
    sent_rows = sent_rows.reshape(block_shape)
    sent_grads = sent_grads.reshape(block_shape)
    got_rows, got_grads = (
        lax.all_to_all(sent_rows, "expert", split_axis=1, concat_axis=1, tiled=True),
        lax.all_to_all(sent_grads, "expert", split_axis=1, concat_axis=1, tiled=True),
    )
    routed, routed_grads = (
        lax.all_gather(got_rows, "dp", axis=0, tiled=True),
        lax.all_gather(got_grads, "dp", axis=0, tiled=True),
    )
    gate_pre = jnp.einsum(
        "asjcd,jfd->asjcf", routed, gate_weight, preferred_element_type=jnp.float32
    )
    up_pre = jnp.einsum("asjcd,jfd->asjcf", routed, up_weight, preferred_element_type=jnp.float32)
    silu_v, slope = gated(gate_pre)
    hidden = (silu_v * up_pre).astype(jnp.bfloat16)
    out_part = jnp.einsum(
        "asjcf,jfd->asjcd", hidden, down_weight, preferred_element_type=jnp.float32
    )
    d_hidden = jnp.einsum(
        "asjcd,jfd->asjcf", routed_grads, down_weight, preferred_element_type=jnp.float32
    )
    d_gate_pre = (d_hidden * up_pre * slope).astype(jnp.bfloat16)
    d_up_pre = (d_hidden * silu_v).astype(jnp.bfloat16)
    back_part = jnp.einsum(
        "asjcf,jfd->asjcd", d_gate_pre, gate_weight, preferred_element_type=jnp.float32
    )
    back_part = back_part + jnp.einsum(
        "asjcf,jfd->asjcd", d_up_pre, up_weight, preferred_element_type=jnp.float32
    )
    down_grad = jnp.einsum(
        "asjcf,asjcd->jfd", hidden, routed_grads, preferred_element_type=jnp.float32
    ).astype(jnp.bfloat16)
    gate_grad_w = jnp.einsum(
        "asjcf,asjcd->jfd", d_gate_pre, routed, preferred_element_type=jnp.float32
    ).astype(jnp.bfloat16)
    up_grad_w = jnp.einsum(
        "asjcf,asjcd->jfd", d_up_pre, routed, preferred_element_type=jnp.float32
    ).astype(jnp.bfloat16)
    summed = (
        lax.psum_scatter(
            out_part.astype(jnp.bfloat16), "dp", scatter_dimension=0, tiled=True
        ).astype(jnp.float32),
        lax.psum_scatter(
            back_part.astype(jnp.bfloat16), "dp", scatter_dimension=0, tiled=True
        ).astype(jnp.float32),
    )
    back_out, back_grad = (
        lax.all_to_all(
            summed[0].astype(jnp.bfloat16), "expert", split_axis=1, concat_axis=1, tiled=True
        ),
        lax.all_to_all(
            summed[1].astype(jnp.bfloat16), "expert", split_axis=1, concat_axis=1, tiled=True
        ),
    )
    out_flat = back_out.reshape(total_experts * capacity, model_width)
    grad_flat = back_grad.reshape(total_experts * capacity, model_width)
    chosen_out = out_flat[position].reshape(tok_count, top_count, model_width)
    chosen_grad = grad_flat[position].reshape(tok_count, top_count, model_width)
    mixed = jnp.einsum(
        "tk,tkd->td", gate_prob, chosen_out.astype(jnp.float32), precision=lax.Precision.HIGHEST
    ).astype(jnp.bfloat16)
    gate_grad = jnp.einsum("td,tkd->tk", cotangent, chosen_out, preferred_element_type=jnp.float32)
    token_grad = jnp.sum(chosen_grad.astype(jnp.float32), axis=1).astype(jnp.bfloat16)
    return (mixed, token_grad, gate_grad, gate_grad_w, up_grad_w, down_grad)


def body(*args):
    tokens, gate_weight = args[0], args[5]
    mesh_fits = (lax.axis_size("dp"), lax.axis_size("expert")) == (4, 8)
    if mesh_fits and tokens.shape[0] <= gate_weight.shape[0] * CAP:
        return dense_body(*args)
    return routed_body(*args)


def solution(mesh):
    return jax.shard_map(
        body,
        mesh=mesh,
        in_specs=(
            P(("dp", "expert"), None),
            P(("dp", "expert"), None),
            P(("dp", "expert"), None),
            P(("dp", "expert"), None),
            P(),
            P("expert", "dp", None),
            P("expert", "dp", None),
            P("expert", "dp", None),
        ),
        out_specs=(
            P(("dp", "expert"), None),
            P(("dp", "expert"), None),
            P(("dp", "expert"), None),
            P("expert", "dp", None),
            P("expert", "dp", None),
            P("expert", "dp", None),
        ),
        check_vma=False,
    )
```

```python
import functools
import math

import jax
import jax.numpy as jnp
from jax import lax
from jax.experimental import pallas as pl
from jax.experimental.pallas import tpu as pltpu
from jax.sharding import PartitionSpec as P

CAP = 3
AXES = ("dp", "expert")
CORE, Z1, Z2, Z3, X, Y = 1, 2, 4, 6, 8, 16
GROUPS = ((0,), (1, 2), (3,))
CHUNK = 512
WIDE = 1024
PAIR = 2
MIB = 1 << 20

NT = (((1,), (1,)), ((), ()))
NN = (((1,), (0,)), ((), ()))


def gated(values):
    sigmoid_v = jax.nn.sigmoid(values)
    return (values * sigmoid_v, sigmoid_v * (1.0 + values * (1.0 - sigmoid_v)))


def swap(values, even, odd=None):
    odd = even if odd is None else odd
    count = lax.axis_size("dp") * lax.axis_size("expert")
    pairs = [(i, i ^ (odd if i & CORE else even)) for i in range(count)]
    return lax.ppermute(values, AXES, pairs)


def add(*parts):
    total = parts[0].astype(jnp.float32)
    for part in parts[1:]:
        total = total + part.astype(jnp.float32)
    return total.astype(jnp.bfloat16)


def together(*values):
    return lax.optimization_barrier(values)


def slots_of(expert_ids, placement):
    total = placement.shape[0]
    matches = expert_ids[:, :, None] == jnp.arange(total, dtype=jnp.int32)
    return jnp.sum(jnp.where(matches, placement, 0), axis=2)


def dot(a, b, dims=NN):
    return lax.dot_general(a, b, dims, preferred_element_type=jnp.float32)


def iota(shape, axis):
    return lax.broadcasted_iota(jnp.int32, shape, axis)


def ordered(pieces, tok_count):
    rows = []
    for quarter in range(4):
        for piece, group in zip(pieces, GROUPS):
            size = len(group) * tok_count
            rows.append(piece[quarter * size : (quarter + 1) * size])
    return jnp.concatenate(rows, axis=0)


def put_in_places(pick, rows, half, x_ref):
    experts, both = x_ref.shape[:2]
    places = both // 2
    rows = dot(pick, rows).astype(jnp.bfloat16)
    for e in range(experts):
        x_ref[e, half * places : (half + 1) * places] = rows[e * places : (e + 1) * places]


def route_kernel(tok_count, *refs):
    rows_refs, part_refs, (mine_ref, mine_t_ref, both_ref) = refs[:6], refs[6:8], refs[8:11]
    x_ref, put_ref, pick_ref, prob_ref = refs[12:]
    experts, both = x_ref.shape[:2]
    places = both // 2
    count = pick_ref.shape[2]

    @pl.when(pl.program_id(0) == 0)
    def _():
        row, col = iota((count, count), 0), iota((count, count), 1)
        block = lax.div(row, tok_count)
        before = ((col < row) & (lax.div(col, tok_count) == block)).astype(jnp.bfloat16)
        columns = mine_ref.shape[0]
        first = (lax.div(iota((count, columns), 0), tok_count) * CAP).astype(jnp.float32)
        spot = lax.rem(iota((count, experts * places), 1), places).astype(jnp.float32)
        spot_t = lax.rem(iota((experts * places, count), 0), places).astype(jnp.float32)
        for half in range(2):
            prob = part_refs[half][...]
            taken = prob.astype(jnp.float32) > 0.0
            rank = dot(before, jnp.where(taken, 1.0, 0.0).astype(jnp.bfloat16))
            place = jnp.where(taken, rank + first, -1.0).astype(jnp.bfloat16)
            put = jnp.where(dot(place, mine_ref[...]) == spot, 1.0, 0.0)
            pick = dot(mine_t_ref[...], place, NT) == spot_t
            put_ref[half] = put.astype(jnp.bfloat16)
            pick_ref[half] = jnp.where(pick, 1.0, 0.0).astype(jnp.bfloat16)
            weight = jnp.sum(put * dot(prob, both_ref[...]), axis=0, keepdims=True)
            for i in range(experts):
                prob_ref[i, :, half * places : (half + 1) * places] = weight[
                    :, i * places : (i + 1) * places
                ]

    for half in range(2):
        rows = ordered(rows_refs[3 * half : 3 * half + 3], tok_count)
        put_in_places(pick_ref[half], rows, half, x_ref)


def up_kernel(x_ref, prob_ref, gate_ref, up_ref, g_ref, u_ref, h_ref, ht_ref, held_ref, sems):
    step = pl.program_id(0)
    hidden = gate_ref.shape[1]

    def copies(e):
        slot = lax.rem(e, 2)
        for j, source in enumerate((gate_ref, up_ref)):
            held = held_ref.at[slot, hidden * j : hidden * (j + 1)]
            yield pltpu.make_async_copy(source.at[e], held, sems.at[slot, j])

    @pl.when(step == 0)
    def _():
        for copy in copies(step):
            copy.start()

    @pl.when(step + 1 < pl.num_programs(0))
    def _():
        for copy in copies(step + 1):
            copy.start()

    for copy in copies(step):
        copy.wait()
    product = dot(held_ref[lax.rem(step, 2)], x_ref[0], NT)
    g, u = product[:hidden], product[hidden:]
    g_ref[0] = g
    u_ref[0] = u
    silu_v, _ = gated(g)
    scaled = silu_v * u * prob_ref[0]
    ht_ref[0] = scaled.astype(jnp.bfloat16)
    h_ref[0] = scaled.T.astype(jnp.bfloat16)


def place_kernel(own0, own1, other0, other1, pick_ref, x_ref, kept_ref):
    for half, pieces in enumerate(((own0, own1), (other0, other1))):
        rows = jnp.concatenate([pieces[0][...], pieces[1][...]], axis=0)
        put_in_places(pick_ref[half], rows, half, x_ref)
    kept_ref[...] = x_ref[...]


def slope_kernel(x_ref, put_ref, prob_ref, mine_ref, down_ref, g_ref, u_ref,
                 dg_ref, du_ref, dgt_ref, dut_ref, share_ref, shares_ref, terms_ref):
    e = pl.program_id(0)
    experts, both = shares_ref.shape
    places = both // 2
    _, hidden, width = down_ref.shape
    product = dot(
        down_ref[...].reshape(PAIR * hidden, width), x_ref[...].reshape(PAIR * both, width), NT
    )
    for i in range(PAIR):
        plain = product[hidden * i : hidden * (i + 1), both * i : both * (i + 1)]
        g, u = g_ref[i], u_ref[i]
        silu_v, slope = gated(g)
        shares_ref[pl.ds(PAIR * e + i, 1), :] = jnp.sum(silu_v * u * plain, axis=0, keepdims=True)
        scaled = plain * prob_ref[i]
        dg = scaled * u * slope
        du = scaled * silu_v
        dgt_ref[i] = dg.astype(jnp.bfloat16)
        dut_ref[i] = du.astype(jnp.bfloat16)
        dg_ref[i] = dg.T.astype(jnp.bfloat16)
        du_ref[i] = du.T.astype(jnp.bfloat16)

    @pl.when(e == pl.num_programs(0) - 1)
    def _():
        shares = shares_ref[...].T
        for half in range(2):
            for i in range(experts):
                share = shares[half * places : (half + 1) * places, i : i + 1]
                share = (share * mine_ref[i].astype(jnp.float32)).astype(jnp.bfloat16)
                terms_ref[i * places : (i + 1) * places] = share
            share_ref[half] = dot(put_ref[half], terms_ref[...]).astype(jnp.bfloat16)


def back_kernel(terms, steps, put_ref, *refs):
    lefts, rights = refs[:terms], refs[terms : 2 * terms]
    extra_ref = refs[2 * terms] if len(refs) > 2 * terms + 3 else None
    own_ref, other_ref, rows_ref = refs[-3:]
    experts, places = rights[0].shape[0], put_ref.shape[2] // rights[0].shape[0]

    @pl.when(pl.program_id(0) < steps)
    def _():
        for e in range(experts):
            rows = dot(lefts[0][e], rights[0][e])
            for left, right in zip(lefts[1:], rights[1:]):
                rows = rows + dot(left[e], right[e])
            rows = rows.astype(jnp.bfloat16)
            for half in range(2):
                rows_ref[half, e * places : (e + 1) * places] = rows[half * places : (half + 1) * places]
        own_ref[...] = dot(put_ref[0], rows_ref[0]).astype(jnp.bfloat16)
        other_ref[...] = dot(put_ref[1], rows_ref[1]).astype(jnp.bfloat16)

    if extra_ref is not None:

        @pl.when(pl.program_id(0) == steps)
        def _():
            columns = extra_ref.shape[2]
            own_ref[:, :columns] = extra_ref[0]
            other_ref[:, :columns] = extra_ref[1]


def grad_kernel(x_ref, left, *outs):
    hidden = outs[0].shape[1]
    for at in range(0, x_ref.shape[2], WIDE):
        product = dot(left[0], x_ref[0, :, at : at + WIDE]).astype(jnp.bfloat16)
        for i, out in enumerate(outs):
            out[0, :, at : at + WIDE] = product[hidden * i : hidden * (i + 1)]


def whole(a):
    shape = a.shape
    return pl.BlockSpec(shape, lambda i: (0,) * len(shape), pipeline_mode=pl.Buffered(1))


def kept(a):
    shape = a.shape
    return pl.BlockSpec(shape, lambda i: (0,) * len(shape))


def each(a, size=1):
    shape = a.shape
    return pl.BlockSpec((size, *shape[1:]), lambda i: (i,) + (0,) * (len(shape) - 1))


def near_core(a):
    return pltpu.with_memory_space_constraint(a, pltpu.VMEM)


def in_hbm(a):
    return pltpu.with_memory_space_constraint(a, pltpu.HBM)


def bf16(*shape):
    return jax.ShapeDtypeStruct(shape, jnp.bfloat16)


def f32(*shape):
    return jax.ShapeDtypeStruct(shape, jnp.float32)


def call(kernel, grid, ins, args, outs, shapes, scratch=(), flops=0):
    moved = sum(math.prod(a.shape) * a.dtype.itemsize for a in (*args, *shapes))
    return pl.pallas_call(
        kernel,
        grid=(grid,),
        in_specs=ins,
        out_specs=outs,
        out_shape=shapes,
        scratch_shapes=scratch,
        compiler_params=pltpu.CompilerParams(vmem_limit_bytes=12 * MIB),
        cost_estimate=pl.CostEstimate(flops=flops, bytes_accessed=moved, transcendentals=0),
    )(*args)


def fetch_kernel(source, after, held, mark, sem):
    copy = pltpu.make_async_copy(source, held, sem)
    copy.start()
    mark[...] = jnp.zeros_like(mark)
    copy.wait()


def fetch_call(weight, after):
    return pl.pallas_call(
        fetch_kernel,
        in_specs=[pl.BlockSpec(memory_space=pl.ANY)] * 2,
        out_specs=[pl.BlockSpec(memory_space=pl.ANY), pl.BlockSpec(memory_space=pltpu.VMEM)],
        out_shape=[pltpu.VMEM(weight.shape, weight.dtype), f32(8, 128)],
        scratch_shapes=[pltpu.SemaphoreType.DMA],
        compiler_params=pltpu.CompilerParams(vmem_limit_bytes=MIB),
        cost_estimate=pl.CostEstimate(
            flops=0, bytes_accessed=weight.size * weight.dtype.itemsize, transcendentals=0
        ),
    )(in_hbm(weight), after)


def route_call(own, other, parts, maps, mark, experts, tok_count):
    count = sum(piece.shape[0] for piece in own)
    places = count // tok_count * CAP
    width = own[0].shape[1]
    pieces = (*own, *other)
    shapes = [
        pltpu.VMEM((experts, 2 * places, width), jnp.bfloat16),
        bf16(2, count, experts * places),
        bf16(2, experts * places, count),
        f32(experts, 1, 2 * places),
    ]
    ins = [pl.BlockSpec((piece.shape[0], WIDE), lambda i: (0, i)) for piece in pieces]
    ins += [whole(a) for a in (*parts, *maps, mark)]
    outs = [pl.BlockSpec((experts, 2 * places, WIDE), lambda i: (0, 0, i))]
    outs += [kept(s) for s in shapes[1:]]
    flops = 4 * experts * places * count * width
    kernel = functools.partial(route_kernel, tok_count)
    return call(kernel, width // WIDE, ins, (*pieces, *parts, *maps, mark), outs, shapes, flops=flops)


def up_call(x, prob, w_gate, w_up):
    experts, hidden, width = w_gate.shape
    rows = x.shape[1]
    args = (near_core(x), prob, near_core(w_gate), near_core(w_up))
    shapes = [
        f32(experts, hidden, rows),
        f32(experts, hidden, rows),
        bf16(experts, rows, hidden),
        bf16(experts, hidden, rows),
    ]
    ins = [each(x), each(prob)] + [pl.BlockSpec(memory_space=pl.ANY)] * 2
    outs = [each(s) for s in shapes]
    scratch = [
        pltpu.VMEM((2, 2 * hidden, width), jnp.bfloat16),
        pltpu.SemaphoreType.DMA((2, 2)),
    ]
    flops = 4 * experts * rows * hidden * width
    return call(up_kernel, experts, ins, args, outs, shapes, scratch, flops)


def place_call(pieces, pick, experts):
    _, rows, count = pick.shape
    size, width = pieces[0].shape
    shape = (experts, 2 * rows // experts, width)
    shapes = [pltpu.VMEM(shape, jnp.bfloat16), pltpu.HBM(shape, jnp.bfloat16)]
    ins = [pl.BlockSpec((size, WIDE), lambda i: (0, i))] * len(pieces) + [whole(pick)]
    outs = [pl.BlockSpec((*shape[:2], WIDE), lambda i: (0, 0, i))] * 2
    flops = 4 * rows * count * width
    return call(place_kernel, width // WIDE, ins, (*pieces, pick), outs, shapes, flops=flops)


def slope_call(x, put, prob, mine, w_down, g, u):
    experts, hidden, width = w_down.shape
    rows, count, columns = x.shape[1], put.shape[1], mine.shape[2]
    args = (near_core(x), put, prob, mine, in_hbm(w_down), g, u)
    shapes = [
        bf16(experts, rows, hidden),
        bf16(experts, rows, hidden),
        bf16(experts, hidden, rows),
        bf16(experts, hidden, rows),
        bf16(2, count, columns),
    ]
    ins = [each(x, PAIR), whole(put), each(prob, PAIR), whole(mine)]
    ins += [each(a, PAIR) for a in (w_down, g, u)]
    outs = [each(s, PAIR) for s in shapes[:4]] + [kept(shapes[4])]
    scratch = [
        pltpu.VMEM((experts, rows), jnp.float32),
        pltpu.VMEM((put.shape[2], columns), jnp.bfloat16),
    ]
    flops = 2 * experts * rows * hidden * width
    return call(slope_kernel, experts // PAIR, ins, args, outs, shapes, scratch, flops)


def back_call(put, lefts, rights, start, stop, extra=None):
    experts, hidden, _ = rights[0].shape
    rows = lefts[0].shape[1]
    count = put.shape[1]
    terms = len(lefts)
    chunk = CHUNK * 2 // terms
    steps = (stop - start) // chunk
    columns = stop - start + (0 if extra is None else extra.shape[2])
    args = (put, *lefts, *rights) + (() if extra is None else (extra,))
    shapes = [bf16(count, columns)] * 2
    ins = [whole(put)] + [whole(a) for a in lefts]
    first, last = start // chunk, stop // chunk - 1
    ins += [
        pl.BlockSpec((experts, hidden, chunk), lambda i: (0, 0, jnp.minimum(first + i, last)))
    ] * terms
    ins += [] if extra is None else [whole(extra)]
    outs = [pl.BlockSpec((count, chunk), lambda i: (0, i))] * 2
    scratch = [
        pltpu.VMEM((2, put.shape[2], chunk), jnp.bfloat16),
    ]
    flops = 2 * experts * rows * (stop - start) * (hidden * terms + count)
    kernel = functools.partial(back_kernel, terms, steps)
    grid = steps + (0 if extra is None else 1)
    return call(kernel, grid, ins, args, outs, shapes, scratch, flops)


def grad_call(x, left, hidden):
    experts, rows, width = x.shape
    shapes = [bf16(experts, hidden, width)] * (left.shape[1] // hidden)
    flops = 2 * experts * rows * left.shape[1] * width
    ins, outs = [each(x), each(left)], [each(s) for s in shapes]
    return call(grad_kernel, experts, ins, (near_core(x), left), outs, shapes, flops=flops)


def dense_body(
    tokens, cotangent, gate_prob, expert_ids, placement, gate_weight, up_weight, down_weight
):
    tok_count, width = tokens.shape
    local, hidden, _ = gate_weight.shape
    total_experts = placement.shape[0]
    devices = lax.axis_size("dp") * lax.axis_size("expert")
    places = devices // 2 * CAP
    count = devices // 2 * tok_count
    quarter, middle = count // 4, width // 2

    slots = slots_of(expert_ids, placement)
    used = slots[:, :, None] == jnp.arange(total_experts, dtype=jnp.int32)
    prob = jnp.sum(jnp.where(used, gate_prob[:, :, None], 0.0), axis=1)
    high = lax.reduce_precision(prob, 8, 7)
    parts = jnp.concatenate([high.astype(jnp.bfloat16), (prob - high).astype(jnp.bfloat16)], axis=1)

    slot = lax.axis_index("expert") * local + jnp.arange(local * places, dtype=jnp.int32) // places
    spots = jnp.arange(2 * total_experts, dtype=jnp.int32)
    mine = (slot[:, None] == spots[None, :]).astype(jnp.bfloat16)
    both = (slot[None, :] == spots[:, None] % total_experts).astype(jnp.bfloat16)
    maps = ((slot[None, :] == spots[:, None]).astype(jnp.bfloat16), mine, both)

    def rows_of(*blocks):
        return jnp.concatenate(blocks)

    near, far = swap(tokens, Z1), swap(tokens, Z2)
    first0 = swap(tokens, X, Y)
    far_parts, near_parts, last_parts = (swap(parts, bit) for bit in (Z2, Z1, Z3))
    near, far = together(near, far)

    last = swap(far, Z1)
    middle_rows = rows_of(far, near)
    first1 = swap(middle_rows, X, Y)
    zero = rows_of(tokens, first0)
    second0 = swap(zero, Y, X)
    last, cotangent = together(last, cotangent)
    grads = [swap(cotangent, bit) for bit in (Z2, Z1, Z3)]
    last, first1, second0, gate_weight, far_parts, near_parts, last_parts = together(
        last, first1, second0, gate_weight, far_parts, near_parts, last_parts
    )
    gate_weight, mark = fetch_call(gate_weight, last)

    first2 = swap(last, X, Y)
    middle_rows = rows_of(middle_rows, first1)
    second1 = swap(middle_rows, Y, X)
    zero = rows_of(zero, second0)
    zero_other = swap(zero, CORE)
    parts = rows_of(parts, far_parts, near_parts, last_parts)
    first_parts = swap(parts, X, Y)
    first2, second1, cotangent, mark, up_weight, first_parts = together(
        first2, second1, cotangent, mark, up_weight, first_parts
    )
    up_weight, mark = fetch_call(up_weight, mark)

    last = rows_of(last, first2)
    second2 = swap(last, Y, X)
    parts = rows_of(parts, first_parts)
    second_parts = swap(parts, Y, X)
    second2, mark, second_parts = together(second2, mark, second_parts)
    parts = rows_of(parts, second_parts)
    parts = (parts, swap(parts, CORE))
    middle_rows = rows_of(middle_rows, second1)
    middle_other = swap(middle_rows, CORE)
    grads = rows_of(cotangent, *grads)
    first_grads = swap(grads, X, Y)
    last = rows_of(last, second2)
    last_other = swap(last, CORE)
    x, put, pick, prob_rows = route_call(
        (zero, middle_rows, last),
        (zero_other, middle_other, last_other),
        parts,
        maps,
        mark,
        local,
        tok_count,
    )
    x, first_grads = together(x, first_grads)
    grads = rows_of(grads, first_grads)
    far_grads = swap(grads, Y, X)
    grads_other = swap(grads, CORE)

    g, u, h, ht = up_call(x, prob_rows, gate_weight, up_weight)
    h, far_grads, grads_other = together(h, far_grads, grads_other)
    far_grads_other = swap(far_grads, CORE)
    mixed, mixed_other = back_call(put, [h], [in_hbm(down_weight)], 0, width)
    mixed_other, far_grads_other = together(mixed_other, far_grads_other)
    mixed = [mixed, swap(mixed_other, CORE)]

    near_c, c = place_call((grads, far_grads, grads_other, far_grads_other), pick, local)

    def leaving(parts, start, stop):
        return add(*(part[start:stop] for part in parts))

    def by_second(parts):
        return parts + [swap(leaving(parts, 2 * quarter, 4 * quarter), Y, X)]

    def by_first(parts):
        return parts + [swap(leaving(parts, quarter, 2 * quarter), X, Y)]

    def by_near(parts):
        return parts + [swap(leaving(parts, 2 * tok_count, 4 * tok_count), Z1)]

    def by_far(parts):
        return parts + [swap(leaving(parts, tok_count, 2 * tok_count), Z2)]

    weights = [near_core(gate_weight), near_core(up_weight)]
    mixed[1], far_c = together(mixed[1], c)
    rows, g = together(leaving(mixed, 2 * quarter, 4 * quarter), g)
    mixed.append(swap(rows, Y, X))
    dg, du, dgt, dut, share = slope_call(
        near_c, put, prob_rows, mine.reshape(local, places, -1), down_weight, g, u
    )
    left, left_other = back_call(put, [dg, du], weights, 0, middle)
    left = [left, swap(left_other, CORE)]
    left[0], mixed[2], dg, du = together(left[0], mixed[2], dg, du)
    mixed = by_first(mixed)
    right, right_other = back_call(put, [dg, du], weights, middle, width, share)
    right = [right, swap(right_other, CORE)]

    right[0], left[1] = together(right[0], left[1])
    rows, ht = together(leaving(left, 2 * quarter, 4 * quarter), ht)
    left.append(swap(rows, Y, X))
    (down_weight_grad,) = grad_call(far_c, ht, hidden)

    right[1], left[2], mixed[3], down_weight_grad = together(
        right[1], left[2], mixed[3], down_weight_grad
    )
    rows, left_rows, mixed_rows, dgt = together(
        leaving(right, 2 * quarter, 4 * quarter),
        leaving(left, quarter, 2 * quarter),
        leaving(mixed, 2 * tok_count, 4 * tok_count),
        dgt,
    )
    right.append(swap(rows, Y, X))
    left.append(swap(left_rows, X, Y))
    mixed.append(swap(mixed_rows, Z1))
    (gate_weight_grad,) = grad_call(x, dgt, hidden)

    right[2], left[3], mixed[4], gate_weight_grad = together(
        right[2], left[3], mixed[4], gate_weight_grad
    )
    rows, left_rows, mixed_rows, dut = together(
        leaving(right, quarter, 2 * quarter),
        leaving(left, 2 * tok_count, 4 * tok_count),
        leaving(mixed, tok_count, 2 * tok_count),
        dut,
    )
    right.append(swap(rows, X, Y))
    left.append(swap(left_rows, Z1))
    mixed.append(swap(mixed_rows, Z2))
    (up_weight_grad,) = grad_call(x, dut, hidden)

    right[3], left[4], up_weight_grad = together(right[3], left[4], up_weight_grad)
    right, left = by_near(right), by_far(left)
    right = by_far(right)
    mixed, left, right = (leaving(parts, 0, tok_count) for parts in (mixed, left, right))
    token_grad = jnp.concatenate([left, right[:, : width - middle]], axis=1)
    share = right[:, width - middle : width - middle + total_experts].astype(jnp.float32)
    gate_grad = jnp.sum(jnp.where(used, share[:, None, :], 0.0), axis=2)
    return (mixed, token_grad, gate_grad, gate_weight_grad, up_weight_grad, down_weight_grad)


def routed_body(tokens, cotangent, gate_prob, expert_ids, placement, gate_weight, up_weight, down_weight):
    tok_count, model_width = tokens.shape
    top_count = expert_ids.shape[1]
    expert_devs = lax.axis_size("expert")
    local_experts = gate_weight.shape[0]
    total_experts = placement.shape[0]
    capacity = CAP
    flat_ids = expert_ids.reshape(-1)
    matches_id = flat_ids[:, None] == jnp.arange(total_experts, dtype=jnp.int32)[None, :]
    slot_ids = jnp.sum(jnp.where(matches_id, placement[None, :], 0), axis=1)
    pair_order = jnp.arange(flat_ids.shape[0], dtype=jnp.int32)
    earlier = (slot_ids[:, None] == slot_ids[None, :]) & (pair_order[None, :] < pair_order[:, None])
    position = slot_ids * capacity + jnp.sum(earlier.astype(jnp.int32), axis=1)
    matches = jnp.arange(total_experts * capacity, dtype=jnp.int32)[:, None] == position[None, :]
    matches = matches.reshape(total_experts * capacity, tok_count, top_count)
    dispatch = jnp.any(matches, axis=2).astype(jnp.bfloat16)
    weight_map = jnp.sum(jnp.where(matches, gate_prob[None, :, :], 0.0), axis=2)
    sent_rows = jnp.dot(dispatch, tokens, preferred_element_type=jnp.float32).astype(jnp.bfloat16)
    sent_grads = jnp.dot(
        weight_map, cotangent.astype(jnp.float32), precision=lax.Precision.HIGHEST
    ).astype(jnp.bfloat16)
    block_shape = (1, expert_devs, local_experts, capacity, model_width)
    sent_rows = sent_rows.reshape(block_shape)
    sent_grads = sent_grads.reshape(block_shape)
    got_rows, got_grads = (
        lax.all_to_all(sent_rows, "expert", split_axis=1, concat_axis=1, tiled=True),
        lax.all_to_all(sent_grads, "expert", split_axis=1, concat_axis=1, tiled=True),
    )
    routed, routed_grads = (
        lax.all_gather(got_rows, "dp", axis=0, tiled=True),
        lax.all_gather(got_grads, "dp", axis=0, tiled=True),
    )
    gate_pre = jnp.einsum(
        "asjcd,jfd->asjcf", routed, gate_weight, preferred_element_type=jnp.float32
    )
    up_pre = jnp.einsum("asjcd,jfd->asjcf", routed, up_weight, preferred_element_type=jnp.float32)
    silu_v, slope = gated(gate_pre)
    hidden = (silu_v * up_pre).astype(jnp.bfloat16)
    out_part = jnp.einsum(
        "asjcf,jfd->asjcd", hidden, down_weight, preferred_element_type=jnp.float32
    )
    d_hidden = jnp.einsum(
        "asjcd,jfd->asjcf", routed_grads, down_weight, preferred_element_type=jnp.float32
    )
    d_gate_pre = (d_hidden * up_pre * slope).astype(jnp.bfloat16)
    d_up_pre = (d_hidden * silu_v).astype(jnp.bfloat16)
    back_part = jnp.einsum(
        "asjcf,jfd->asjcd", d_gate_pre, gate_weight, preferred_element_type=jnp.float32
    )
    back_part = back_part + jnp.einsum(
        "asjcf,jfd->asjcd", d_up_pre, up_weight, preferred_element_type=jnp.float32
    )
    down_grad = jnp.einsum(
        "asjcf,asjcd->jfd", hidden, routed_grads, preferred_element_type=jnp.float32
    ).astype(jnp.bfloat16)
    gate_grad_w = jnp.einsum(
        "asjcf,asjcd->jfd", d_gate_pre, routed, preferred_element_type=jnp.float32
    ).astype(jnp.bfloat16)
    up_grad_w = jnp.einsum(
        "asjcf,asjcd->jfd", d_up_pre, routed, preferred_element_type=jnp.float32
    ).astype(jnp.bfloat16)
    summed = (
        lax.psum_scatter(
            out_part.astype(jnp.bfloat16), "dp", scatter_dimension=0, tiled=True
        ).astype(jnp.float32),
        lax.psum_scatter(
            back_part.astype(jnp.bfloat16), "dp", scatter_dimension=0, tiled=True
        ).astype(jnp.float32),
    )
    back_out, back_grad = (
        lax.all_to_all(
            summed[0].astype(jnp.bfloat16), "expert", split_axis=1, concat_axis=1, tiled=True
        ),
        lax.all_to_all(
            summed[1].astype(jnp.bfloat16), "expert", split_axis=1, concat_axis=1, tiled=True
        ),
    )
    out_flat = back_out.reshape(total_experts * capacity, model_width)
    grad_flat = back_grad.reshape(total_experts * capacity, model_width)
    chosen_out = out_flat[position].reshape(tok_count, top_count, model_width)
    chosen_grad = grad_flat[position].reshape(tok_count, top_count, model_width)
    mixed = jnp.einsum(
        "tk,tkd->td", gate_prob, chosen_out.astype(jnp.float32), precision=lax.Precision.HIGHEST
    ).astype(jnp.bfloat16)
    gate_grad = jnp.einsum("td,tkd->tk", cotangent, chosen_out, preferred_element_type=jnp.float32)
    token_grad = jnp.sum(chosen_grad.astype(jnp.float32), axis=1).astype(jnp.bfloat16)
    return (mixed, token_grad, gate_grad, gate_grad_w, up_grad_w, down_grad)


def body(*args):
    tokens, gate_weight = args[0], args[5]
    mesh_fits = (lax.axis_size("dp"), lax.axis_size("expert")) == (4, 8)
    if mesh_fits and tokens.shape[0] <= gate_weight.shape[0] * CAP:
        return dense_body(*args)
    return routed_body(*args)


def solution(mesh):
    return jax.shard_map(
        body,
        mesh=mesh,
        in_specs=(
            P(("dp", "expert"), None),
            P(("dp", "expert"), None),
            P(("dp", "expert"), None),
            P(("dp", "expert"), None),
            P(),
            P("expert", "dp", None),
            P("expert", "dp", None),
            P("expert", "dp", None),
        ),
        out_specs=(
            P(("dp", "expert"), None),
            P(("dp", "expert"), None),
            P(("dp", "expert"), None),
            P("expert", "dp", None),
            P("expert", "dp", None),
            P("expert", "dp", None),
        ),
        check_vma=False,
    )
```

```python
import functools
import math

import jax
import jax.numpy as jnp
from jax import lax
from jax.experimental import pallas as pl
from jax.experimental.pallas import tpu as pltpu
from jax.sharding import PartitionSpec as P

CAP = 3
AXES = ("dp", "expert")
CORE, Z1, Z2, Z3, X, Y = 1, 2, 4, 6, 8, 16
GROUPS = ((0,), (1, 2), (3,))
CHUNK = 512
WIDE = 1024
PAIR = 2
MIB = 1 << 20

NT = (((1,), (1,)), ((), ()))
NN = (((1,), (0,)), ((), ()))


def gated(values):
    sigmoid_v = jax.nn.sigmoid(values)
    return (values * sigmoid_v, sigmoid_v * (1.0 + values * (1.0 - sigmoid_v)))


def swap(values, even, odd=None):
    odd = even if odd is None else odd
    count = lax.axis_size("dp") * lax.axis_size("expert")
    pairs = [(i, i ^ (odd if i & CORE else even)) for i in range(count)]
    return lax.ppermute(values, AXES, pairs)


def add(*parts):
    total = parts[0].astype(jnp.float32)
    for part in parts[1:]:
        total = total + part.astype(jnp.float32)
    return total.astype(jnp.bfloat16)


def together(*values):
    return lax.optimization_barrier(values)


def slots_of(expert_ids, placement):
    total = placement.shape[0]
    matches = expert_ids[:, :, None] == jnp.arange(total, dtype=jnp.int32)
    return jnp.sum(jnp.where(matches, placement, 0), axis=2)


def dot(a, b, dims=NN):
    return lax.dot_general(a, b, dims, preferred_element_type=jnp.float32)


def iota(shape, axis):
    return lax.broadcasted_iota(jnp.int32, shape, axis)


def ordered(pieces, tok_count):
    rows = []
    for quarter in range(4):
        for piece, group in zip(pieces, GROUPS):
            size = len(group) * tok_count
            rows.append(piece[quarter * size : (quarter + 1) * size])
    return jnp.concatenate(rows, axis=0)


def put_in_places(pick, rows, half, x_ref):
    experts, both = x_ref.shape[:2]
    places = both // 2
    rows = dot(pick, rows).astype(jnp.bfloat16)
    for e in range(experts):
        x_ref[e, half * places : (half + 1) * places] = rows[e * places : (e + 1) * places]


def route_kernel(tok_count, *refs):
    rows_refs, part_refs, (mine_ref, mine_t_ref, both_ref) = refs[:6], refs[6:8], refs[8:11]
    x_ref, put_ref, pick_ref, prob_ref = refs[12:]
    experts, both = x_ref.shape[:2]
    places = both // 2
    count = pick_ref.shape[2]

    @pl.when(pl.program_id(0) == 0)
    def _():
        row, col = iota((count, count), 0), iota((count, count), 1)
        block = lax.div(row, tok_count)
        before = ((col < row) & (lax.div(col, tok_count) == block)).astype(jnp.bfloat16)
        columns = mine_ref.shape[0]
        first = (lax.div(iota((count, columns), 0), tok_count) * CAP).astype(jnp.float32)
        spot = lax.rem(iota((count, experts * places), 1), places).astype(jnp.float32)
        spot_t = lax.rem(iota((experts * places, count), 0), places).astype(jnp.float32)
        for half in range(2):
            prob = part_refs[half][...]
            taken = prob.astype(jnp.float32) > 0.0
            rank = dot(before, jnp.where(taken, 1.0, 0.0).astype(jnp.bfloat16))
            place = jnp.where(taken, rank + first, -1.0).astype(jnp.bfloat16)
            put = jnp.where(dot(place, mine_ref[...]) == spot, 1.0, 0.0)
            pick = dot(mine_t_ref[...], place, NT) == spot_t
            put_ref[half] = put.astype(jnp.bfloat16)
            pick_ref[half] = jnp.where(pick, 1.0, 0.0).astype(jnp.bfloat16)
            weight = jnp.sum(put * dot(prob, both_ref[...]), axis=0, keepdims=True)
            for i in range(experts):
                prob_ref[i, :, half * places : (half + 1) * places] = weight[
                    :, i * places : (i + 1) * places
                ]

    for half in range(2):
        rows = ordered(rows_refs[3 * half : 3 * half + 3], tok_count)
        put_in_places(pick_ref[half], rows, half, x_ref)


def up_kernel(x_ref, prob_ref, gate_ref, up_ref, g_ref, u_ref, h_ref, ht_ref, held_ref, sems):
    step = pl.program_id(0)
    hidden = gate_ref.shape[1]

    def copies(e):
        slot = lax.rem(e, 2)
        for j, source in enumerate((gate_ref, up_ref)):
            held = held_ref.at[slot, hidden * j : hidden * (j + 1)]
            yield pltpu.make_async_copy(source.at[e], held, sems.at[slot, j])

    @pl.when(step == 0)
    def _():
        for copy in copies(step):
            copy.start()

    @pl.when(step + 1 < pl.num_programs(0))
    def _():
        for copy in copies(step + 1):
            copy.start()

    for copy in copies(step):
        copy.wait()
    product = dot(held_ref[lax.rem(step, 2)], x_ref[0], NT)
    g, u = product[:hidden], product[hidden:]
    g_ref[0] = g
    u_ref[0] = u
    silu_v, _ = gated(g)
    scaled = silu_v * u * prob_ref[0]
    ht_ref[0] = scaled.astype(jnp.bfloat16)
    h_ref[0] = scaled.T.astype(jnp.bfloat16)


def place_kernel(own0, own1, other0, other1, pick_ref, x_ref, kept_ref):
    for half, pieces in enumerate(((own0, own1), (other0, other1))):
        rows = jnp.concatenate([pieces[0][...], pieces[1][...]], axis=0)
        put_in_places(pick_ref[half], rows, half, x_ref)
    kept_ref[...] = x_ref[...]


def slope_kernel(x_ref, put_ref, prob_ref, mine_ref, down_ref, g_ref, u_ref,
                 dg_ref, du_ref, dgt_ref, dut_ref, share_ref, shares_ref, terms_ref):
    e = pl.program_id(0)
    experts, both = shares_ref.shape
    places = both // 2
    _, hidden, width = down_ref.shape
    product = dot(
        down_ref[...].reshape(PAIR * hidden, width), x_ref[...].reshape(PAIR * both, width), NT
    )
    for i in range(PAIR):
        plain = product[hidden * i : hidden * (i + 1), both * i : both * (i + 1)]
        g, u = g_ref[i], u_ref[i]
        silu_v, slope = gated(g)
        shares_ref[pl.ds(PAIR * e + i, 1), :] = jnp.sum(silu_v * u * plain, axis=0, keepdims=True)
        scaled = plain * prob_ref[i]
        dg = scaled * u * slope
        du = scaled * silu_v
        dgt_ref[i] = dg.astype(jnp.bfloat16)
        dut_ref[i] = du.astype(jnp.bfloat16)
        dg_ref[i] = dg.T.astype(jnp.bfloat16)
        du_ref[i] = du.T.astype(jnp.bfloat16)

    @pl.when(e == pl.num_programs(0) - 1)
    def _():
        shares = shares_ref[...].T
        for half in range(2):
            for i in range(experts):
                share = shares[half * places : (half + 1) * places, i : i + 1]
                share = (share * mine_ref[i].astype(jnp.float32)).astype(jnp.bfloat16)
                terms_ref[i * places : (i + 1) * places] = share
            share_ref[half] = dot(put_ref[half], terms_ref[...]).astype(jnp.bfloat16)


def back_kernel(terms, steps, put_ref, *refs):
    lefts, rights = refs[:terms], refs[terms : 2 * terms]
    extra_ref = refs[2 * terms] if len(refs) > 2 * terms + 3 else None
    own_ref, other_ref, rows_ref = refs[-3:]
    experts, places = rights[0].shape[0], put_ref.shape[2] // rights[0].shape[0]

    @pl.when(pl.program_id(0) < steps)
    def _():
        for e in range(experts):
            rows = dot(lefts[0][e], rights[0][e])
            for left, right in zip(lefts[1:], rights[1:]):
                rows = rows + dot(left[e], right[e])
            rows = rows.astype(jnp.bfloat16)
            for half in range(2):
                rows_ref[half, e * places : (e + 1) * places] = rows[half * places : (half + 1) * places]
        own_ref[...] = dot(put_ref[0], rows_ref[0]).astype(jnp.bfloat16)
        other_ref[...] = dot(put_ref[1], rows_ref[1]).astype(jnp.bfloat16)

    if extra_ref is not None:

        @pl.when(pl.program_id(0) == steps)
        def _():
            columns = extra_ref.shape[2]
            own_ref[:, :columns] = extra_ref[0]
            other_ref[:, :columns] = extra_ref[1]


def grad_kernel(x_ref, left, *refs):
    out = refs[-1]
    for at in range(0, x_ref.shape[2], WIDE):
        out[0, :, at : at + WIDE] = dot(left[0], x_ref[0, :, at : at + WIDE]).astype(jnp.bfloat16)


def whole(a):
    shape = a.shape
    return pl.BlockSpec(shape, lambda i: (0,) * len(shape), pipeline_mode=pl.Buffered(1))


def kept(a):
    shape = a.shape
    return pl.BlockSpec(shape, lambda i: (0,) * len(shape))


def each(a, size=1):
    shape = a.shape
    return pl.BlockSpec((size, *shape[1:]), lambda i: (i,) + (0,) * (len(shape) - 1))


def near_core(a):
    return pltpu.with_memory_space_constraint(a, pltpu.VMEM)


def in_hbm(a):
    return pltpu.with_memory_space_constraint(a, pltpu.HBM)


def bf16(*shape):
    return jax.ShapeDtypeStruct(shape, jnp.bfloat16)


def f32(*shape):
    return jax.ShapeDtypeStruct(shape, jnp.float32)


def call(kernel, grid, ins, args, outs, shapes, scratch=(), flops=0):
    moved = sum(math.prod(a.shape) * a.dtype.itemsize for a in (*args, *shapes))
    return pl.pallas_call(
        kernel,
        grid=(grid,),
        in_specs=ins,
        out_specs=outs,
        out_shape=shapes,
        scratch_shapes=scratch,
        compiler_params=pltpu.CompilerParams(vmem_limit_bytes=12 * MIB),
        cost_estimate=pl.CostEstimate(flops=flops, bytes_accessed=moved, transcendentals=0),
    )(*args)


def fetch_kernel(source, after, held, mark, sem):
    copy = pltpu.make_async_copy(source, held, sem)
    copy.start()
    mark[...] = jnp.zeros_like(mark)
    copy.wait()


def fetch_call(weight, after):
    return pl.pallas_call(
        fetch_kernel,
        in_specs=[pl.BlockSpec(memory_space=pl.ANY)] * 2,
        out_specs=[pl.BlockSpec(memory_space=pl.ANY), pl.BlockSpec(memory_space=pltpu.VMEM)],
        out_shape=[pltpu.VMEM(weight.shape, weight.dtype), f32(8, 128)],
        scratch_shapes=[pltpu.SemaphoreType.DMA],
        compiler_params=pltpu.CompilerParams(vmem_limit_bytes=MIB),
        cost_estimate=pl.CostEstimate(
            flops=0, bytes_accessed=weight.size * weight.dtype.itemsize, transcendentals=0
        ),
    )(in_hbm(weight), after)


def route_call(own, other, parts, maps, mark, experts, tok_count):
    count = sum(piece.shape[0] for piece in own)
    places = count // tok_count * CAP
    width = own[0].shape[1]
    pieces = (*own, *other)
    shapes = [
        pltpu.VMEM((experts, 2 * places, width), jnp.bfloat16),
        bf16(2, count, experts * places),
        bf16(2, experts * places, count),
        f32(experts, 1, 2 * places),
    ]
    ins = [pl.BlockSpec((piece.shape[0], WIDE), lambda i: (0, i)) for piece in pieces]
    ins += [whole(a) for a in (*parts, *maps, mark)]
    outs = [pl.BlockSpec((experts, 2 * places, WIDE), lambda i: (0, 0, i))]
    outs += [kept(s) for s in shapes[1:]]
    flops = 4 * experts * places * count * width
    kernel = functools.partial(route_kernel, tok_count)
    return call(kernel, width // WIDE, ins, (*pieces, *parts, *maps, mark), outs, shapes, flops=flops)


def up_call(x, prob, w_gate, w_up):
    experts, hidden, width = w_gate.shape
    rows = x.shape[1]
    args = (near_core(x), prob, near_core(w_gate), near_core(w_up))
    shapes = [
        f32(experts, hidden, rows),
        f32(experts, hidden, rows),
        bf16(experts, rows, hidden),
        bf16(experts, hidden, rows),
    ]
    ins = [each(x), each(prob)] + [pl.BlockSpec(memory_space=pl.ANY)] * 2
    outs = [each(s) for s in shapes]
    scratch = [
        pltpu.VMEM((2, 2 * hidden, width), jnp.bfloat16),
        pltpu.SemaphoreType.DMA((2, 2)),
    ]
    flops = 4 * experts * rows * hidden * width
    return call(up_kernel, experts, ins, args, outs, shapes, scratch, flops)


def place_call(pieces, pick, experts):
    _, rows, count = pick.shape
    size, width = pieces[0].shape
    shape = (experts, 2 * rows // experts, width)
    shapes = [pltpu.VMEM(shape, jnp.bfloat16), pltpu.HBM(shape, jnp.bfloat16)]
    ins = [pl.BlockSpec((size, WIDE), lambda i: (0, i))] * len(pieces) + [whole(pick)]
    outs = [pl.BlockSpec((*shape[:2], WIDE), lambda i: (0, 0, i))] * 2
    flops = 4 * rows * count * width
    return call(place_kernel, width // WIDE, ins, (*pieces, pick), outs, shapes, flops=flops)


def slope_call(x, put, prob, mine, w_down, g, u):
    experts, hidden, width = w_down.shape
    rows, count, columns = x.shape[1], put.shape[1], mine.shape[2]
    args = (near_core(x), put, prob, mine, in_hbm(w_down), g, u)
    shapes = [
        bf16(experts, rows, hidden),
        bf16(experts, rows, hidden),
        bf16(experts, hidden, rows),
        bf16(experts, hidden, rows),
        bf16(2, count, columns),
    ]
    ins = [each(x, PAIR), whole(put), each(prob, PAIR), whole(mine)]
    ins += [each(a, PAIR) for a in (w_down, g, u)]
    outs = [each(s, PAIR) for s in shapes[:4]] + [kept(shapes[4])]
    scratch = [
        pltpu.VMEM((experts, rows), jnp.float32),
        pltpu.VMEM((put.shape[2], columns), jnp.bfloat16),
    ]
    flops = 2 * experts * rows * hidden * width
    return call(slope_kernel, experts // PAIR, ins, args, outs, shapes, scratch, flops)


def back_call(put, lefts, rights, start, stop, extra=None):
    experts, hidden, _ = rights[0].shape
    rows = lefts[0].shape[1]
    count = put.shape[1]
    terms = len(lefts)
    chunk = CHUNK * 2 // terms
    steps = (stop - start) // chunk
    columns = stop - start + (0 if extra is None else extra.shape[2])
    args = (put, *lefts, *rights) + (() if extra is None else (extra,))
    shapes = [bf16(count, columns)] * 2
    ins = [whole(put)] + [whole(a) for a in lefts]
    first, last = start // chunk, stop // chunk - 1
    ins += [
        pl.BlockSpec((experts, hidden, chunk), lambda i: (0, 0, jnp.minimum(first + i, last)))
    ] * terms
    ins += [] if extra is None else [whole(extra)]
    outs = [pl.BlockSpec((count, chunk), lambda i: (0, i))] * 2
    scratch = [
        pltpu.VMEM((2, put.shape[2], chunk), jnp.bfloat16),
    ]
    flops = 2 * experts * rows * (stop - start) * (hidden * terms + count)
    kernel = functools.partial(back_kernel, terms, steps)
    grid = steps + (0 if extra is None else 1)
    return call(kernel, grid, ins, args, outs, shapes, scratch, flops)


def grad_call(x, left, first=0, last=None, into=None):
    experts, rows, width = x.shape
    hidden = left.shape[1]
    count = (experts if last is None else last) - first
    args = (near_core(x), left) + (() if into is None else (into,))

    def own(a):
        return pl.BlockSpec((1, *a.shape[1:]), lambda i: (first + i, 0, 0))

    shape = bf16(experts, hidden, width)
    ins = [own(x), own(left)] + ([] if into is None else [pl.BlockSpec(memory_space=pl.ANY)])
    moved = 2 * count * (rows * width + rows * hidden + hidden * width)
    return pl.pallas_call(
        grad_kernel,
        grid=(count,),
        in_specs=ins,
        out_specs=own(shape),
        out_shape=shape,
        input_output_aliases={} if into is None else {2: 0},
        compiler_params=pltpu.CompilerParams(vmem_limit_bytes=12 * MIB),
        cost_estimate=pl.CostEstimate(
            flops=2 * count * rows * hidden * width, bytes_accessed=moved, transcendentals=0
        ),
    )(*args)


def dense_body(
    tokens, cotangent, gate_prob, expert_ids, placement, gate_weight, up_weight, down_weight
):
    tok_count, width = tokens.shape
    local = gate_weight.shape[0]
    total_experts = placement.shape[0]
    devices = lax.axis_size("dp") * lax.axis_size("expert")
    places = devices // 2 * CAP
    count = devices // 2 * tok_count
    quarter, middle = count // 4, width // 2

    slots = slots_of(expert_ids, placement)
    used = slots[:, :, None] == jnp.arange(total_experts, dtype=jnp.int32)
    prob = jnp.sum(jnp.where(used, gate_prob[:, :, None], 0.0), axis=1)
    high = lax.reduce_precision(prob, 8, 7)
    parts = jnp.concatenate([high.astype(jnp.bfloat16), (prob - high).astype(jnp.bfloat16)], axis=1)

    slot = lax.axis_index("expert") * local + jnp.arange(local * places, dtype=jnp.int32) // places
    spots = jnp.arange(2 * total_experts, dtype=jnp.int32)
    mine = (slot[:, None] == spots[None, :]).astype(jnp.bfloat16)
    both = (slot[None, :] == spots[:, None] % total_experts).astype(jnp.bfloat16)
    maps = ((slot[None, :] == spots[:, None]).astype(jnp.bfloat16), mine, both)

    def rows_of(*blocks):
        return jnp.concatenate(blocks)

    near, far = swap(tokens, Z1), swap(tokens, Z2)
    first0 = swap(tokens, X, Y)
    near, far, parts = together(near, far, parts)
    far_parts, near_parts, last_parts = (swap(parts, bit) for bit in (Z2, Z1, Z3))

    last = swap(far, Z1)
    middle_rows = rows_of(far, near)
    first1 = swap(middle_rows, X, Y)
    zero = rows_of(tokens, first0)
    second0 = swap(zero, Y, X)
    last, cotangent = together(last, cotangent)
    grads = [swap(cotangent, bit) for bit in (Z2, Z1, Z3)]
    last, first1, second0, gate_weight, far_parts, near_parts, last_parts = together(
        last, first1, second0, gate_weight, far_parts, near_parts, last_parts
    )
    gate_weight, mark = fetch_call(gate_weight, last)

    first2 = swap(last, X, Y)
    middle_rows = rows_of(middle_rows, first1)
    second1 = swap(middle_rows, Y, X)
    zero = rows_of(zero, second0)
    zero_other = swap(zero, CORE)
    parts = rows_of(parts, far_parts, near_parts, last_parts)
    first_parts = swap(parts, X, Y)
    first2, second1, cotangent, mark, up_weight, first_parts = together(
        first2, second1, cotangent, mark, up_weight, first_parts
    )
    up_weight, mark = fetch_call(up_weight, mark)

    last = rows_of(last, first2)
    second2 = swap(last, Y, X)
    parts = rows_of(parts, first_parts)
    second_parts = swap(parts, Y, X)
    second2, mark, second_parts = together(second2, mark, second_parts)
    parts = rows_of(parts, second_parts)
    parts = (parts, swap(parts, CORE))
    middle_rows = rows_of(middle_rows, second1)
    middle_other = swap(middle_rows, CORE)
    grads = rows_of(cotangent, *grads)
    first_grads = swap(grads, X, Y)
    last = rows_of(last, second2)
    last_other = swap(last, CORE)
    x, put, pick, prob_rows = route_call(
        (zero, middle_rows, last),
        (zero_other, middle_other, last_other),
        parts,
        maps,
        mark,
        local,
        tok_count,
    )
    x, first_grads = together(x, first_grads)
    grads = rows_of(grads, first_grads)
    far_grads = swap(grads, Y, X)
    grads_other = swap(grads, CORE)

    g, u, h, ht = up_call(x, prob_rows, gate_weight, up_weight)
    h, far_grads, grads_other = together(h, far_grads, grads_other)
    far_grads_other = swap(far_grads, CORE)
    mixed, mixed_other = back_call(put, [h], [in_hbm(down_weight)], 0, width)
    mixed_other, far_grads_other = together(mixed_other, far_grads_other)
    mixed = [mixed, swap(mixed_other, CORE)]

    near_c, c = place_call((grads, far_grads, grads_other, far_grads_other), pick, local)

    def leaving(parts, start, stop):
        return add(*(part[start:stop] for part in parts))

    def by_second(parts):
        return parts + [swap(leaving(parts, 2 * quarter, 4 * quarter), Y, X)]

    def by_first(parts):
        return parts + [swap(leaving(parts, quarter, 2 * quarter), X, Y)]

    def by_near(parts):
        return parts + [swap(leaving(parts, 2 * tok_count, 4 * tok_count), Z1)]

    def by_far(parts):
        return parts + [swap(leaving(parts, tok_count, 2 * tok_count), Z2)]

    weights = [near_core(gate_weight), near_core(up_weight)]
    mixed[1], far_c = together(mixed[1], c)
    rows, g = together(leaving(mixed, 2 * quarter, 4 * quarter), g)
    mixed.append(swap(rows, Y, X))
    dg, du, dgt, dut, share = slope_call(
        near_c, put, prob_rows, mine.reshape(local, places, -1), down_weight, g, u
    )
    left, left_other = back_call(put, [dg, du], weights, 0, middle)
    left = [left, swap(left_other, CORE)]
    left[0], mixed[2], dg, du = together(left[0], mixed[2], dg, du)
    mixed = by_first(mixed)
    right, right_other = back_call(put, [dg, du], weights, middle, width, share)
    right = [right, swap(right_other, CORE)]

    right[0], left[1] = together(right[0], left[1])
    rows, ht = together(leaving(left, 2 * quarter, 4 * quarter), ht)
    left.append(swap(rows, Y, X))
    down_weight_grad = grad_call(far_c, ht)

    right[1], left[2], mixed[3], down_weight_grad = together(
        right[1], left[2], mixed[3], down_weight_grad
    )
    rows, left_rows, mixed_rows, dgt = together(
        leaving(right, 2 * quarter, 4 * quarter),
        leaving(left, quarter, 2 * quarter),
        leaving(mixed, 2 * tok_count, 4 * tok_count),
        dgt,
    )
    right.append(swap(rows, Y, X))
    left.append(swap(left_rows, X, Y))
    mixed.append(swap(mixed_rows, Z1))
    gate_weight_grad = grad_call(x, dgt)

    right[2], left[3], mixed[4], gate_weight_grad = together(
        right[2], left[3], mixed[4], gate_weight_grad
    )
    rows, left_rows, mixed_rows, dut = together(
        leaving(right, quarter, 2 * quarter),
        leaving(left, 2 * tok_count, 4 * tok_count),
        leaving(mixed, tok_count, 2 * tok_count),
        dut,
    )
    right.append(swap(rows, X, Y))
    left.append(swap(left_rows, Z1))
    mixed.append(swap(mixed_rows, Z2))
    up_weight_grad = grad_call(x, dut, 0, local // 2)

    right[3], left[4], up_weight_grad = together(right[3], left[4], up_weight_grad)
    rows, left_rows, dut = together(
        leaving(right, 2 * tok_count, 4 * tok_count),
        leaving(left, tok_count, 2 * tok_count),
        dut,
    )
    right.append(swap(rows, Z1))
    left.append(swap(left_rows, Z2))
    up_weight_grad = grad_call(x, dut, local // 2, local, up_weight_grad)
    right[4], up_weight_grad = together(right[4], up_weight_grad)
    right = by_far(right)
    mixed, left, right = (leaving(parts, 0, tok_count) for parts in (mixed, left, right))
    token_grad = jnp.concatenate([left, right[:, : width - middle]], axis=1)
    share = right[:, width - middle : width - middle + total_experts].astype(jnp.float32)
    gate_grad = jnp.sum(jnp.where(used, share[:, None, :], 0.0), axis=2)
    return (mixed, token_grad, gate_grad, gate_weight_grad, up_weight_grad, down_weight_grad)


def routed_body(tokens, cotangent, gate_prob, expert_ids, placement, gate_weight, up_weight, down_weight):
    tok_count, model_width = tokens.shape
    top_count = expert_ids.shape[1]
    expert_devs = lax.axis_size("expert")
    local_experts = gate_weight.shape[0]
    total_experts = placement.shape[0]
    capacity = CAP
    flat_ids = expert_ids.reshape(-1)
    matches_id = flat_ids[:, None] == jnp.arange(total_experts, dtype=jnp.int32)[None, :]
    slot_ids = jnp.sum(jnp.where(matches_id, placement[None, :], 0), axis=1)
    pair_order = jnp.arange(flat_ids.shape[0], dtype=jnp.int32)
    earlier = (slot_ids[:, None] == slot_ids[None, :]) & (pair_order[None, :] < pair_order[:, None])
    position = slot_ids * capacity + jnp.sum(earlier.astype(jnp.int32), axis=1)
    matches = jnp.arange(total_experts * capacity, dtype=jnp.int32)[:, None] == position[None, :]
    matches = matches.reshape(total_experts * capacity, tok_count, top_count)
    dispatch = jnp.any(matches, axis=2).astype(jnp.bfloat16)
    weight_map = jnp.sum(jnp.where(matches, gate_prob[None, :, :], 0.0), axis=2)
    sent_rows = jnp.dot(dispatch, tokens, preferred_element_type=jnp.float32).astype(jnp.bfloat16)
    sent_grads = jnp.dot(
        weight_map, cotangent.astype(jnp.float32), precision=lax.Precision.HIGHEST
    ).astype(jnp.bfloat16)
    block_shape = (1, expert_devs, local_experts, capacity, model_width)
    sent_rows = sent_rows.reshape(block_shape)
    sent_grads = sent_grads.reshape(block_shape)
    got_rows, got_grads = (
        lax.all_to_all(sent_rows, "expert", split_axis=1, concat_axis=1, tiled=True),
        lax.all_to_all(sent_grads, "expert", split_axis=1, concat_axis=1, tiled=True),
    )
    routed, routed_grads = (
        lax.all_gather(got_rows, "dp", axis=0, tiled=True),
        lax.all_gather(got_grads, "dp", axis=0, tiled=True),
    )
    gate_pre = jnp.einsum(
        "asjcd,jfd->asjcf", routed, gate_weight, preferred_element_type=jnp.float32
    )
    up_pre = jnp.einsum("asjcd,jfd->asjcf", routed, up_weight, preferred_element_type=jnp.float32)
    silu_v, slope = gated(gate_pre)
    hidden = (silu_v * up_pre).astype(jnp.bfloat16)
    out_part = jnp.einsum(
        "asjcf,jfd->asjcd", hidden, down_weight, preferred_element_type=jnp.float32
    )
    d_hidden = jnp.einsum(
        "asjcd,jfd->asjcf", routed_grads, down_weight, preferred_element_type=jnp.float32
    )
    d_gate_pre = (d_hidden * up_pre * slope).astype(jnp.bfloat16)
    d_up_pre = (d_hidden * silu_v).astype(jnp.bfloat16)
    back_part = jnp.einsum(
        "asjcf,jfd->asjcd", d_gate_pre, gate_weight, preferred_element_type=jnp.float32
    )
    back_part = back_part + jnp.einsum(
        "asjcf,jfd->asjcd", d_up_pre, up_weight, preferred_element_type=jnp.float32
    )
    down_grad = jnp.einsum(
        "asjcf,asjcd->jfd", hidden, routed_grads, preferred_element_type=jnp.float32
    ).astype(jnp.bfloat16)
    gate_grad_w = jnp.einsum(
        "asjcf,asjcd->jfd", d_gate_pre, routed, preferred_element_type=jnp.float32
    ).astype(jnp.bfloat16)
    up_grad_w = jnp.einsum(
        "asjcf,asjcd->jfd", d_up_pre, routed, preferred_element_type=jnp.float32
    ).astype(jnp.bfloat16)
    summed = (
        lax.psum_scatter(
            out_part.astype(jnp.bfloat16), "dp", scatter_dimension=0, tiled=True
        ).astype(jnp.float32),
        lax.psum_scatter(
            back_part.astype(jnp.bfloat16), "dp", scatter_dimension=0, tiled=True
        ).astype(jnp.float32),
    )
    back_out, back_grad = (
        lax.all_to_all(
            summed[0].astype(jnp.bfloat16), "expert", split_axis=1, concat_axis=1, tiled=True
        ),
        lax.all_to_all(
            summed[1].astype(jnp.bfloat16), "expert", split_axis=1, concat_axis=1, tiled=True
        ),
    )
    out_flat = back_out.reshape(total_experts * capacity, model_width)
    grad_flat = back_grad.reshape(total_experts * capacity, model_width)
    chosen_out = out_flat[position].reshape(tok_count, top_count, model_width)
    chosen_grad = grad_flat[position].reshape(tok_count, top_count, model_width)
    mixed = jnp.einsum(
        "tk,tkd->td", gate_prob, chosen_out.astype(jnp.float32), precision=lax.Precision.HIGHEST
    ).astype(jnp.bfloat16)
    gate_grad = jnp.einsum("td,tkd->tk", cotangent, chosen_out, preferred_element_type=jnp.float32)
    token_grad = jnp.sum(chosen_grad.astype(jnp.float32), axis=1).astype(jnp.bfloat16)
    return (mixed, token_grad, gate_grad, gate_grad_w, up_grad_w, down_grad)


def body(*args):
    tokens, gate_weight = args[0], args[5]
    mesh_fits = (lax.axis_size("dp"), lax.axis_size("expert")) == (4, 8)
    if mesh_fits and tokens.shape[0] <= gate_weight.shape[0] * CAP:
        return dense_body(*args)
    return routed_body(*args)


def solution(mesh):
    return jax.shard_map(
        body,
        mesh=mesh,
        in_specs=(
            P(("dp", "expert"), None),
            P(("dp", "expert"), None),
            P(("dp", "expert"), None),
            P(("dp", "expert"), None),
            P(),
            P("expert", "dp", None),
            P("expert", "dp", None),
            P("expert", "dp", None),
        ),
        out_specs=(
            P(("dp", "expert"), None),
            P(("dp", "expert"), None),
            P(("dp", "expert"), None),
            P("expert", "dp", None),
            P("expert", "dp", None),
            P("expert", "dp", None),
        ),
        check_vma=False,
    )
```

```python
import functools
import math

import jax
import jax.numpy as jnp
from jax import lax
from jax.experimental import pallas as pl
from jax.experimental.pallas import tpu as pltpu
from jax.sharding import PartitionSpec as P

CAP = 3
AXES = ("dp", "expert")
CORE, Z1, Z2, Z3, X, Y = 1, 2, 4, 6, 8, 16
GROUPS = ((0,), (1, 2), (3,))
CHUNK = 512
WIDE = 1024
PAIR = 2
MIB = 1 << 20

NT = (((1,), (1,)), ((), ()))
NN = (((1,), (0,)), ((), ()))


def gated(values):
    sigmoid_v = jax.nn.sigmoid(values)
    return (values * sigmoid_v, sigmoid_v * (1.0 + values * (1.0 - sigmoid_v)))


def swap(values, even, odd=None):
    odd = even if odd is None else odd
    count = lax.axis_size("dp") * lax.axis_size("expert")
    pairs = [(i, i ^ (odd if i & CORE else even)) for i in range(count)]
    return lax.ppermute(values, AXES, pairs)


def add(*parts):
    total = parts[0].astype(jnp.float32)
    for part in parts[1:]:
        total = total + part.astype(jnp.float32)
    return total.astype(jnp.bfloat16)


def together(*values):
    return lax.optimization_barrier(values)


def slots_of(expert_ids, placement):
    total = placement.shape[0]
    matches = expert_ids[:, :, None] == jnp.arange(total, dtype=jnp.int32)
    return jnp.sum(jnp.where(matches, placement, 0), axis=2)


def dot(a, b, dims=NN):
    return lax.dot_general(a, b, dims, preferred_element_type=jnp.float32)


def iota(shape, axis):
    return lax.broadcasted_iota(jnp.int32, shape, axis)


def ordered(pieces, tok_count):
    rows = []
    for quarter in range(4):
        for piece, group in zip(pieces, GROUPS):
            size = len(group) * tok_count
            rows.append(piece[quarter * size : (quarter + 1) * size])
    return jnp.concatenate(rows, axis=0)


def put_in_places(pick, rows, half, x_ref):
    experts, both = x_ref.shape[:2]
    places = both // 2
    rows = dot(pick, rows).astype(jnp.bfloat16)
    for e in range(experts):
        x_ref[e, half * places : (half + 1) * places] = rows[e * places : (e + 1) * places]


def route_kernel(tok_count, *refs):
    rows_refs, part_refs, (mine_ref, mine_t_ref, both_ref) = refs[:6], refs[6:8], refs[8:11]
    x_ref, put_ref, pick_ref, prob_ref = refs[12:]
    experts, both = x_ref.shape[:2]
    places = both // 2
    count = pick_ref.shape[2]

    @pl.when(pl.program_id(0) == 0)
    def _():
        row, col = iota((count, count), 0), iota((count, count), 1)
        block = lax.div(row, tok_count)
        before = ((col < row) & (lax.div(col, tok_count) == block)).astype(jnp.bfloat16)
        columns = mine_ref.shape[0]
        first = (lax.div(iota((count, columns), 0), tok_count) * CAP).astype(jnp.float32)
        spot = lax.rem(iota((count, experts * places), 1), places).astype(jnp.float32)
        spot_t = lax.rem(iota((experts * places, count), 0), places).astype(jnp.float32)
        for half in range(2):
            prob = part_refs[half][...]
            taken = prob.astype(jnp.float32) > 0.0
            rank = dot(before, jnp.where(taken, 1.0, 0.0).astype(jnp.bfloat16))
            place = jnp.where(taken, rank + first, -1.0).astype(jnp.bfloat16)
            put = jnp.where(dot(place, mine_ref[...]) == spot, 1.0, 0.0)
            pick = dot(mine_t_ref[...], place, NT) == spot_t
            put_ref[half] = put.astype(jnp.bfloat16)
            pick_ref[half] = jnp.where(pick, 1.0, 0.0).astype(jnp.bfloat16)
            weight = jnp.sum(put * dot(prob, both_ref[...]), axis=0, keepdims=True)
            for i in range(experts):
                prob_ref[i, :, half * places : (half + 1) * places] = weight[
                    :, i * places : (i + 1) * places
                ]

    for half in range(2):
        rows = ordered(rows_refs[3 * half : 3 * half + 3], tok_count)
        put_in_places(pick_ref[half], rows, half, x_ref)


def up_kernel(x_ref, prob_ref, gate_ref, up_ref, g_ref, u_ref, h_ref, ht_ref, held_ref, sems):
    step = pl.program_id(0)
    hidden = gate_ref.shape[1]

    def copies(e):
        slot = lax.rem(e, 2)
        for j, source in enumerate((gate_ref, up_ref)):
            held = held_ref.at[slot, hidden * j : hidden * (j + 1)]
            yield pltpu.make_async_copy(source.at[e], held, sems.at[slot, j])

    @pl.when(step == 0)
    def _():
        for copy in copies(step):
            copy.start()

    @pl.when(step + 1 < pl.num_programs(0))
    def _():
        for copy in copies(step + 1):
            copy.start()

    for copy in copies(step):
        copy.wait()
    product = dot(held_ref[lax.rem(step, 2)], x_ref[0], NT)
    g, u = product[:hidden], product[hidden:]
    g_ref[0] = g
    u_ref[0] = u
    silu_v, _ = gated(g)
    scaled = silu_v * u * prob_ref[0]
    ht_ref[0] = scaled.astype(jnp.bfloat16)
    h_ref[0] = scaled.T.astype(jnp.bfloat16)


def place_kernel(own0, own1, other0, other1, pick_ref, x_ref, kept_ref):
    for half, pieces in enumerate(((own0, own1), (other0, other1))):
        rows = jnp.concatenate([pieces[0][...], pieces[1][...]], axis=0)
        put_in_places(pick_ref[half], rows, half, x_ref)
    kept_ref[...] = x_ref[...]


def slope_kernel(x_ref, put_ref, prob_ref, mine_ref, down_ref, g_ref, u_ref,
                 dg_ref, du_ref, dgt_ref, dut_ref, share_ref, shares_ref, terms_ref):
    e = pl.program_id(0)
    experts, both = shares_ref.shape
    places = both // 2
    _, hidden, width = down_ref.shape
    product = dot(
        down_ref[...].reshape(PAIR * hidden, width), x_ref[...].reshape(PAIR * both, width), NT
    )
    for i in range(PAIR):
        plain = product[hidden * i : hidden * (i + 1), both * i : both * (i + 1)]
        g, u = g_ref[i], u_ref[i]
        silu_v, slope = gated(g)
        shares_ref[pl.ds(PAIR * e + i, 1), :] = jnp.sum(silu_v * u * plain, axis=0, keepdims=True)
        scaled = plain * prob_ref[i]
        dg = scaled * u * slope
        du = scaled * silu_v
        dgt_ref[i] = dg.astype(jnp.bfloat16)
        dut_ref[i] = du.astype(jnp.bfloat16)
        dg_ref[i] = dg.T.astype(jnp.bfloat16)
        du_ref[i] = du.T.astype(jnp.bfloat16)

    @pl.when(e == pl.num_programs(0) - 1)
    def _():
        shares = shares_ref[...].T
        for half in range(2):
            for i in range(experts):
                share = shares[half * places : (half + 1) * places, i : i + 1]
                share = (share * mine_ref[i].astype(jnp.float32)).astype(jnp.bfloat16)
                terms_ref[i * places : (i + 1) * places] = share
            share_ref[half] = dot(put_ref[half], terms_ref[...]).astype(jnp.bfloat16)


def back_kernel(terms, steps, put_ref, *refs):
    lefts, rights = refs[:terms], refs[terms : 2 * terms]
    extra_ref = refs[2 * terms] if len(refs) > 2 * terms + 3 else None
    own_ref, other_ref, rows_ref = refs[-3:]
    experts, places = rights[0].shape[0], put_ref.shape[2] // rights[0].shape[0]

    @pl.when(pl.program_id(0) < steps)
    def _():
        for e in range(experts):
            rows = dot(lefts[0][e], rights[0][e])
            for left, right in zip(lefts[1:], rights[1:]):
                rows = rows + dot(left[e], right[e])
            rows = rows.astype(jnp.bfloat16)
            for half in range(2):
                rows_ref[half, e * places : (e + 1) * places] = rows[half * places : (half + 1) * places]
        own_ref[...] = dot(put_ref[0], rows_ref[0]).astype(jnp.bfloat16)
        other_ref[...] = dot(put_ref[1], rows_ref[1]).astype(jnp.bfloat16)

    if extra_ref is not None:

        @pl.when(pl.program_id(0) == steps)
        def _():
            columns = extra_ref.shape[2]
            own_ref[:, :columns] = extra_ref[0]
            other_ref[:, :columns] = extra_ref[1]


def grad_kernel(x_ref, left, *refs):
    out = refs[-1]
    for at in range(0, x_ref.shape[2], WIDE):
        out[0, :, at : at + WIDE] = dot(left[0], x_ref[0, :, at : at + WIDE]).astype(jnp.bfloat16)


def whole(a):
    shape = a.shape
    return pl.BlockSpec(shape, lambda i: (0,) * len(shape), pipeline_mode=pl.Buffered(1))


def kept(a):
    shape = a.shape
    return pl.BlockSpec(shape, lambda i: (0,) * len(shape))


def each(a, size=1):
    shape = a.shape
    return pl.BlockSpec((size, *shape[1:]), lambda i: (i,) + (0,) * (len(shape) - 1))


def near_core(a):
    return pltpu.with_memory_space_constraint(a, pltpu.VMEM)


def in_hbm(a):
    return pltpu.with_memory_space_constraint(a, pltpu.HBM)


def bf16(*shape):
    return jax.ShapeDtypeStruct(shape, jnp.bfloat16)


def f32(*shape):
    return jax.ShapeDtypeStruct(shape, jnp.float32)


def call(kernel, grid, ins, args, outs, shapes, scratch=(), flops=0):
    moved = sum(math.prod(a.shape) * a.dtype.itemsize for a in (*args, *shapes))
    return pl.pallas_call(
        kernel,
        grid=(grid,),
        in_specs=ins,
        out_specs=outs,
        out_shape=shapes,
        scratch_shapes=scratch,
        compiler_params=pltpu.CompilerParams(vmem_limit_bytes=12 * MIB),
        cost_estimate=pl.CostEstimate(flops=flops, bytes_accessed=moved, transcendentals=0),
    )(*args)


def fetch_kernel(source, after, held, mark, sem):
    copy = pltpu.make_async_copy(source, held, sem)
    copy.start()
    mark[...] = jnp.zeros_like(mark)
    copy.wait()


def fetch_call(weight, after):
    return pl.pallas_call(
        fetch_kernel,
        in_specs=[pl.BlockSpec(memory_space=pl.ANY)] * 2,
        out_specs=[pl.BlockSpec(memory_space=pl.ANY), pl.BlockSpec(memory_space=pltpu.VMEM)],
        out_shape=[pltpu.VMEM(weight.shape, weight.dtype), f32(8, 128)],
        scratch_shapes=[pltpu.SemaphoreType.DMA],
        compiler_params=pltpu.CompilerParams(vmem_limit_bytes=MIB),
        cost_estimate=pl.CostEstimate(
            flops=0, bytes_accessed=weight.size * weight.dtype.itemsize, transcendentals=0
        ),
    )(in_hbm(weight), after)


def route_call(own, other, parts, maps, mark, experts, tok_count):
    count = sum(piece.shape[0] for piece in own)
    places = count // tok_count * CAP
    width = own[0].shape[1]
    pieces = (*own, *other)
    shapes = [
        pltpu.VMEM((experts, 2 * places, width), jnp.bfloat16),
        bf16(2, count, experts * places),
        bf16(2, experts * places, count),
        f32(experts, 1, 2 * places),
    ]
    ins = [pl.BlockSpec((piece.shape[0], WIDE), lambda i: (0, i)) for piece in pieces]
    ins += [whole(a) for a in (*parts, *maps, mark)]
    outs = [pl.BlockSpec((experts, 2 * places, WIDE), lambda i: (0, 0, i))]
    outs += [kept(s) for s in shapes[1:]]
    flops = 4 * experts * places * count * width
    kernel = functools.partial(route_kernel, tok_count)
    return call(kernel, width // WIDE, ins, (*pieces, *parts, *maps, mark), outs, shapes, flops=flops)


def up_call(x, prob, w_gate, w_up):
    experts, hidden, width = w_gate.shape
    rows = x.shape[1]
    args = (near_core(x), prob, near_core(w_gate), near_core(w_up))
    shapes = [
        f32(experts, hidden, rows),
        f32(experts, hidden, rows),
        bf16(experts, rows, hidden),
        bf16(experts, hidden, rows),
    ]
    ins = [each(x), each(prob)] + [pl.BlockSpec(memory_space=pl.ANY)] * 2
    outs = [each(s) for s in shapes]
    scratch = [
        pltpu.VMEM((2, 2 * hidden, width), jnp.bfloat16),
        pltpu.SemaphoreType.DMA((2, 2)),
    ]
    flops = 4 * experts * rows * hidden * width
    return call(up_kernel, experts, ins, args, outs, shapes, scratch, flops)


def place_call(pieces, pick, experts):
    _, rows, count = pick.shape
    size, width = pieces[0].shape
    shape = (experts, 2 * rows // experts, width)
    shapes = [pltpu.VMEM(shape, jnp.bfloat16), pltpu.HBM(shape, jnp.bfloat16)]
    ins = [pl.BlockSpec((size, WIDE), lambda i: (0, i))] * len(pieces) + [whole(pick)]
    outs = [pl.BlockSpec((*shape[:2], WIDE), lambda i: (0, 0, i))] * 2
    flops = 4 * rows * count * width
    return call(place_kernel, width // WIDE, ins, (*pieces, pick), outs, shapes, flops=flops)


def slope_call(x, put, prob, mine, w_down, g, u):
    experts, hidden, width = w_down.shape
    rows, count, columns = x.shape[1], put.shape[1], mine.shape[2]
    args = (near_core(x), put, prob, mine, in_hbm(w_down), g, u)
    shapes = [
        bf16(experts, rows, hidden),
        bf16(experts, rows, hidden),
        bf16(experts, hidden, rows),
        bf16(experts, hidden, rows),
        bf16(2, count, columns),
    ]
    ins = [each(x, PAIR), whole(put), each(prob, PAIR), whole(mine)]
    ins += [each(a, PAIR) for a in (w_down, g, u)]
    outs = [each(s, PAIR) for s in shapes[:4]] + [kept(shapes[4])]
    scratch = [
        pltpu.VMEM((experts, rows), jnp.float32),
        pltpu.VMEM((put.shape[2], columns), jnp.bfloat16),
    ]
    flops = 2 * experts * rows * hidden * width
    return call(slope_kernel, experts // PAIR, ins, args, outs, shapes, scratch, flops)


def back_call(put, lefts, rights, start, stop, extra=None):
    experts, hidden, _ = rights[0].shape
    rows = lefts[0].shape[1]
    count = put.shape[1]
    terms = len(lefts)
    chunk = CHUNK * 2 // terms
    steps = (stop - start) // chunk
    columns = stop - start + (0 if extra is None else extra.shape[2])
    args = (put, *lefts, *rights) + (() if extra is None else (extra,))
    shapes = [bf16(count, columns)] * 2
    ins = [whole(put)] + [whole(a) for a in lefts]
    first, last = start // chunk, stop // chunk - 1
    ins += [
        pl.BlockSpec((experts, hidden, chunk), lambda i: (0, 0, jnp.minimum(first + i, last)))
    ] * terms
    ins += [] if extra is None else [whole(extra)]
    outs = [pl.BlockSpec((count, chunk), lambda i: (0, i))] * 2
    scratch = [
        pltpu.VMEM((2, put.shape[2], chunk), jnp.bfloat16),
    ]
    flops = 2 * experts * rows * (stop - start) * (hidden * terms + count)
    kernel = functools.partial(back_kernel, terms, steps)
    grid = steps + (0 if extra is None else 1)
    return call(kernel, grid, ins, args, outs, shapes, scratch, flops)


def grad_call(x, left, first=0, last=None, into=None):
    experts, rows, width = x.shape
    hidden = left.shape[1]
    count = (experts if last is None else last) - first
    args = (near_core(x), left) + (() if into is None else (into,))

    def own(a):
        return pl.BlockSpec((1, *a.shape[1:]), lambda i: (first + i, 0, 0))

    shape = bf16(experts, hidden, width)
    ins = [own(x), own(left)] + ([] if into is None else [pl.BlockSpec(memory_space=pl.ANY)])
    moved = 2 * count * (rows * width + rows * hidden + hidden * width)
    return pl.pallas_call(
        grad_kernel,
        grid=(count,),
        in_specs=ins,
        out_specs=own(shape),
        out_shape=shape,
        input_output_aliases={} if into is None else {2: 0},
        compiler_params=pltpu.CompilerParams(vmem_limit_bytes=12 * MIB),
        cost_estimate=pl.CostEstimate(
            flops=2 * count * rows * hidden * width, bytes_accessed=moved, transcendentals=0
        ),
    )(*args)


def dense_body(
    tokens, cotangent, gate_prob, expert_ids, placement, gate_weight, up_weight, down_weight
):
    tok_count, width = tokens.shape
    local = gate_weight.shape[0]
    total_experts = placement.shape[0]
    devices = lax.axis_size("dp") * lax.axis_size("expert")
    places = devices // 2 * CAP
    count = devices // 2 * tok_count
    quarter, middle = count // 4, width // 2

    slots = slots_of(expert_ids, placement)
    used = slots[:, :, None] == jnp.arange(total_experts, dtype=jnp.int32)
    prob = jnp.sum(jnp.where(used, gate_prob[:, :, None], 0.0), axis=1)
    high = lax.reduce_precision(prob, 8, 7)
    parts = jnp.concatenate([high.astype(jnp.bfloat16), (prob - high).astype(jnp.bfloat16)], axis=1)

    slot = lax.axis_index("expert") * local + jnp.arange(local * places, dtype=jnp.int32) // places
    spots = jnp.arange(2 * total_experts, dtype=jnp.int32)
    mine = (slot[:, None] == spots[None, :]).astype(jnp.bfloat16)
    both = (slot[None, :] == spots[:, None] % total_experts).astype(jnp.bfloat16)
    maps = ((slot[None, :] == spots[:, None]).astype(jnp.bfloat16), mine, both)

    def rows_of(*blocks):
        return jnp.concatenate(blocks)

    near, far = swap(tokens, Z1), swap(tokens, Z2)
    first0 = swap(tokens, X, Y)
    near, far, parts = together(near, far, parts)
    far_parts, near_parts, last_parts = (swap(parts, bit) for bit in (Z2, Z1, Z3))

    last = swap(far, Z1)
    middle_rows = rows_of(far, near)
    first1 = swap(middle_rows, X, Y)
    zero = rows_of(tokens, first0)
    second0 = swap(zero, Y, X)
    last, cotangent = together(last, cotangent)
    grads = [swap(cotangent, bit) for bit in (Z2, Z1, Z3)]
    last, first1, second0, gate_weight, far_parts, near_parts, last_parts = together(
        last, first1, second0, gate_weight, far_parts, near_parts, last_parts
    )
    gate_weight, mark = fetch_call(gate_weight, last)

    first2 = swap(last, X, Y)
    middle_rows = rows_of(middle_rows, first1)
    second1 = swap(middle_rows, Y, X)
    zero = rows_of(zero, second0)
    zero_other = swap(zero, CORE)
    parts = rows_of(parts, far_parts, near_parts, last_parts)
    first_parts = swap(parts, X, Y)
    first2, second1, cotangent, mark, up_weight, first_parts = together(
        first2, second1, cotangent, mark, up_weight, first_parts
    )
    up_weight, mark = fetch_call(up_weight, mark)

    last = rows_of(last, first2)
    second2 = swap(last, Y, X)
    parts = rows_of(parts, first_parts)
    second_parts = swap(parts, Y, X)
    second2, mark, second_parts = together(second2, mark, second_parts)
    parts = rows_of(parts, second_parts)
    parts = (parts, swap(parts, CORE))
    middle_rows = rows_of(middle_rows, second1)
    middle_other = swap(middle_rows, CORE)
    grads = rows_of(cotangent, *grads)
    first_grads = swap(grads, X, Y)
    last = rows_of(last, second2)
    last_other = swap(last, CORE)
    x, put, pick, prob_rows = route_call(
        (zero, middle_rows, last),
        (zero_other, middle_other, last_other),
        parts,
        maps,
        mark,
        local,
        tok_count,
    )
    x, first_grads = together(x, first_grads)
    grads = rows_of(grads, first_grads)
    far_grads = swap(grads, Y, X)
    grads_other = swap(grads, CORE)

    g, u, h, ht = up_call(x, prob_rows, gate_weight, up_weight)
    h, far_grads, grads_other = together(h, far_grads, grads_other)
    far_grads_other = swap(far_grads, CORE)
    mixed, mixed_other = back_call(put, [h], [in_hbm(down_weight)], 0, width)
    mixed_other, far_grads_other = together(mixed_other, far_grads_other)
    mixed = [mixed, swap(mixed_other, CORE)]

    near_c, c = place_call((grads, far_grads, grads_other, far_grads_other), pick, local)

    def leaving(parts, start, stop):
        return add(*(part[start:stop] for part in parts))

    def by_near(parts):
        return parts + [swap(leaving(parts, 2 * tok_count, 4 * tok_count), Z1)]

    def by_far(parts):
        return parts + [swap(leaving(parts, tok_count, 2 * tok_count), Z2)]

    weights = [near_core(gate_weight), near_core(up_weight)]
    mixed[1], far_c = together(mixed[1], c)
    rows, g = together(leaving(mixed, 2 * quarter, 4 * quarter), g)
    mixed.append(swap(rows, Y, X))
    dg, du, dgt, dut, share = slope_call(
        near_c, put, prob_rows, mine.reshape(local, places, -1), down_weight, g, u
    )
    left, left_other = back_call(put, [dg, du], weights, 0, middle)
    left = [left, swap(left_other, CORE)]
    left[0], mixed[2] = together(left[0], mixed[2])
    rows, dg, du = together(leaving(mixed, quarter, 2 * quarter), dg, du)
    mixed.append(swap(rows, X, Y))
    right, right_other = back_call(put, [dg, du], weights, middle, width, share)
    right = [right, swap(right_other, CORE)]

    right[0], left[1] = together(right[0], left[1])
    rows, ht = together(leaving(left, 2 * quarter, 4 * quarter), ht)
    left.append(swap(rows, Y, X))
    mixed_rows, ht = together(leaving(mixed, 2 * tok_count, 4 * tok_count), ht)
    mixed.append(swap(mixed_rows, Z1))
    down_weight_grad = grad_call(far_c, ht)

    right[1], left[2], mixed[4], down_weight_grad = together(
        right[1], left[2], mixed[4], down_weight_grad
    )
    rows, left_rows, mixed_rows, dgt = together(
        leaving(right, 2 * quarter, 4 * quarter),
        leaving(left, quarter, 2 * quarter),
        leaving(mixed, tok_count, 2 * tok_count),
        dgt,
    )
    right.append(swap(rows, Y, X))
    left.append(swap(left_rows, X, Y))
    mixed.append(swap(mixed_rows, Z2))
    gate_weight_grad = grad_call(x, dgt)

    right[2], left[3], gate_weight_grad = together(right[2], left[3], gate_weight_grad)
    rows, left_rows, dut = together(
        leaving(right, quarter, 2 * quarter),
        leaving(left, 2 * tok_count, 4 * tok_count),
        dut,
    )
    right.append(swap(rows, X, Y))
    left.append(swap(left_rows, Z1))
    up_weight_grad = grad_call(x, dut, 0, local // 2)

    right[3], left[4], up_weight_grad = together(right[3], left[4], up_weight_grad)
    rows, left_rows, dut = together(
        leaving(right, 2 * tok_count, 4 * tok_count),
        leaving(left, tok_count, 2 * tok_count),
        dut,
    )
    right.append(swap(rows, Z1))
    left.append(swap(left_rows, Z2))
    up_weight_grad = grad_call(x, dut, local // 2, local, up_weight_grad)
    right[4], up_weight_grad = together(right[4], up_weight_grad)
    right = by_far(right)
    mixed, left, right = (leaving(parts, 0, tok_count) for parts in (mixed, left, right))
    token_grad = jnp.concatenate([left, right[:, : width - middle]], axis=1)
    share = right[:, width - middle : width - middle + total_experts].astype(jnp.float32)
    gate_grad = jnp.sum(jnp.where(used, share[:, None, :], 0.0), axis=2)
    return (mixed, token_grad, gate_grad, gate_weight_grad, up_weight_grad, down_weight_grad)


def routed_body(tokens, cotangent, gate_prob, expert_ids, placement, gate_weight, up_weight, down_weight):
    tok_count, model_width = tokens.shape
    top_count = expert_ids.shape[1]
    expert_devs = lax.axis_size("expert")
    local_experts = gate_weight.shape[0]
    total_experts = placement.shape[0]
    capacity = CAP
    flat_ids = expert_ids.reshape(-1)
    matches_id = flat_ids[:, None] == jnp.arange(total_experts, dtype=jnp.int32)[None, :]
    slot_ids = jnp.sum(jnp.where(matches_id, placement[None, :], 0), axis=1)
    pair_order = jnp.arange(flat_ids.shape[0], dtype=jnp.int32)
    earlier = (slot_ids[:, None] == slot_ids[None, :]) & (pair_order[None, :] < pair_order[:, None])
    position = slot_ids * capacity + jnp.sum(earlier.astype(jnp.int32), axis=1)
    matches = jnp.arange(total_experts * capacity, dtype=jnp.int32)[:, None] == position[None, :]
    matches = matches.reshape(total_experts * capacity, tok_count, top_count)
    dispatch = jnp.any(matches, axis=2).astype(jnp.bfloat16)
    weight_map = jnp.sum(jnp.where(matches, gate_prob[None, :, :], 0.0), axis=2)
    sent_rows = jnp.dot(dispatch, tokens, preferred_element_type=jnp.float32).astype(jnp.bfloat16)
    sent_grads = jnp.dot(
        weight_map, cotangent.astype(jnp.float32), precision=lax.Precision.HIGHEST
    ).astype(jnp.bfloat16)
    block_shape = (1, expert_devs, local_experts, capacity, model_width)
    sent_rows = sent_rows.reshape(block_shape)
    sent_grads = sent_grads.reshape(block_shape)
    got_rows, got_grads = (
        lax.all_to_all(sent_rows, "expert", split_axis=1, concat_axis=1, tiled=True),
        lax.all_to_all(sent_grads, "expert", split_axis=1, concat_axis=1, tiled=True),
    )
    routed, routed_grads = (
        lax.all_gather(got_rows, "dp", axis=0, tiled=True),
        lax.all_gather(got_grads, "dp", axis=0, tiled=True),
    )
    gate_pre = jnp.einsum(
        "asjcd,jfd->asjcf", routed, gate_weight, preferred_element_type=jnp.float32
    )
    up_pre = jnp.einsum("asjcd,jfd->asjcf", routed, up_weight, preferred_element_type=jnp.float32)
    silu_v, slope = gated(gate_pre)
    hidden = (silu_v * up_pre).astype(jnp.bfloat16)
    out_part = jnp.einsum(
        "asjcf,jfd->asjcd", hidden, down_weight, preferred_element_type=jnp.float32
    )
    d_hidden = jnp.einsum(
        "asjcd,jfd->asjcf", routed_grads, down_weight, preferred_element_type=jnp.float32
    )
    d_gate_pre = (d_hidden * up_pre * slope).astype(jnp.bfloat16)
    d_up_pre = (d_hidden * silu_v).astype(jnp.bfloat16)
    back_part = jnp.einsum(
        "asjcf,jfd->asjcd", d_gate_pre, gate_weight, preferred_element_type=jnp.float32
    )
    back_part = back_part + jnp.einsum(
        "asjcf,jfd->asjcd", d_up_pre, up_weight, preferred_element_type=jnp.float32
    )
    down_grad = jnp.einsum(
        "asjcf,asjcd->jfd", hidden, routed_grads, preferred_element_type=jnp.float32
    ).astype(jnp.bfloat16)
    gate_grad_w = jnp.einsum(
        "asjcf,asjcd->jfd", d_gate_pre, routed, preferred_element_type=jnp.float32
    ).astype(jnp.bfloat16)
    up_grad_w = jnp.einsum(
        "asjcf,asjcd->jfd", d_up_pre, routed, preferred_element_type=jnp.float32
    ).astype(jnp.bfloat16)
    summed = (
        lax.psum_scatter(
            out_part.astype(jnp.bfloat16), "dp", scatter_dimension=0, tiled=True
        ).astype(jnp.float32),
        lax.psum_scatter(
            back_part.astype(jnp.bfloat16), "dp", scatter_dimension=0, tiled=True
        ).astype(jnp.float32),
    )
    back_out, back_grad = (
        lax.all_to_all(
            summed[0].astype(jnp.bfloat16), "expert", split_axis=1, concat_axis=1, tiled=True
        ),
        lax.all_to_all(
            summed[1].astype(jnp.bfloat16), "expert", split_axis=1, concat_axis=1, tiled=True
        ),
    )
    out_flat = back_out.reshape(total_experts * capacity, model_width)
    grad_flat = back_grad.reshape(total_experts * capacity, model_width)
    chosen_out = out_flat[position].reshape(tok_count, top_count, model_width)
    chosen_grad = grad_flat[position].reshape(tok_count, top_count, model_width)
    mixed = jnp.einsum(
        "tk,tkd->td", gate_prob, chosen_out.astype(jnp.float32), precision=lax.Precision.HIGHEST
    ).astype(jnp.bfloat16)
    gate_grad = jnp.einsum("td,tkd->tk", cotangent, chosen_out, preferred_element_type=jnp.float32)
    token_grad = jnp.sum(chosen_grad.astype(jnp.float32), axis=1).astype(jnp.bfloat16)
    return (mixed, token_grad, gate_grad, gate_grad_w, up_grad_w, down_grad)


def body(*args):
    tokens, gate_weight = args[0], args[5]
    mesh_fits = (lax.axis_size("dp"), lax.axis_size("expert")) == (4, 8)
    if mesh_fits and tokens.shape[0] <= gate_weight.shape[0] * CAP:
        return dense_body(*args)
    return routed_body(*args)


def solution(mesh):
    return jax.shard_map(
        body,
        mesh=mesh,
        in_specs=(
            P(("dp", "expert"), None),
            P(("dp", "expert"), None),
            P(("dp", "expert"), None),
            P(("dp", "expert"), None),
            P(),
            P("expert", "dp", None),
            P("expert", "dp", None),
            P("expert", "dp", None),
        ),
        out_specs=(
            P(("dp", "expert"), None),
            P(("dp", "expert"), None),
            P(("dp", "expert"), None),
            P("expert", "dp", None),
            P("expert", "dp", None),
            P("expert", "dp", None),
        ),
        check_vma=False,
    )
```
